128 devices in a mesh: dp: 2 (over core), ctx: 16 (over y, x), head: 4 (over z).
Axes of the slice: x: 4, y: 4, z: 4, core: 2. Of those that a mesh axis runs over, the one named last changes fastest.
Arguments:
- inputs: bfloat16 [12288, 1024], P(('dp', 'ctx')), may hold values from -6 to 6
- cotangent: bfloat16 [12288, 1024], P(('dp', 'ctx')), may hold values from -6 to 6
- attention_gain: float32 [1024], replicated, may hold values from 0.1 to 1.9
- query_gain: float32 [64], replicated, may hold values from 0.1 to 1.9
- key_gain: float32 [64], replicated, may hold values from 0.1 to 1.9
- w_query: bfloat16 [1024, 1024], P(None, 'head'), may hold values from -0.1875 to 0.1875
- key_weight: bfloat16 [1024, 512], P(None, 'head'), may hold values from -0.1875 to 0.1875
- value_weight: bfloat16 [1024, 512], P(None, 'head'), may hold values from -0.1875 to 0.1875
- w_out: bfloat16 [1024, 1024], P(None, 'head'), may hold values from -3 to 3
- feed_gain: float32 [1024], replicated, may hold values from 0.1 to 1.9
- w_gate: bfloat16 [1024, 4608], P(None, 'head'), may hold values from -0.1875 to 0.1875
- w_up: bfloat16 [1024, 4608], P(None, 'head'), may hold values from -0.1875 to 0.1875
- w_down: bfloat16 [1024, 4608], P(None, 'head'), may hold values from -0.09375 to 0.09375
Outputs:
- block_out: bfloat16 [12288, 1024], P(('dp', 'ctx'))
- input_grad: float32 [12288, 1024], P(('dp', 'ctx'))
- attention_gain_grad: float32 [1024], P(('dp', 'ctx'))
- query_gain_grad: float32 [64], P(('dp', 'ctx'))
- key_gain_grad: float32 [64], P(('dp', 'ctx'))
- w_query_grad: float32 [1024, 1024], P(('dp', 'ctx'), 'head')
- w_key_grad: float32 [1024, 512], P(('dp', 'ctx'), 'head')
- w_value_grad: float32 [1024, 512], P(('dp', 'ctx'), 'head')
- w_out_grad: float32 [1024, 1024], P(('dp', 'ctx'), 'head')
- feed_gain_grad: float32 [1024], P(('dp', 'ctx'))
- w_gate_grad: float32 [1024, 4608], P(('dp', 'ctx'), 'head')
- w_up_grad: float32 [1024, 4608], P(('dp', 'ctx'), 'head')
- w_down_grad: float32 [1024, 4608], P(('dp', 'ctx'), 'head')
The draws below stay inside these ranges and needn't reach their ends.
All inputs are finite; a program needn't handle non-finite values.
Results may differ from the reference program's by a relative error of at most 0.04.
Values may be sent and summed in bfloat16 or wider, within the bound.
A program may use at most 192 MiB of HBM per device.

```python
import math
import jax
import jax.numpy as jnp
from jax import lax

MODEL_WIDTH = 1024
QUERY_HEADS = 16
KEY_VALUE_HEADS = 8
HEAD_SIZE = 64
FF = 4608
SEQUENCE_LENGTH = 6144
TOKENS = 12288
N_DP = 2


def spiked(drawn, rng, source, target, shards_of, factor):
    def block_of(axis_at):
        return (jnp.arange(drawn.shape[axis_at]) // (drawn.shape[axis_at] // shards_of)).reshape((-1,) + (1,) * (drawn.ndim - 1 - axis_at))

    first = jax.random.permutation(rng, shards_of)[block_of(target)]
    second = (block_of(target) + shards_of // 2) % shards_of
    return jnp.where((block_of(source) == first) | (block_of(source) == second), factor * drawn, drawn)


def level_of(rng, dims, pieces, low, largest):
    level = 1.0
    for position, shards_of in pieces:
        draws = jax.random.uniform(jax.random.fold_in(jax.random.fold_in(rng, 6), position), (shards_of,), jnp.float32, low / len(pieces), largest / len(pieces))
        level = level * jnp.repeat(jnp.exp(draws), dims[position] // shards_of).reshape((-1,) + (1,) * (len(dims) - 1 - position))
    return level


def normal_values(stream_key, dims, width, limit, cuts=(), kind=jnp.bfloat16):
    drawn = width * jax.random.normal(stream_key, dims, jnp.float32)
    if cuts:
        drawn = drawn * level_of(stream_key, dims, cuts, -0.22, 0.18)
    return jnp.clip(drawn, -limit, limit).astype(kind)


def bell_draw_with(stream_key, extent, deviation, most, shards, heavy, kind=jnp.bfloat16):
    entries = deviation * jax.random.normal(stream_key, extent, jnp.float32)
    if shards:
        entries = entries * level_of(stream_key, extent, shards, -0.22, 0.18)
    return jnp.clip(spiked(entries, jax.random.fold_in(stream_key, 3), *heavy), -most, most).astype(kind)


def setup_inputs(seed: int = 0) -> dict:
    keys = jax.random.split(jax.random.key(seed), 14)
    return {
        "inputs": normal_values(keys[0], (TOKENS, MODEL_WIDTH), 1.0, 6.0, ((0, 32),)),
        "cotangent": bell_draw_with(keys[1], (TOKENS, MODEL_WIDTH), 1.0, 6.0, ((0, 32),), (0, 1, 32, 2.75)),
        "attention_gain": jnp.clip(1.0 + 0.18 * jax.random.normal(keys[2], (MODEL_WIDTH,), jnp.float32), 0.1, 1.9),
        "query_gain": jnp.clip(1.0 + 0.18 * jax.random.normal(keys[3], (HEAD_SIZE,), jnp.float32), 0.1, 1.9),
        "key_gain": jnp.clip(1.0 + 0.18 * jax.random.normal(keys[4], (HEAD_SIZE,), jnp.float32), 0.1, 1.9),
        "w_query": normal_values(keys[5], (MODEL_WIDTH, QUERY_HEADS * HEAD_SIZE), MODEL_WIDTH ** -0.5, 0.1875, ((1, 4),)),
        "key_weight": normal_values(keys[6], (MODEL_WIDTH, KEY_VALUE_HEADS * HEAD_SIZE), MODEL_WIDTH ** -0.5, 0.1875, ((1, 4),)),
        "value_weight": normal_values(keys[7], (MODEL_WIDTH, KEY_VALUE_HEADS * HEAD_SIZE), MODEL_WIDTH ** -0.5, 0.1875, ((1, 4),)),
        "w_out": normal_values(keys[8], (MODEL_WIDTH, QUERY_HEADS * HEAD_SIZE), 4 ** -0.5, 3.0, ((1, 4),)),
        "feed_gain": jnp.clip(1.0 + 0.18 * jax.random.normal(keys[9], (MODEL_WIDTH,), jnp.float32), 0.1, 1.9),
        "w_gate": normal_values(keys[10], (MODEL_WIDTH, FF), MODEL_WIDTH ** -0.5, 0.1875, ((1, 4),)),
        "w_up": normal_values(keys[11], (MODEL_WIDTH, FF), MODEL_WIDTH ** -0.5, 0.1875, ((1, 4),)),
        "w_down": normal_values(keys[12], (MODEL_WIDTH, FF), FF ** -0.5, 0.09375, ((1, 4),)),
    }


@jax.custom_vjp
def lower_bound(v):
    return lax.optimization_barrier(v.astype(jnp.bfloat16)).astype(jnp.float32)

@jax.custom_vjp
def backward_lower_bound(v):
    return v

def low_keep(v):
    return (lower_bound(v), None)

def low_pass(kept, grad):
    return (grad,)

def back_keep(v):
    return (v, None)

def back_low(kept, grad):
    return (lower_bound(grad),)
lower_bound.defvjp(low_keep, low_pass)
backward_lower_bound.defvjp(back_keep, back_low)
epsilon = 1e-05
theta_base = 1000000.0
masked_value = -1e+30
highest_precision = lax.Precision.HIGHEST

def rms_scale(values):
    return lax.rsqrt(lax.optimization_barrier(jnp.mean(values * values, axis=-1, keepdims=True)) + epsilon)

def row_norm(values, gain):
    return values * rms_scale(values) * gain

def rotary_tables(positions, head_dim):
    half_width = head_dim // 2
    frequency = theta_base ** (-(jnp.arange(half_width).astype(jnp.float32) * 2.0) / head_dim)
    angles = positions.astype(jnp.float32)[:, None] * frequency[None, :]
    cosine_table = jnp.cos(angles)
    sine_table = jnp.sin(angles)
    return (jnp.concatenate([cosine_table, cosine_table], -1), jnp.concatenate([sine_table, sine_table], -1))

def rotate(values, cosine_table, sine_table):
    half_width = values.shape[-1] // 2
    turned = jnp.concatenate([-values[..., half_width:], values[..., :half_width]], -1)
    return values * cosine_table + turned * sine_table

def silu_gate(values):
    return values * jax.nn.sigmoid(values)

def attention(query_rows, key_matrix_rows, value_matrix_rows):
    heads_per_group = QUERY_HEADS // KEY_VALUE_HEADS
    key_full = jnp.repeat(key_matrix_rows, heads_per_group, axis=2)
    value_full = jnp.repeat(value_matrix_rows, heads_per_group, axis=2)
    block_rows = math.gcd(SEQUENCE_LENGTH, 512)
    key_pos = jnp.arange(SEQUENCE_LENGTH, dtype=jnp.int32)

    def one_block(block_index):
        first_row = block_index * block_rows
        chosen = lax.dynamic_slice_in_dim(query_rows, first_row, block_rows, 1)
        scores = backward_lower_bound(HEAD_SIZE ** (-0.5) * jnp.einsum('sqhd,skhd->shqk', chosen, key_full, precision=highest_precision))
        allowed = (first_row + jnp.arange(block_rows, dtype=jnp.int32))[:, None] >= key_pos[None, :]
        scores = jnp.where(allowed, scores, masked_value)
        row_top = lax.optimization_barrier(jnp.max(scores, axis=-1, keepdims=True))
        weights = jnp.exp(scores - row_top)
        probabilities = weights / lax.optimization_barrier(jnp.sum(weights, axis=-1, keepdims=True))
        return jnp.einsum('shqk,skhd->sqhd', lower_bound(probabilities), value_full, precision=highest_precision)
    outputs = lax.map(jax.checkpoint(one_block), jnp.arange(SEQUENCE_LENGTH // block_rows, dtype=jnp.int32))
    return jnp.moveaxis(outputs, 0, 1).reshape(N_DP, SEQUENCE_LENGTH, QUERY_HEADS, HEAD_SIZE)

def forward(inputs, attention_gain, query_gain, key_gain, w_query, key_weight, value_weight, w_out, feed_gain, w_gate, w_up, w_down):
    normalized_input = lower_bound(row_norm(inputs, attention_gain))
    query_rows = backward_lower_bound(jnp.dot(normalized_input, w_query, precision=highest_precision)).reshape(N_DP, SEQUENCE_LENGTH, QUERY_HEADS, HEAD_SIZE)
    key_matrix_rows = backward_lower_bound(jnp.dot(normalized_input, key_weight, precision=highest_precision)).reshape(N_DP, SEQUENCE_LENGTH, KEY_VALUE_HEADS, HEAD_SIZE)
    value_matrix_rows = lower_bound(backward_lower_bound(jnp.dot(normalized_input, value_weight, precision=highest_precision))).reshape(N_DP, SEQUENCE_LENGTH, KEY_VALUE_HEADS, HEAD_SIZE)
    cosine_table, sine_table = rotary_tables(jnp.arange(SEQUENCE_LENGTH, dtype=jnp.int32), HEAD_SIZE)
    cosine_table = cosine_table[:, None, :]
    sine_table = sine_table[:, None, :]
    query_rows = lower_bound(rotate(row_norm(query_rows, query_gain), cosine_table, sine_table))
    key_matrix_rows = lower_bound(rotate(row_norm(key_matrix_rows, key_gain), cosine_table, sine_table))
    attended = attention(query_rows, key_matrix_rows, value_matrix_rows)
    attended = lower_bound(backward_lower_bound(attended)).reshape(TOKENS, QUERY_HEADS * HEAD_SIZE)
    hidden_first = inputs + backward_lower_bound(jnp.dot(attended, w_out.T, precision=highest_precision))
    mixed = lower_bound(row_norm(hidden_first, feed_gain))
    gate_rows = backward_lower_bound(jnp.dot(mixed, w_gate, precision=highest_precision))
    up_rows = backward_lower_bound(jnp.dot(mixed, w_up, precision=highest_precision))
    inner_rows = lower_bound(silu_gate(gate_rows) * up_rows)
    return hidden_first + backward_lower_bound(jnp.dot(inner_rows, w_down.T, precision=highest_precision))

def reference(inputs, cotangent, attention_gain, query_gain, key_gain, w_query, key_weight, value_weight, w_out, feed_gain, w_gate, w_up, w_down):
    floats = tuple((argument.astype(jnp.float32) for argument in (inputs, attention_gain, query_gain, key_gain, w_query, key_weight, value_weight, w_out, feed_gain, w_gate, w_up, w_down)))
    result, pullback = jax.vjp(forward, *floats)
    grads = pullback(cotangent.astype(jnp.float32))
    return (result.astype(jnp.bfloat16), grads[0], grads[1], grads[2], grads[3], grads[4], grads[5], grads[6], grads[7], grads[8], grads[9], grads[10], grads[11])
```

```python
from functools import partial

import jax
import jax.numpy as jnp
from jax import lax
from jax.experimental import pallas as pl
from jax.experimental.pallas import tpu as pltpu
from jax.sharding import PartitionSpec as P

epsilon = 1e-05
theta_base = 1000000.0
MESH = pl.DeviceIdType.MESH
F32 = jnp.float32
BF16 = jnp.bfloat16
ROWS = 384
LOG2E = 1.4426950408889634
VMEM_LIMIT = 56 * 1024 * 1024


def rms_scale(values):
    return lax.rsqrt(jnp.mean(values * values, axis=-1, keepdims=True) + epsilon)


def row_norm(values, gain):
    return values * rms_scale(values) * gain


def rotary_tables(positions, head_dim):
    half_width = head_dim // 2
    frequency = theta_base ** (-(jnp.arange(half_width).astype(F32) * 2.0) / head_dim)
    angles = positions.astype(F32)[:, None] * frequency[None, :]
    cosine_table = jnp.cos(angles)
    sine_table = jnp.sin(angles)
    return (
        jnp.concatenate([cosine_table, cosine_table], -1),
        jnp.concatenate([sine_table, sine_table], -1),
    )


def rotate(values, cosine_table, sine_table):
    half_width = values.shape[-1] // 2
    turned = jnp.concatenate([-values[..., half_width:], values[..., :half_width]], -1)
    return values * cosine_table + turned * sine_table


def head_norm_rotate(values, gain, cosine_table, sine_table):
    shaped = values.reshape(values.shape[0], -1, gain.shape[0])
    turned = rotate(row_norm(shaped, gain), cosine_table[:, None, :], sine_table[:, None, :])
    return turned.reshape(values.shape[0], -1)


def contract_rows(left_side, right_side):
    return lax.dot_general(
        left_side, right_side, (((0,), (0,)), ((), ())), preferred_element_type=F32
    )


def contract_cols(left_side, right_side):
    return lax.dot_general(
        left_side, right_side, (((1,), (1,)), ((), ())), preferred_element_type=F32
    )


def remote(src, dst, send_sem, recv_sem, d, c, z):
    return pltpu.make_async_remote_copy(
        src_ref=src,
        dst_ref=dst,
        send_sem=send_sem,
        recv_sem=recv_sem,
        device_id=(d, c, z),
        device_id_type=MESH,
    )


def local_sem(src, dst, sem):
    return pltpu.make_async_copy(src, dst, sem)


def place():
    return lax.axis_index("dp"), lax.axis_index("ctx"), lax.axis_index("head")


def plane_barrier(d, c, z, with_z):
    barrier = pltpu.get_barrier_semaphore()

    def greet(index, carry):
        other_d, other_c = index // 16, lax.rem(index, 16)

        @pl.when((other_d != d) | (other_c != c))
        def _():
            pl.semaphore_signal(
                barrier, inc=1, device_id=(other_d, other_c, z), device_id_type=MESH
            )

        return carry

    lax.fori_loop(0, 32, greet, 0)
    count = 31
    if with_z:
        for step in (1, 3):
            pl.semaphore_signal(
                barrier, inc=1, device_id=(d, c, lax.rem(z + step, 4)), device_id_type=MESH
            )
        count += 2
    pl.semaphore_wait(barrier, count)


def role_of(d, c):
    sequence = jnp.where(c >= 8, 1, 0)
    low = jnp.where(c >= 8, 15 - c, c)
    return sequence, d, low, 15 - low


def spread_heads(pair, upper):
    pair = pair.astype(F32)
    lane = lax.broadcasted_iota(jnp.int32, pair.shape, 1)
    turned = pltpu.roll(pair, 64, 1)
    if upper:
        first, second = jnp.where(lane >= 64, turned, 0.0), jnp.where(lane >= 64, pair, 0.0)
    else:
        first, second = jnp.where(lane < 64, pair, 0.0), jnp.where(lane < 64, turned, 0.0)
    return first.astype(BF16), second.astype(BF16)


def nt(left, right):
    return lax.dot_general(left, right, (((1,), (1,)), ((), ())), preferred_element_type=F32)


def nn(left, right):
    return lax.dot_general(left, right, (((1,), (0,)), ((), ())), preferred_element_type=F32)


SCORE_SCALE = LOG2E / 8.0


def attention_forward_kernel(
    q_ref,
    kv_ref,
    wo_ref,
    kvs_ref,
    qs_ref,
    os_ref,
    l2_ref,
    oall_ref,
    wall_ref,
    qz,
    acc,
    sums,
    own_o,
    q_send,
    q_recv,
    kv_send,
    kv_recv,
    o_send,
    o_recv,
    g_send,
    g_recv,
    w_send,
    w_recv,
):
    d, c, z = place()
    s, j_role, low, high = role_of(d, c)
    own_group = low
    plane_barrier(d, c, z, True)

    slot = jnp.where(c >= 8, 1, 0)
    home = jnp.where(slot == d, c, 15 - c)
    for j in range(2):
        here = (home == c) & (d == j)

        @pl.when(jnp.logical_not(here))
        def _():
            remote(q_ref.at[j], qs_ref.at[slot], q_send.at[j], q_recv.at[slot], j, home, z).start()

        @pl.when(here)
        def _():
            local_sem(q_ref.at[j], qs_ref.at[slot], q_recv.at[slot]).start()

    def kv_target(k):
        group = lax.rem(own_group + k, 8)
        target = jnp.where(d == 0, group, 15 - group)
        return target, (15 - group) >= c

    def kv_start(k, carry):
        target, needed = kv_target(k)
        for j in range(2):
            here = (target == c) & (d == j)

            @pl.when(needed & jnp.logical_not(here))
            def _():
                remote(
                    kv_ref.at[j],
                    kvs_ref.at[c],
                    kv_send.at[2 * k + j],
                    kv_recv.at[c],
                    j,
                    target,
                    z,
                ).start()

            @pl.when(needed & here)
            def _():
                local_sem(kv_ref.at[j], kvs_ref.at[c], kv_recv.at[c]).start()

        return carry

    lax.fori_loop(0, 8, kv_start, 0)

    column = pl.ds(pl.multiple_of(z * 256, 256), 256)
    up, down = lax.rem(z + 1, 4), lax.rem(z + 3, 4)
    wall_ref[:, column] = wo_ref[...]
    w_up = remote(wall_ref.at[:, column], wall_ref.at[:, column], w_send.at[0], w_recv.at[0], d, c, up)
    w_down = remote(
        wall_ref.at[:, column], wall_ref.at[:, column], w_send.at[1], w_recv.at[1], d, c, down
    )
    w_up.start()
    w_down.start()

    acc[...] = jnp.zeros_like(acc)
    sums[...] = jnp.zeros_like(sums)
    for which in range(2):
        local_sem(q_ref.at[0], qs_ref.at[which], q_recv.at[which]).wait()
        first, second = spread_heads(qs_ref[which], False)
        qz[which, 0:ROWS, :] = first
        qz[which, ROWS : 2 * ROWS, :] = second

    def kv_wait(block):
        local_sem(kv_ref.at[0], kvs_ref.at[block], kv_recv.at[block]).wait()

    def tile(block, which, masked):
        keys = kvs_ref[block]
        for head in range(2):
            rows = slice(head * ROWS, (head + 1) * ROWS)
            weights = jnp.exp2(nt(qz[which, rows, :], keys) * SCORE_SCALE)
            if masked:
                row = lax.broadcasted_iota(jnp.int32, weights.shape, 0)
                key = lax.broadcasted_iota(jnp.int32, weights.shape, 1)
                weights = jnp.where(row >= key, weights, 0.0)
            sums[which, rows, :] += weights[:, 0:128] + weights[:, 128:256] + weights[:, 256:384]
            acc[which, rows, :] += nn(weights.astype(BF16), keys)

    kv_wait(low)
    kv_wait(high)
    tile(low, 1, False)
    tile(low, 0, True)
    tile(high, 1, True)

    def step(k, carry):
        first = lax.rem(own_group + 8 - k, 8)
        below = first < own_group
        kv_wait(first)

        @pl.when(jnp.logical_not(below))
        def _():
            kv_wait(15 - first)

        tile(first, 1, False)
        tile(jnp.where(below, first, 15 - first), jnp.where(below, 0, 1), False)
        return carry

    lax.fori_loop(1, 8, step, 0)

    lane = lax.broadcasted_iota(jnp.int32, (ROWS, 128), 1)
    for which in range(2):
        total = jnp.sum(sums[which], axis=1, keepdims=True)
        result = acc[which] / total
        os_ref[which] = jnp.where(
            lane < 64, pltpu.roll(result[:ROWS], 64, 1), result[ROWS:]
        ).astype(BF16)
        logs = jnp.broadcast_to(jnp.log2(total), (2 * ROWS, 128))
        l2_ref[which] = logs.T[0:8]
        block = high if which else low
        here = (s == d) & (block == c)

        @pl.when(jnp.logical_not(here))
        def _():
            remote(
                os_ref.at[which], own_o.at[j_role], o_send.at[which], o_recv.at[j_role], s, block, z
            ).start()

        @pl.when(here)
        def _():
            local_sem(os_ref.at[which], own_o.at[j_role], o_recv.at[j_role]).start()

    w_up.wait_recv()
    w_down.wait_recv()
    below_column = pl.ds(pl.multiple_of(down * 256, 256), 256)
    above_column = pl.ds(pl.multiple_of(up * 256, 256), 256)
    w_up2 = remote(
        wall_ref.at[0:512, below_column],
        wall_ref.at[0:512, below_column],
        w_send.at[2],
        w_recv.at[2],
        d,
        c,
        up,
    )
    w_down2 = remote(
        wall_ref.at[512:1024, above_column],
        wall_ref.at[512:1024, above_column],
        w_send.at[3],
        w_recv.at[3],
        d,
        c,
        down,
    )
    w_up2.start()
    w_down2.start()

    for j in range(2):
        local_sem(os_ref.at[0], own_o.at[j], o_recv.at[j]).wait()
        oall_ref[:, pl.ds(pl.multiple_of(z * 256 + j * 128, 128), 128)] = own_o[j]
    g_up = remote(oall_ref.at[:, column], oall_ref.at[:, column], g_send.at[0], g_recv.at[0], d, c, up)
    g_down = remote(
        oall_ref.at[:, column], oall_ref.at[:, column], g_send.at[1], g_recv.at[1], d, c, down
    )
    g_up.start()
    g_down.start()
    g_up.wait_recv()
    low_half = pl.ds(pl.multiple_of(down * 256, 128), 128)
    g_up2 = remote(
        oall_ref.at[:, low_half], oall_ref.at[:, low_half], g_send.at[2], g_recv.at[2], d, c, up
    )
    g_up2.start()
    g_down.wait_recv()
    high_half = pl.ds(pl.multiple_of(up * 256 + 128, 128), 128)
    g_down2 = remote(
        oall_ref.at[:, high_half], oall_ref.at[:, high_half], g_send.at[3], g_recv.at[3], d, c, down
    )
    g_down2.start()
    g_up2.wait_recv()
    g_down2.wait_recv()
    w_up2.wait_recv()
    w_down2.wait_recv()

    for copy in (w_up, w_down, w_up2, w_down2, g_up, g_down, g_up2, g_down2):
        copy.wait_send()
    for j in range(2):

        @pl.when(jnp.logical_not((home == c) & (d == j)))
        def _():
            remote(q_ref.at[j], qs_ref.at[slot], q_send.at[j], q_recv.at[slot], j, home, z).wait_send()

    def kv_sent(k, carry):
        target, needed = kv_target(k)
        for j in range(2):

            @pl.when(needed & jnp.logical_not((target == c) & (d == j)))
            def _():
                remote(
                    kv_ref.at[j],
                    kvs_ref.at[c],
                    kv_send.at[2 * k + j],
                    kv_recv.at[c],
                    j,
                    target,
                    z,
                ).wait_send()

        return carry

    lax.fori_loop(0, 8, kv_sent, 0)
    for which in range(2):
        block = high if which else low

        @pl.when(jnp.logical_not((s == d) & (block == c)))
        def _():
            remote(
                os_ref.at[which], own_o.at[j_role], o_send.at[which], o_recv.at[j_role], s, block, z
            ).wait_send()


def attention_backward_kernel(
    do_ref,
    kvs_ref,
    qs_ref,
    os_ref,
    l2_ref,
    dq_ref,
    dkv_ref,
    qz,
    doz,
    delta,
    dos,
    dqt,
    dq_out,
    dq_in,
    dkv_out,
    dkv_in,
    do_send,
    do_recv,
    dq_send,
    dq_recv,
    dkv_send,
    dkv_recv,
):
    d, c, z = place()
    s, j_role, low, high = role_of(d, c)
    own_group = low
    plane_barrier(d, c, z, False)

    slot = jnp.where(c >= 8, 1, 0)
    home = jnp.where(slot == d, c, 15 - c)
    for j in range(2):
        here = (home == c) & (d == j)

        @pl.when(jnp.logical_not(here))
        def _():
            remote(do_ref.at[j], dos.at[slot], do_send.at[j], do_recv.at[slot], j, home, z).start()

        @pl.when(here)
        def _():
            local_sem(do_ref.at[j], dos.at[slot], do_recv.at[slot]).start()

    dqt[...] = jnp.zeros_like(dqt)
    for which in range(2):
        first, second = spread_heads(qs_ref[which], False)
        qz[which, 0:ROWS, :] = first
        qz[which, ROWS : 2 * ROWS, :] = second
    for which in range(2):
        local_sem(do_ref.at[0], dos.at[which], do_recv.at[which]).wait()
        first, second = spread_heads(dos[which], True)
        doz[which, 0:ROWS, :] = first
        doz[which, ROWS : 2 * ROWS, :] = second
        product = (dos[which].astype(F32) * os_ref[which].astype(F32)).T
        delta[which, :, 0:ROWS] = jnp.broadcast_to(
            jnp.sum(product[0:64], axis=0, keepdims=True), (8, ROWS)
        )
        delta[which, :, ROWS : 2 * ROWS] = jnp.broadcast_to(
            jnp.sum(product[64:128], axis=0, keepdims=True), (8, ROWS)
        )

    lane = lax.broadcasted_iota(jnp.int32, (ROWS, 128), 1)
    key_scale = jnp.where(lane < 64, 0.125, 1.0)

    def tile(block, which, masked):
        keys = kvs_ref[block]
        keys_t = keys.T
        result = None
        for head in range(2):
            rows = slice(head * ROWS, (head + 1) * ROWS)
            q_rows = qz[which, rows, :]
            do_rows = doz[which, rows, :]
            weights = jnp.exp2(nt(keys, q_rows) * SCORE_SCALE - l2_ref[which, 0:1, rows])
            if masked:
                key = lax.broadcasted_iota(jnp.int32, weights.shape, 0)
                row = lax.broadcasted_iota(jnp.int32, weights.shape, 1)
                weights = jnp.where(row >= key, weights, 0.0)
            score_grad = (weights * (nt(keys, do_rows) - delta[which, 0:1, rows])).astype(BF16)
            part = nn(score_grad, q_rows) + nn(weights.astype(BF16), do_rows)
            result = part if result is None else result + part
            dqt[which, :, rows] += nn(keys_t, score_grad)
        return result * key_scale

    def send(block):
        here = (s == d) & (block == c)

        @pl.when(jnp.logical_not(here))
        def _():
            remote(
                dkv_out.at[block],
                dkv_in.at[j_role, own_group],
                dkv_send.at[block],
                dkv_recv.at[j_role, own_group],
                s,
                block,
                z,
            ).start()

        @pl.when(here)
        def _():
            local_sem(
                dkv_out.at[block], dkv_in.at[j_role, own_group], dkv_recv.at[j_role, own_group]
            ).start()

    dkv_out[low] = (tile(low, 1, False) + tile(low, 0, True)).astype(BF16)
    send(low)
    dkv_out[high] = tile(high, 1, True).astype(BF16)
    send(high)

    def step(k, carry):
        first = lax.rem(own_group + 8 - k, 8)
        below = first < own_group
        one = tile(first, 1, False)
        two = tile(jnp.where(below, first, 15 - first), jnp.where(below, 0, 1), False)

        @pl.when(below)
        def _():
            dkv_out[first] = (one + two).astype(BF16)
            send(first)

        @pl.when(jnp.logical_not(below))
        def _():
            dkv_out[first] = one.astype(BF16)
            send(first)
            dkv_out[15 - first] = two.astype(BF16)
            send(15 - first)

        return carry

    lax.fori_loop(1, 8, step, 0)

    for which in range(2):
        flat = dqt[which].T * 0.125
        dq_out[which] = jnp.where(
            lane < 64, flat[:ROWS], pltpu.roll(flat[ROWS:], 64, 1)
        ).astype(BF16)
        block = high if which else low
        here = (s == d) & (block == c)

        @pl.when(jnp.logical_not(here))
        def _():
            remote(
                dq_out.at[which], dq_in.at[j_role], dq_send.at[which], dq_recv.at[j_role], s, block, z
            ).start()

        @pl.when(here)
        def _():
            local_sem(dq_out.at[which], dq_in.at[j_role], dq_recv.at[j_role]).start()

    for j in range(2):
        dkv_ref[j] = jnp.zeros((ROWS, 128), F32)

    def collect(k, carry):
        group = lax.rem(own_group + k, 8)

        @pl.when((15 - group) >= c)
        def _():
            for j in range(2):
                local_sem(dkv_out.at[0], dkv_in.at[j, group], dkv_recv.at[j, group]).wait()
                dkv_ref[j] += dkv_in[j, group].astype(F32)

        return carry

    lax.fori_loop(0, 8, collect, 0)
    for j in range(2):
        local_sem(dq_out.at[0], dq_in.at[j], dq_recv.at[j]).wait()
        dq_ref[:, j * 128 : (j + 1) * 128] = dq_in[j]

    for j in range(2):

        @pl.when(jnp.logical_not((home == c) & (d == j)))
        def _():
            remote(
                do_ref.at[j], dos.at[slot], do_send.at[j], do_recv.at[slot], j, home, z
            ).wait_send()

    for which in range(2):
        block = high if which else low

        @pl.when(jnp.logical_not((s == d) & (block == c)))
        def _():
            remote(
                dq_out.at[which], dq_in.at[j_role], dq_send.at[which], dq_recv.at[j_role], s, block, z
            ).wait_send()

    def sent(block, carry):
        @pl.when((block <= high) & jnp.logical_not((s == d) & (block == c)))
        def _():
            remote(
                dkv_out.at[block],
                dkv_in.at[j_role, own_group],
                dkv_send.at[block],
                dkv_recv.at[j_role, own_group],
                s,
                block,
                z,
            ).wait_send()

        return carry

    lax.fori_loop(0, 16, sent, 0)


def z_barrier(d, c, z):
    barrier = pltpu.get_barrier_semaphore()
    for step in (1, 2, 3):
        pl.semaphore_signal(
            barrier, inc=1, device_id=(d, c, lax.rem(z + step, 4)), device_id_type=MESH
        )
    pl.semaphore_wait(barrier, 3)


def z_reduce_kernel(count, *refs):
    parts, outs = refs[:count], refs[count : 2 * count]
    landed, send_sem, recv_sem = refs[2 * count :]
    d, c, z = place()
    z_barrier(d, c, z)
    copies = []
    for index in range(count):
        for step in (1, 2, 3):
            other = lax.rem(z + step, 4)
            copy = remote(
                parts[index].at[other],
                landed.at[index, step - 1],
                send_sem.at[index, step - 1],
                recv_sem.at[index, step - 1],
                d,
                c,
                other,
            )
            copy.start()
            copies.append(copy)
    for index in range(count):
        for step in range(3):
            copies[index * 3 + step].wait_recv()
        outs[index][...] = (
            parts[index][z].astype(F32)
            + landed[index, 0].astype(F32)
            + landed[index, 1].astype(F32)
            + landed[index, 2].astype(F32)
        )
    for copy in copies:
        copy.wait_send()


def z_reduce(parts, collective_id):
    count = len(parts)
    return pl.pallas_call(
        partial(z_reduce_kernel, count),
        out_shape=[jax.ShapeDtypeStruct((96, 1024), F32)] * count,
        in_specs=[pl.BlockSpec(memory_space=pltpu.VMEM)] * count,
        out_specs=[pl.BlockSpec(memory_space=pltpu.VMEM)] * count,
        scratch_shapes=[
            pltpu.VMEM((count, 3, 96, 1024), BF16),
            pltpu.SemaphoreType.DMA((count, 3)),
            pltpu.SemaphoreType.DMA((count, 3)),
        ],
        compiler_params=pltpu.CompilerParams(
            collective_id=collective_id, has_side_effects=True, vmem_limit_bytes=VMEM_LIMIT
        ),
        name="z_reduce",
    )(*[part.reshape(4, 96, 1024) for part in parts])


def z_gather_kernel(count, *refs):
    parts, outs = refs[:count], refs[count : 2 * count]
    send_sem, recv_sem = refs[2 * count :]
    d, c, z = place()
    z_barrier(d, c, z)
    copies = []
    for index in range(count):
        for step in (1, 2, 3):
            copy = remote(
                parts[index],
                outs[index].at[z],
                send_sem.at[index, step - 1],
                recv_sem.at[index, step - 1],
                d,
                c,
                lax.rem(z + step, 4),
            )
            copy.start()
            copies.append(copy)
    for index in range(count):
        outs[index][z] = parts[index][...]
    for copy in copies:
        copy.wait_recv()
    for copy in copies:
        copy.wait_send()


def z_gather(parts, collective_id):
    count = len(parts)
    return pl.pallas_call(
        partial(z_gather_kernel, count),
        out_shape=[jax.ShapeDtypeStruct((4,) + part.shape, part.dtype) for part in parts],
        in_specs=[pl.BlockSpec(memory_space=pltpu.VMEM)] * count,
        out_specs=[pl.BlockSpec(memory_space=pltpu.VMEM)] * count,
        scratch_shapes=[
            pltpu.SemaphoreType.DMA((count, 3)),
            pltpu.SemaphoreType.DMA((count, 3)),
        ],
        compiler_params=pltpu.CompilerParams(
            collective_id=collective_id, has_side_effects=True, vmem_limit_bytes=VMEM_LIMIT
        ),
        name="z_gather",
    )(*parts)


def weight_reduce_kernel(items, count, *refs):
    grads, outs = refs[:count], refs[count : 2 * count]
    number = len(items)
    scratch = refs[2 * count :]
    held = scratch[0 * number : 1 * number]
    from_core = scratch[1 * number : 2 * number]
    landed = scratch[2 * number : 3 * number]
    summed = scratch[3 * number : 4 * number]
    landed_last = scratch[4 * number : 5 * number]
    load_sem, core_sems, first_sems, last_sems = scratch[5 * number :]
    d, c, z = place()
    y, x = c // 4, lax.rem(c, 4)
    barrier = pltpu.get_barrier_semaphore()
    pl.semaphore_signal(barrier, inc=1, device_id=(1 - d, c, z), device_id_type=MESH)
    for step in (1, 2, 3):
        for other in (lax.rem(y + step, 4) * 4 + x, y * 4 + lax.rem(x + step, 4)):
            pl.semaphore_signal(barrier, inc=1, device_id=(d, other, z), device_id_type=MESH)
    pl.semaphore_wait(barrier, 7)

    loads, cores = [], []
    for i, (index, start, width, y_first) in enumerate(items):
        columns = pl.ds(start, width)
        core = remote(
            grads[index].at[1 - d, :, :, :, columns],
            from_core[i],
            core_sems.at[0, i],
            core_sems.at[1, i],
            1 - d,
            c,
            z,
        )
        core.start()
        load = local_sem(grads[index].at[d, :, :, :, columns], held[i], load_sem.at[i])
        load.start()
        cores.append(core)
        loads.append(load)

    firsts = []
    for i, (index, start, width, y_first) in enumerate(items):
        loads[i].wait()
        cores[i].wait_recv()

        def add(row, carry):
            held[i][row] = (held[i][row].astype(F32) + from_core[i][row].astype(F32)).astype(BF16)
            return carry

        lax.fori_loop(0, 4, add, 0)
        copies = []
        for step in (1, 2, 3):
            if y_first:
                other = lax.rem(y + step, 4)
                source, chip = held[i].at[other], other * 4 + x
            else:
                other = lax.rem(x + step, 4)
                source, chip = held[i].at[:, other], y * 4 + other
            copy = remote(
                source,
                landed[i].at[step - 1],
                first_sems.at[0, i, step - 1],
                first_sems.at[1, i, step - 1],
                d,
                chip,
                z,
            )
            copy.start()
            copies.append(copy)
        firsts.append(copies)

    lasts = []
    for i, (index, start, width, y_first) in enumerate(items):
        for copy in firsts[i]:
            copy.wait_recv()
        own = held[i][y] if y_first else held[i][:, x]
        total = own.astype(F32)
        for step in range(3):
            total = total + landed[i][step].astype(F32)
        summed[i][...] = total.astype(BF16)
        copies = []
        for step in (1, 2, 3):
            if y_first:
                other = lax.rem(x + step, 4)
                chip = y * 4 + other
            else:
                other = lax.rem(y + step, 4)
                chip = other * 4 + x
            copy = remote(
                summed[i].at[other],
                landed_last[i].at[step - 1],
                last_sems.at[0, i, step - 1],
                last_sems.at[1, i, step - 1],
                d,
                chip,
                z,
            )
            copy.start()
            copies.append(copy)
        lasts.append(copies)

    for i, (index, start, width, y_first) in enumerate(items):
        for copy in lasts[i]:
            copy.wait_recv()
        mine = x if y_first else y
        total = summed[i][mine].astype(F32)
        for step in range(3):
            total = total + landed_last[i][step].astype(F32)
        outs[index][:, start : start + width] = total
    for i in range(number):
        cores[i].wait_send()
        for copy in firsts[i] + lasts[i]:
            copy.wait_send()


def weight_reduce(grads, items, collective_id):
    count, number = len(grads), len(items)
    widths = [grad.shape[1] for grad in grads]
    shaped = [grad.reshape(2, 4, 4, 32, width) for grad, width in zip(grads, widths)]
    scratch = []
    for lead in ((4, 4), (4, 4), (3, 4), (4,), (3,)):
        scratch += [pltpu.VMEM(lead + (32, item[2]), BF16) for item in items]
    return pl.pallas_call(
        partial(weight_reduce_kernel, items, count),
        out_shape=[jax.ShapeDtypeStruct((32, width), F32) for width in widths],
        in_specs=[pl.BlockSpec(memory_space=pl.ANY)] * count,
        out_specs=[pl.BlockSpec(memory_space=pltpu.VMEM)] * count,
        scratch_shapes=scratch
        + [
            pltpu.SemaphoreType.DMA((number,)),
            pltpu.SemaphoreType.DMA((2, number)),
            pltpu.SemaphoreType.DMA((2, number, 3)),
            pltpu.SemaphoreType.DMA((2, number, 3)),
        ],
        compiler_params=pltpu.CompilerParams(
            collective_id=collective_id, has_side_effects=True, vmem_limit_bytes=VMEM_LIMIT
        ),
        name="weight_reduce",
    )(*shaped)


EARLY_ITEMS = (
    (0, 0, 640, True),
    (0, 640, 512, False),
    (1, 0, 640, True),
    (1, 640, 512, False),
    (2, 0, 512, True),
    (2, 512, 640, False),
)
LATE_ITEMS = (
    (0, 0, 256, True),
    (3, 0, 256, False),
    (1, 0, 128, False),
    (2, 0, 128, True),
    (4, 0, 128, False),
)


def attention_forward(query_pairs, key_values, w_out):
    sems = pltpu.SemaphoreType.DMA
    vmem = pl.BlockSpec(memory_space=pltpu.VMEM)
    return pl.pallas_call(
        attention_forward_kernel,
        out_shape=[
            jax.ShapeDtypeStruct((16, ROWS, 128), BF16),
            jax.ShapeDtypeStruct((2, ROWS, 128), BF16),
            jax.ShapeDtypeStruct((2, ROWS, 128), BF16),
            jax.ShapeDtypeStruct((2, 8, 2 * ROWS), F32),
            jax.ShapeDtypeStruct((ROWS, 1024), BF16),
            jax.ShapeDtypeStruct((1024, 1024), BF16),
        ],
        in_specs=[vmem] * 3,
        out_specs=[vmem] * 6,
        scratch_shapes=[
            pltpu.VMEM((2, 2 * ROWS, 128), BF16),
            pltpu.VMEM((2, 2 * ROWS, 128), F32),
            pltpu.VMEM((2, 2 * ROWS, 128), F32),
            pltpu.VMEM((2, ROWS, 128), BF16),
            sems((2,)),
            sems((2,)),
            sems((16,)),
            sems((16,)),
            sems((2,)),
            sems((2,)),
            sems((4,)),
            sems((4,)),
            sems((4,)),
            sems((4,)),
        ],
        compiler_params=pltpu.CompilerParams(
            collective_id=1, has_side_effects=True, vmem_limit_bytes=VMEM_LIMIT
        ),
        name="attention_forward",
    )(query_pairs, key_values, w_out)


def attention_backward(dout_pairs, key_values, queries, outputs, logs):
    sems = pltpu.SemaphoreType.DMA
    vmem = pl.BlockSpec(memory_space=pltpu.VMEM)
    return pl.pallas_call(
        attention_backward_kernel,
        out_shape=[
            jax.ShapeDtypeStruct((ROWS, 256), BF16),
            jax.ShapeDtypeStruct((2, ROWS, 128), F32),
        ],
        in_specs=[vmem] * 5,
        out_specs=[vmem] * 2,
        scratch_shapes=[
            pltpu.VMEM((2, 2 * ROWS, 128), BF16),
            pltpu.VMEM((2, 2 * ROWS, 128), BF16),
            pltpu.VMEM((2, 8, 2 * ROWS), F32),
            pltpu.VMEM((2, ROWS, 128), BF16),
            pltpu.VMEM((2, 128, 2 * ROWS), F32),
            pltpu.VMEM((2, ROWS, 128), BF16),
            pltpu.VMEM((2, ROWS, 128), BF16),
            pltpu.VMEM((16, ROWS, 128), BF16),
            pltpu.VMEM((2, 8, ROWS, 128), BF16),
            sems((2,)),
            sems((2,)),
            sems((2,)),
            sems((2,)),
            sems((16,)),
            sems((2, 8)),
        ],
        compiler_params=pltpu.CompilerParams(
            collective_id=2, has_side_effects=True, vmem_limit_bytes=VMEM_LIMIT
        ),
        name="attention_backward",
    )(dout_pairs, key_values, queries, outputs, logs)


def head_pairs(values):
    return values.reshape(values.shape[0], 2, 128).transpose(1, 0, 2)


def shards(
    inputs,
    cotangent,
    attention_gain,
    query_gain,
    key_gain,
    w_query,
    key_weight,
    value_weight,
    w_out,
    feed_gain,
    w_gate,
    w_up,
    w_down,
):
    block_rows = inputs.shape[0]
    head_dim = query_gain.shape[0]
    z = lax.axis_index("head")
    positions = lax.axis_index("ctx") * block_rows + jnp.arange(block_rows, dtype=jnp.int32)
    cosine_table, sine_table = rotary_tables(positions, head_dim)
    rotate_head = partial(head_norm_rotate, cosine_table=cosine_table, sine_table=sine_table)
    input_rows = inputs.astype(F32)
    normalized_input = row_norm(input_rows, attention_gain).astype(BF16)
    query_raw = jnp.dot(normalized_input, w_query, preferred_element_type=F32)
    key_raw = jnp.dot(normalized_input, key_weight, preferred_element_type=F32)
    value_bf = jnp.dot(normalized_input, value_weight, preferred_element_type=F32).astype(BF16)
    query_rot, query_pull = jax.vjp(rotate_head, query_raw, query_gain)
    key_rot, key_pull = jax.vjp(rotate_head, key_raw, key_gain)
    key_bf = key_rot.astype(BF16)
    key_values = jnp.concatenate(
        [key_bf.reshape(block_rows, 2, head_dim), value_bf.reshape(block_rows, 2, head_dim)], -1
    ).transpose(1, 0, 2)
    role_kv, role_q, role_o, role_logs, attended, w_out_all = attention_forward(
        head_pairs(query_rot.astype(BF16)), key_values, w_out
    )
    attended_own = lax.dynamic_slice_in_dim(attended, z * 256, 256, 1)
    hidden_first = input_rows + contract_cols(attended, w_out_all)

    def own_rows(values):
        return lax.dynamic_slice_in_dim(values, z * 96, 96, 0)

    hidden_rows = own_rows(hidden_first)
    mixed = row_norm(hidden_first, feed_gain).astype(BF16)
    gate_rows = jnp.dot(mixed, w_gate, preferred_element_type=F32)
    up_rows = jnp.dot(mixed, w_up, preferred_element_type=F32)
    sigmoid_gate = jax.nn.sigmoid(gate_rows)
    silu_rows = gate_rows * sigmoid_gate
    inner_bf = (silu_rows * up_rows).astype(BF16)
    down_part = contract_cols(inner_bf, w_down)
    w_down_grad = contract_rows(cotangent, inner_bf)
    grad_inner = jnp.dot(cotangent, w_down, preferred_element_type=F32)
    grad_gate = (
        grad_inner * up_rows * sigmoid_gate * (1.0 + gate_rows * (1.0 - sigmoid_gate))
    ).astype(BF16)
    grad_up = (grad_inner * silu_rows).astype(BF16)
    w_gate_grad = contract_rows(mixed, grad_gate)
    w_up_grad = contract_rows(mixed, grad_up)
    mixed_part = contract_cols(grad_gate, w_gate) + contract_cols(grad_up, w_up)
    down_rows, grad_mixed_rows = z_reduce([down_part.astype(BF16), mixed_part.astype(BF16)], 3)
    block_out_rows = (hidden_rows + down_rows).astype(BF16)
    _, feed_pull = jax.vjp(row_norm, hidden_rows, feed_gain)
    hidden_from_norm, feed_gain_part = feed_pull(grad_mixed_rows)
    grad_hidden_rows = own_rows(cotangent).astype(F32) + hidden_from_norm
    block_out, grad_branch = z_gather([block_out_rows, grad_hidden_rows.astype(BF16)], 4)
    block_out = block_out.reshape(block_rows, -1)
    grad_branch = grad_branch.reshape(block_rows, -1)
    gate_sum, up_sum, down_sum = weight_reduce(
        [w_gate_grad.astype(BF16), w_up_grad.astype(BF16), w_down_grad.astype(BF16)],
        EARLY_ITEMS,
        5,
    )
    w_out_grad = contract_rows(grad_branch, attended_own)
    grad_attended = jnp.dot(grad_branch, w_out, preferred_element_type=F32).astype(BF16)
    grad_query, grad_kv = attention_backward(
        head_pairs(grad_attended), role_kv, role_q, role_o, role_logs
    )
    grad_key = grad_kv[:, :, :head_dim].transpose(1, 0, 2).reshape(block_rows, -1)
    grad_v = grad_kv[:, :, head_dim:].transpose(1, 0, 2).reshape(block_rows, -1).astype(BF16)
    query_raw_grad, query_gain_part = query_pull(grad_query.astype(F32))
    key_raw_grad, key_gain_part = key_pull(grad_key)
    grad_q = query_raw_grad.astype(BF16)
    grad_k = key_raw_grad.astype(BF16)
    w_query_grad = contract_rows(normalized_input, grad_q)
    w_key_grad = contract_rows(normalized_input, grad_k)
    w_value_grad = contract_rows(normalized_input, grad_v)
    normed_part = (
        contract_cols(grad_q, w_query)
        + contract_cols(grad_k, key_weight)
        + contract_cols(grad_v, value_weight)
    )
    (grad_normed_rows,) = z_reduce([normed_part.astype(BF16)], 6)
    _, attention_pull = jax.vjp(row_norm, own_rows(input_rows), attention_gain)
    input_from_norm, attention_gain_part = attention_pull(grad_normed_rows)
    input_grad_rows = grad_hidden_rows + input_from_norm
    gains = jnp.zeros((8, 1024), F32)
    gains = gains.at[0].set(attention_gain_part).at[1].set(feed_gain_part)
    gains = gains.at[2, :64].set(query_gain_part).at[3, :64].set(key_gain_part)
    input_grad, gains = z_gather([input_grad_rows.astype(BF16), gains], 7)
    input_grad = input_grad.reshape(block_rows, -1).astype(F32)
    gains = jnp.sum(gains, axis=0)

    def two_per_device(vector):
        return jnp.pad(vector[:64].reshape(32, 2), ((0, 0), (0, 30))).reshape(1024)

    chunk = jnp.stack(
        [gains[0], gains[1], two_per_device(gains[2]), two_per_device(gains[3])], axis=1
    )
    chunk = jnp.pad(chunk, ((0, 0), (0, 124)))
    query_sum, key_sum, value_sum, out_sum, gain_sum = weight_reduce(
        [
            w_query_grad.astype(BF16),
            w_key_grad.astype(BF16),
            w_value_grad.astype(BF16),
            w_out_grad.astype(BF16),
            chunk.astype(BF16),
        ],
        LATE_ITEMS,
        8,
    )
    return (
        block_out,
        input_grad,
        gain_sum[:, 0],
        gain_sum[:2, 2],
        gain_sum[:2, 3],
        query_sum,
        key_sum,
        value_sum,
        out_sum,
        gain_sum[:, 1],
        gate_sum,
        up_sum,
        down_sum,
    )


def solution(mesh):
    both = ("dp", "ctx")
    by_head = P(None, "head")
    reduced = P(both, "head")
    return jax.shard_map(
        shards,
        mesh=mesh,
        in_specs=(
            P(both, None),
            P(both, None),
            P(),
            P(),
            P(),
            by_head,
            by_head,
            by_head,
            by_head,
            P(),
            by_head,
            by_head,
            by_head,
        ),
        out_specs=(
            P(both, None),
            P(both, None),
            P(both),
            P(both),
            P(both),
            reduced,
            reduced,
            reduced,
            reduced,
            P(both),
            reduced,
            reduced,
            reduced,
        ),
        check_vma=False,
    )
```

```python
from functools import partial

import jax
import jax.numpy as jnp
import numpy as np
from jax import lax
from jax.experimental import pallas as pl
from jax.experimental.pallas import tpu as pltpu
from jax.sharding import PartitionSpec as P

epsilon = 1e-05
theta_base = 1000000.0
MESH = pl.DeviceIdType.MESH
F32 = jnp.float32
BF16 = jnp.bfloat16
ROWS = 384
LOG2E = 1.4426950408889634
VMEM_LIMIT = 56 * 1024 * 1024


def remote(src, dst, send_sem, recv_sem, d, c, z):
    return pltpu.make_async_remote_copy(
        src_ref=src,
        dst_ref=dst,
        send_sem=send_sem,
        recv_sem=recv_sem,
        device_id=(d, c, z),
        device_id_type=MESH,
    )


def local_sem(src, dst, sem):
    return pltpu.make_async_copy(src, dst, sem)


def place():
    return lax.axis_index("dp"), lax.axis_index("ctx"), lax.axis_index("head")


def role_of(d, c):
    sequence = jnp.where(c >= 8, 1, 0)
    low = jnp.where(c >= 8, 15 - c, c)
    return sequence, d, low, 15 - low


def spread_heads(pair, upper):
    pair = pair.astype(F32)
    lane = lax.broadcasted_iota(jnp.int32, pair.shape, 1)
    turned = pltpu.roll(pair, 64, 1)
    if upper:
        first, second = jnp.where(lane >= 64, turned, 0.0), jnp.where(lane >= 64, pair, 0.0)
    else:
        first, second = jnp.where(lane < 64, pair, 0.0), jnp.where(lane < 64, turned, 0.0)
    return first.astype(BF16), second.astype(BF16)


def nt(left, right):
    return lax.dot_general(left, right, (((1,), (1,)), ((), ())), preferred_element_type=F32)


def nn(left, right):
    return lax.dot_general(left, right, (((1,), (0,)), ((), ())), preferred_element_type=F32)


SCORE_SCALE = LOG2E / 8.0


def split_columns(half_width=32, rows=ROWS, blocks=16):
    lane = np.arange(128) % half_width
    frequency = theta_base ** (-2.0 * lane / (2 * half_width))
    row_angle = np.arange(rows)[:, None] * frequency[None, :]
    block_angle = (np.arange(blocks) * rows)[:, None] * frequency[None, :]
    return [
        np.asarray(table, np.float32)
        for table in (
            np.cos(row_angle),
            np.sin(row_angle),
            np.cos(block_angle),
            np.sin(block_angle),
        )
    ]


def tables(c, row_cos, row_sin, block_cos, block_sin):
    bc, bs = block_cos[pl.ds(c, 1), :], block_sin[pl.ds(c, 1), :]
    rc, rs = row_cos[...], row_sin[...]
    return rc * bc - rs * bs, rs * bc + rc * bs


def lanes(rows=ROWS):
    return lax.broadcasted_iota(jnp.int32, (rows, 128), 1)


def half_sums(values):
    lane = lanes(values.shape[0])
    first = jnp.sum(jnp.where(lane < 64, values, 0.0), axis=1, keepdims=True)
    second = jnp.sum(jnp.where(lane >= 64, values, 0.0), axis=1, keepdims=True)
    return jnp.where(lane < 64, first, second)


def turn(values):
    lane = lanes(values.shape[0])
    return jnp.where(lax.rem(lane, 64) < 32, -pltpu.roll(values, 96, 1), pltpu.roll(values, 32, 1))


def turn_back(values):
    lane = lanes(values.shape[0])
    return jnp.where(lax.rem(lane, 64) < 32, pltpu.roll(values, 96, 1), -pltpu.roll(values, 32, 1))


def pair_forward(raw, gain, cosine, sine):
    scale = lax.rsqrt(half_sums(raw * raw) * (1.0 / 64.0) + epsilon)
    normed = raw * scale * gain
    return normed * cosine + turn(normed) * sine


def pair_backward(grad, raw, gain, cosine, sine):
    incoming = grad * cosine + turn_back(grad * sine)
    scale = lax.rsqrt(half_sums(raw * raw) * (1.0 / 64.0) + epsilon)
    weighted = incoming * gain
    inner = half_sums(weighted * raw) * (1.0 / 64.0)
    raw_grad = scale * weighted - raw * (scale * scale * scale) * inner
    return raw_grad, jnp.sum(incoming * raw * scale, axis=0, keepdims=True)


def attention_forward_kernel(
    x_ref,
    gain_ref,
    wq_ref,
    wk_ref,
    wv_ref,
    qgain_ref,
    kgain_ref,
    row_cos,
    row_sin,
    block_cos,
    block_sin,
    wo_ref,
    kvs_ref,
    qs_ref,
    os_ref,
    l2_ref,
    oall_ref,
    wall_ref,
    normed_ref,
    qraw_ref,
    kraw_ref,
    q_ref,
    kv_ref,
    qz,
    acc,
    sums,
    q_send,
    q_recv,
    kv_send,
    kv_recv,
    o_send,
    o_recv,
    w_send,
    w_recv,
    wc_send,
    wc_recv,
):
    d, c, z = place()
    s, j_role, low, high = role_of(d, c)
    own_group = low
    slot = jnp.where(c >= 8, 1, 0)
    home = jnp.where(slot == d, c, 15 - c)

    barrier = pltpu.get_barrier_semaphore()

    def greet(index, carry):
        other_d, other_c = index // 16, lax.rem(index, 16)

        @pl.when((other_d != d) | (other_c != c))
        def _():
            pl.semaphore_signal(
                barrier, inc=1, device_id=(other_d, other_c, z), device_id_type=MESH
            )

        return carry

    lax.fori_loop(0, 32, greet, 0)
    for step in (1, 2, 3):
        other = lax.rem(z + step, 4)
        pl.semaphore_signal(barrier, inc=1, device_id=(d, c, other), device_id_type=MESH)
        for j in range(2):
            pl.semaphore_signal(barrier, inc=1, device_id=(j, home, other), device_id_type=MESH)

    x = x_ref[...].astype(F32)
    scale = lax.rsqrt(jnp.mean(x * x, axis=1, keepdims=True) + epsilon)
    normed_ref[...] = (x * scale * gain_ref[...]).astype(BF16)
    normed = normed_ref[...]
    cosine, sine = tables(c, row_cos, row_sin, block_cos, block_sin)
    key_raw = nn(normed, wk_ref[...])
    kraw_ref[...] = key_raw
    value = nn(normed, wv_ref[...])
    key = pair_forward(key_raw, kgain_ref[...], cosine, sine)
    lane = lanes()
    kv_ref[0] = jnp.where(lane < 64, key, pltpu.roll(value, 64, 1)).astype(BF16)
    kv_ref[1] = jnp.where(lane < 64, pltpu.roll(key, 64, 1), value).astype(BF16)
    pl.semaphore_wait(barrier, 31 + 3 + 6)

    def kv_target(k):
        group = lax.rem(own_group + k, 8)
        target = jnp.where(d == 0, group, 15 - group)
        return target, (15 - group) >= c

    def kv_copy(k, j, target):
        return remote(
            kv_ref.at[j], kvs_ref.at[c], kv_send.at[2 * k + j], kv_recv.at[c], j, target, z
        )

    def kv_start(k, carry):
        target, needed = kv_target(k)
        for j in range(2):
            here = (target == c) & (d == j)

            @pl.when(needed & jnp.logical_not(here))
            def _():
                kv_copy(k, j, target).start()

            @pl.when(needed & here)
            def _():
                local_sem(kv_ref.at[j], kvs_ref.at[c], kv_recv.at[c]).start()

        return carry

    kv_start(0, 0)
    query_raw = nn(normed, wq_ref[...])
    qraw_ref[...] = query_raw
    for j in range(2):
        pair = query_raw[:, j * 128 : (j + 1) * 128]
        q_ref[j] = pair_forward(pair, qgain_ref[...], cosine, sine).astype(BF16)
        here = (home == c) & (d == j)

        @pl.when(jnp.logical_not(here))
        def _():
            remote(q_ref.at[j], qs_ref.at[slot], q_send.at[j], q_recv.at[slot], j, home, z).start()

        @pl.when(here)
        def _():
            local_sem(q_ref.at[j], qs_ref.at[slot], q_recv.at[slot]).start()

    lax.fori_loop(1, 8, kv_start, 0)

    column = pl.ds(pl.multiple_of(z * 256, 256), 256)
    mine = pl.ds(pl.multiple_of(d * 512, 512), 512)
    wall_ref[:, column] = wo_ref[...]
    w_copies = []
    for step in (1, 2, 3):
        copy = remote(
            wall_ref.at[mine, column],
            wall_ref.at[mine, column],
            w_send.at[step - 1],
            w_recv.at[step - 1],
            d,
            c,
            lax.rem(z + step, 4),
        )
        copy.start()
        w_copies.append(copy)

    acc[...] = jnp.zeros_like(acc)
    sums[...] = jnp.zeros_like(sums)
    for which in range(2):
        local_sem(q_ref.at[0], qs_ref.at[which], q_recv.at[which]).wait()
        first, second = spread_heads(qs_ref[which], False)
        qz[which, 0:ROWS, :] = first
        qz[which, ROWS : 2 * ROWS, :] = second

    def kv_wait(block):
        local_sem(kv_ref.at[0], kvs_ref.at[block], kv_recv.at[block]).wait()

    def tile(block, which, masked):
        keys = kvs_ref[block]
        for head in range(2):
            rows = slice(head * ROWS, (head + 1) * ROWS)
            weights = jnp.exp2(nt(qz[which, rows, :], keys) * SCORE_SCALE)
            if masked:
                row = lax.broadcasted_iota(jnp.int32, weights.shape, 0)
                key = lax.broadcasted_iota(jnp.int32, weights.shape, 1)
                weights = jnp.where(row >= key, weights, 0.0)
            sums[which, rows, :] += weights[:, 0:128] + weights[:, 128:256] + weights[:, 256:384]
            acc[which, rows, :] += nn(weights.astype(BF16), keys)

    kv_wait(low)
    kv_wait(high)
    tile(low, 1, False)
    tile(low, 0, True)
    tile(high, 1, True)

    def step(k, carry):
        first = lax.rem(own_group + 8 - k, 8)
        below = first < own_group
        kv_wait(first)

        @pl.when(jnp.logical_not(below))
        def _():
            kv_wait(15 - first)

        tile(first, 1, False)
        tile(jnp.where(below, first, 15 - first), jnp.where(below, 0, 1), False)
        return carry

    lax.fori_loop(1, 8, step, 0)

    def o_copy(which, step):
        block = high if which else low
        other = lax.rem(z + step, 4)
        there = oall_ref.at[:, pl.ds(pl.multiple_of(z * 256 + j_role * 128, 128), 128)]
        arrived = o_recv.at[z * 2 + j_role]
        return os_ref.at[which], there, o_send.at[which, step], arrived, s, block, other

    for which in range(2):
        total = jnp.sum(sums[which], axis=1, keepdims=True)
        result = acc[which] / total
        os_ref[which] = jnp.where(
            lane < 64, pltpu.roll(result[:ROWS], 64, 1), result[ROWS:]
        ).astype(BF16)
        block = high if which else low
        here = (s == d) & (block == c)
        for step in (2, 1, 3):
            remote(*o_copy(which, step)).start()

        @pl.when(jnp.logical_not(here))
        def _():
            remote(*o_copy(which, 0)).start()

        @pl.when(here)
        def _():
            source, there, _, arrived = o_copy(which, 0)[:4]
            local_sem(source, there, arrived).start()

        logs = jnp.broadcast_to(jnp.log2(total), (2 * ROWS, 128))
        l2_ref[which] = logs.T[0:8]

    forwards = []
    for step in (1, 2, 3):
        w_copies[step - 1].wait_recv()
        other = pl.ds(pl.multiple_of(lax.rem(z + 4 - step, 4) * 256, 256), 256)
        copy = remote(
            wall_ref.at[mine, other],
            wall_ref.at[mine, other],
            wc_send.at[step - 1],
            wc_recv.at[step - 1],
            1 - d,
            c,
            z,
        )
        copy.start()
        forwards.append(copy)
    for copy in forwards:
        copy.wait_recv()
    for source in range(4):
        for j in range(2):
            there = oall_ref.at[:, source * 256 + j * 128 : source * 256 + (j + 1) * 128]
            local_sem(os_ref.at[0], there, o_recv.at[source * 2 + j]).wait()

    for copy in w_copies + forwards:
        copy.wait_send()
    for j in range(2):

        @pl.when(jnp.logical_not((home == c) & (d == j)))
        def _():
            remote(q_ref.at[j], qs_ref.at[slot], q_send.at[j], q_recv.at[slot], j, home, z).wait_send()

    def kv_sent(k, carry):
        target, needed = kv_target(k)
        for j in range(2):

            @pl.when(needed & jnp.logical_not((target == c) & (d == j)))
            def _():
                kv_copy(k, j, target).wait_send()

        return carry

    lax.fori_loop(0, 8, kv_sent, 0)
    for which in range(2):
        block = high if which else low
        for step in (1, 2, 3):
            remote(*o_copy(which, step)).wait_send()

        @pl.when(jnp.logical_not((s == d) & (block == c)))
        def _():
            remote(*o_copy(which, 0)).wait_send()


def z_send(source_of, landed, send_sem, recv_sem, d, c, z):
    copies = []
    for step in (1, 2, 3):
        other = lax.rem(z + step, 4)
        copy = remote(
            source_of(other),
            landed(step),
            send_sem.at[step - 1],
            recv_sem.at[step - 1],
            d,
            c,
            other,
        )
        copy.start()
        copies.append(copy)
    return copies


def feed_kernel(
    x_ref,
    oall_ref,
    wall_ref,
    gain_ref,
    cot_ref,
    wg_ref,
    wu_ref,
    wd_ref,
    down_ref,
    hrows_ref,
    ghrows_ref,
    branch_ref,
    dob_ref,
    feed_ref,
    held_g,
    held_u,
    held_d,
    hidden,
    scale,
    mixed,
    mixed_t,
    cot_t,
    inner,
    grad_gate,
    grad_up,
    mixed_part,
    part_send,
    part_land,
    dw_g,
    dw_u,
    dw_d,
    land_g,
    land_u,
    land_d,
    z_sems,
    core_sems,
):
    d, c, z = place()
    barrier = pltpu.get_barrier_semaphore()
    for step in (1, 2, 3):
        pl.semaphore_signal(
            barrier, inc=1, device_id=(d, c, lax.rem(z + step, 4)), device_id_type=MESH
        )
    pl.semaphore_signal(barrier, inc=1, device_id=(1 - d, c, z), device_id_type=MESH)

    def project(t, carry):
        columns = pl.ds(pl.multiple_of(t * 256, 256), 256)
        hidden[:, columns] = x_ref[:, columns].astype(F32) + nt(oall_ref[...], wall_ref[columns, :])
        return carry

    lax.fori_loop(0, 4, project, 0)

    def normalize(r, carry):
        rows = pl.ds(pl.multiple_of(r * 96, 96), 96)
        values = hidden[rows, :]
        factor = lax.rsqrt(jnp.mean(values * values, axis=1, keepdims=True) + epsilon)
        scale[rows, :] = jnp.broadcast_to(factor, (96, 128))
        mixed[rows, :] = (values * factor * gain_ref[...]).astype(BF16)
        return carry

    lax.fori_loop(0, 4, normalize, 0)
    mixed_part[...] = jnp.zeros_like(mixed_part)

    def units(t, carry):
        columns = pl.ds(pl.multiple_of(t * 384, 384), 384)
        gate = nn(mixed[...], wg_ref[:, columns])
        up = nn(mixed[...], wu_ref[:, columns])
        sigmoid = 1.0 / (1.0 + jnp.exp(-gate))
        silu = gate * sigmoid
        inner[:, columns] = (silu * up).astype(BF16)
        grad_inner = nn(cot_ref[...], wd_ref[:, columns])
        grad_up[:, columns] = (grad_inner * silu).astype(BF16)
        grad_gate[:, columns] = (
            grad_inner * up * sigmoid * (1.0 + gate * (1.0 - sigmoid))
        ).astype(BF16)
        mixed_part[...] += nt(grad_gate[:, columns], wg_ref[:, columns]) + nt(
            grad_up[:, columns], wu_ref[:, columns]
        )
        return carry

    lax.fori_loop(0, 3, units, 0)
    for other in range(4):
        part_send[other] = mixed_part[other * 96 : (other + 1) * 96, :].astype(BF16)
    pl.semaphore_wait(barrier, 4)
    reduce = z_send(
        lambda other: part_send.at[other],
        lambda step: part_land.at[step - 1],
        z_sems.at[0],
        z_sems.at[1],
        d,
        c,
        z,
    )

    def transpose(t, carry):
        columns = pl.ds(pl.multiple_of(t * 128, 128), 128)
        mixed_t[columns, :] = mixed[:, columns].T
        cot_t[columns, :] = cot_ref[:, columns].T
        return carry

    lax.fori_loop(0, 8, transpose, 0)
    theirs = pl.ds(pl.multiple_of((1 - d) * 512, 512), 512)
    ours = pl.multiple_of(d * 512, 512)
    cores = []
    for index, (left, right, out, land) in enumerate(
        (
            (mixed_t, grad_gate, dw_g, land_g),
            (mixed_t, grad_up, dw_u, land_u),
            (cot_t, inner, dw_d, land_d),
        )
    ):

        def weights(t, carry):
            columns = pl.ds(pl.multiple_of(t * 384, 384), 384)
            out[:, columns] = nn(left[...], right[:, columns]).astype(BF16)
            return carry

        lax.fori_loop(0, 3, weights, 0)
        copy = remote(
            out.at[theirs], land, core_sems.at[0, index], core_sems.at[1, index], 1 - d, c, z
        )
        copy.start()
        cores.append(copy)

    for copy in reduce:
        copy.wait_recv()
    rows = pl.ds(pl.multiple_of(z * 96, 96), 96)
    incoming = mixed_part[rows, :]
    for step in range(3):
        incoming = incoming + part_land[step].astype(F32)
    values = hidden[rows, :]
    factor = scale[rows, 0:1]
    hrows_ref[...] = values
    weighted = incoming * gain_ref[...]
    projected = jnp.sum(weighted * values, axis=1, keepdims=True) * (1.0 / 1024.0)
    grad_rows = (
        cot_ref[rows, :].astype(F32)
        + factor * weighted
        - values * (factor * factor * factor * projected)
    )
    feed_ref[...] = jnp.broadcast_to(
        jnp.sum(incoming * values * factor, axis=0, keepdims=True), (8, 1024)
    )
    ghrows_ref[...] = grad_rows
    branch_ref[...] = grad_rows.astype(BF16)

    def attended(t, carry):
        columns = pl.ds(pl.multiple_of(t * 256, 256), 256)
        dob_ref[:, columns] = nn(branch_ref[...], wall_ref[:, columns]).astype(BF16)
        return carry

    lax.fori_loop(0, 4, attended, 0)

    def down(t, carry):
        columns = pl.ds(pl.multiple_of(t * 256, 256), 256)
        value = nt(inner[...], wd_ref[columns, :])
        for other in range(4):
            down_ref[other, :, columns] = value[other * 96 : (other + 1) * 96].astype(BF16)
        return carry

    lax.fori_loop(0, 4, down, 0)
    for copy, out, land, held in zip(
        cores, (dw_g, dw_u, dw_d), (land_g, land_u, land_d), (held_g, held_u, held_d)
    ):
        copy.wait_recv()

        def add(r, carry):
            here = pl.ds(pl.multiple_of(ours + r * 128, 128), 128)
            there = pl.ds(pl.multiple_of(r * 128, 128), 128)
            held[there, :] = (out[here, :].astype(F32) + land[there, :].astype(F32)).astype(BF16)
            return carry

        lax.fori_loop(0, 4, add, 0)
    for copy in reduce + cores:
        copy.wait_send()


class PlaneSum:
    def __init__(self, index, source, y_first, buffers, sems):
        self.index, self.source, self.y_first = index, source, y_first
        self.own, self.landed, self.summed, self.landed_last = buffers
        self.own_sem, self.first_sems, self.last_sems = sems
        self.d, c, self.z = place()
        self.y, self.x = c // 4, lax.rem(c, 4)

    def along(self, first, step):
        if first == self.y_first:
            other = lax.rem(self.y + step, 4)
            return other, other * 4 + self.x
        other = lax.rem(self.x + step, 4)
        return other, self.y * 4 + other

    def part(self, place_):
        return self.source.at[place_] if self.y_first else self.source.at[:, place_]

    def start(self):
        self.firsts = []
        for step in (2, 1, 3):
            other, chip = self.along(True, step)
            copy = remote(
                self.part(other),
                self.landed.at[step - 1],
                self.first_sems.at[0, self.index, step - 1],
                self.first_sems.at[1, self.index, step - 1],
                self.d,
                chip,
                self.z,
            )
            copy.start()
            self.firsts.append(copy)
        self.load = local_sem(
            self.part(self.y if self.y_first else self.x), self.own, self.own_sem.at[self.index]
        )
        self.load.start()

    def middle(self):
        self.load.wait()
        for copy in self.firsts:
            copy.wait_recv()

        def add(r, carry):
            total = self.own[r].astype(F32)
            for step in range(3):
                total = total + self.landed[step, r].astype(F32)
            self.summed[r] = total.astype(BF16)
            return carry

        lax.fori_loop(0, 4, add, 0)
        self.lasts = []
        for step in (2, 1, 3):
            other, chip = self.along(False, step)
            copy = remote(
                self.summed.at[other],
                self.landed_last.at[step - 1],
                self.last_sems.at[0, self.index, step - 1],
                self.last_sems.at[1, self.index, step - 1],
                self.d,
                chip,
                self.z,
            )
            copy.start()
            self.lasts.append(copy)

    def finish(self):
        for copy in self.lasts:
            copy.wait_recv()
        total = self.summed[self.x if self.y_first else self.y].astype(F32)
        for step in range(3):
            total = total + self.landed_last[step].astype(F32)
        return total

    def sent(self):
        for copy in self.firsts + self.lasts:
            copy.wait_send()


def plane_sum_scratch(widths):
    number = len(widths)
    scratch = []
    for width in widths:
        for lead in ((4,), (3, 4), (4,), (3,)):
            scratch.append(pltpu.VMEM(lead + (32, width), BF16))
    return scratch + [
        pltpu.SemaphoreType.DMA((number,)),
        pltpu.SemaphoreType.DMA((2, number, 3)),
        pltpu.SemaphoreType.DMA((2, number, 3)),
    ]


def plane_sums(sources, y_firsts, scratch):
    number = len(sources)
    return [
        PlaneSum(i, sources[i], y_firsts[i], scratch[4 * i : 4 * i + 4], scratch[4 * number :])
        for i in range(number)
    ]


BACKWARD_ITEMS = ((0, 0, 640, True), (0, 640, 512, False), (1, 0, 256, True), (1, 256, 384, False))
FINAL_ITEMS = ((0, 640, 256, True), (0, 896, 256, False), (1, 0, 512, True), (1, 512, 640, False))
LATE_ITEMS = ((0, 384, True), (384, 384, False))


def attention_backward_kernel(
    dob_ref,
    kvs_ref,
    qs_ref,
    os_ref,
    l2_ref,
    down_ref,
    hrows_ref,
    branch_ref,
    held_g,
    held_u,
    dq_ref,
    dkv_ref,
    block_ref,
    branches_ref,
    gate_ref,
    up_ref,
    qz,
    doz,
    delta,
    dos,
    dqt,
    dq_out,
    dq_in,
    dkv_out,
    dkv_in,
    down_land,
    do_send,
    do_recv,
    dq_send,
    dq_recv,
    dkv_send,
    dkv_recv,
    z_sems,
    *sum_scratch,
):
    d, c, z = place()
    s, j_role, low, high = role_of(d, c)
    own_group = low
    slot = jnp.where(c >= 8, 1, 0)
    home = jnp.where(slot == d, c, 15 - c)
    barrier = pltpu.get_barrier_semaphore()

    def greet(index, carry):
        other_d, other_c = index // 16, lax.rem(index, 16)

        @pl.when((other_d != d) | (other_c != c))
        def _():
            pl.semaphore_signal(
                barrier, inc=1, device_id=(other_d, other_c, z), device_id_type=MESH
            )

        return carry

    lax.fori_loop(0, 32, greet, 0)
    for step in (1, 2, 3):
        other = lax.rem(z + step, 4)
        pl.semaphore_signal(barrier, inc=1, device_id=(d, c, other), device_id_type=MESH)
        for block in (low, high):
            pl.semaphore_signal(barrier, inc=1, device_id=(s, block, other), device_id_type=MESH)
    pl.semaphore_wait(barrier, 31 + 3 + 6)

    def do_copy(j, step):
        other = lax.rem(z + step, 4)
        source = dob_ref.at[:, pl.ds(pl.multiple_of(other * 256 + j * 128, 128), 128)]
        there = dos.at[slot, pl.ds(pl.multiple_of(z * 96, 96), 96)]
        return source, there, do_send.at[j, step], do_recv.at[slot, z], j, home, other

    for j in range(2):
        for step in (2, 1, 3):
            remote(*do_copy(j, step)).start()
        here = (home == c) & (d == j)

        @pl.when(jnp.logical_not(here))
        def _():
            remote(*do_copy(j, 0)).start()

        @pl.when(here)
        def _():
            source, there, _, arrived = do_copy(j, 0)[:4]
            local_sem(source, there, arrived).start()

    reduce = z_send(
        lambda other: down_ref.at[other],
        lambda step: down_land.at[step - 1],
        z_sems.at[0, 0],
        z_sems.at[0, 1],
        d,
        c,
        z,
    )
    gather = z_send(
        lambda other: branch_ref,
        lambda step: branches_ref.at[z],
        z_sems.at[1, 0],
        z_sems.at[1, 1],
        d,
        c,
        z,
    )
    sources = [
        (held_g, held_u)[index].at[:, :, :, start : start + width]
        for index, start, width, _ in BACKWARD_ITEMS
    ]
    sums = plane_sums(sources, [item[3] for item in BACKWARD_ITEMS], sum_scratch)
    for item in sums:
        item.start()
    branches_ref[z] = branch_ref[...]

    dqt[...] = jnp.zeros_like(dqt)
    for which in range(2):
        first, second = spread_heads(qs_ref[which], False)
        qz[which, 0:ROWS, :] = first
        qz[which, ROWS : 2 * ROWS, :] = second
    for which in range(2):
        for source in range(4):
            there = dos.at[which, source * 96 : (source + 1) * 96]
            local_sem(dob_ref.at[:, 0:128], there, do_recv.at[which, source]).wait()
        first, second = spread_heads(dos[which], True)
        doz[which, 0:ROWS, :] = first
        doz[which, ROWS : 2 * ROWS, :] = second
        product = (dos[which].astype(F32) * os_ref[which].astype(F32)).T
        delta[which, :, 0:ROWS] = jnp.broadcast_to(
            jnp.sum(product[0:64], axis=0, keepdims=True), (8, ROWS)
        )
        delta[which, :, ROWS : 2 * ROWS] = jnp.broadcast_to(
            jnp.sum(product[64:128], axis=0, keepdims=True), (8, ROWS)
        )

    lane = lanes()
    key_scale = jnp.where(lane < 64, 0.125, 1.0)

    def tile(block, which, masked):
        keys = kvs_ref[block]
        keys_t = keys.T
        result = None
        for head in range(2):
            rows = slice(head * ROWS, (head + 1) * ROWS)
            q_rows = qz[which, rows, :]
            do_rows = doz[which, rows, :]
            weights = jnp.exp2(nt(keys, q_rows) * SCORE_SCALE - l2_ref[which, 0:1, rows])
            if masked:
                key = lax.broadcasted_iota(jnp.int32, weights.shape, 0)
                row = lax.broadcasted_iota(jnp.int32, weights.shape, 1)
                weights = jnp.where(row >= key, weights, 0.0)
            score_grad = (weights * (nt(keys, do_rows) - delta[which, 0:1, rows])).astype(BF16)
            part = nn(score_grad, q_rows) + nn(weights.astype(BF16), do_rows)
            result = part if result is None else result + part
            dqt[which, :, rows] += nn(keys_t, score_grad)
        return result * key_scale

    def dkv_copy(block):
        return (
            dkv_out.at[block],
            dkv_in.at[j_role, own_group],
            dkv_send.at[block],
            dkv_recv.at[j_role, own_group],
            s,
            block,
            z,
        )

    def send(block):
        here = (s == d) & (block == c)

        @pl.when(jnp.logical_not(here))
        def _():
            remote(*dkv_copy(block)).start()

        @pl.when(here)
        def _():
            source, there, _, arrived = dkv_copy(block)[:4]
            local_sem(source, there, arrived).start()

    dkv_out[low] = (tile(low, 1, False) + tile(low, 0, True)).astype(BF16)
    send(low)
    dkv_out[high] = tile(high, 1, True).astype(BF16)
    send(high)

    def step(k, carry):
        first = lax.rem(own_group + 8 - k, 8)
        below = first < own_group
        one = tile(first, 1, False)
        two = tile(jnp.where(below, first, 15 - first), jnp.where(below, 0, 1), False)

        @pl.when(below)
        def _():
            dkv_out[first] = (one + two).astype(BF16)
            send(first)

        @pl.when(jnp.logical_not(below))
        def _():
            dkv_out[first] = one.astype(BF16)
            send(first)
            dkv_out[15 - first] = two.astype(BF16)
            send(15 - first)

        return carry

    lax.fori_loop(1, 8, step, 0)

    def dq_copy(which):
        block = high if which else low
        return (
            dq_out.at[which],
            dq_in.at[j_role],
            dq_send.at[which],
            dq_recv.at[j_role],
            s,
            block,
            z,
        )

    for which in range(2):
        flat = dqt[which].T * 0.125
        dq_out[which] = jnp.where(
            lane < 64, flat[:ROWS], pltpu.roll(flat[ROWS:], 64, 1)
        ).astype(BF16)
        block = high if which else low
        here = (s == d) & (block == c)

        @pl.when(jnp.logical_not(here))
        def _():
            remote(*dq_copy(which)).start()

        @pl.when(here)
        def _():
            source, there, _, arrived = dq_copy(which)[:4]
            local_sem(source, there, arrived).start()

    for copy in reduce:
        copy.wait_recv()
    total = hrows_ref[...] + down_ref[z].astype(F32)
    for step in range(3):
        total = total + down_land[step].astype(F32)
    block_ref[z] = total.astype(BF16)
    last = z_send(
        lambda other: block_ref.at[z],
        lambda step: block_ref.at[z],
        z_sems.at[2, 0],
        z_sems.at[2, 1],
        d,
        c,
        z,
    )
    for item in sums:
        item.middle()

    for j in range(2):
        dkv_ref[j] = jnp.zeros((ROWS, 128), F32)

    def collect(k, carry):
        group = lax.rem(own_group + k, 8)

        @pl.when((15 - group) >= c)
        def _():
            for j in range(2):
                local_sem(dkv_out.at[0], dkv_in.at[j, group], dkv_recv.at[j, group]).wait()
                dkv_ref[j] += dkv_in[j, group].astype(F32)

        return carry

    lax.fori_loop(0, 8, collect, 0)
    for j in range(2):
        local_sem(dq_out.at[0], dq_in.at[j], dq_recv.at[j]).wait()
        dq_ref[:, j * 128 : (j + 1) * 128] = dq_in[j]
    for item, (index, start, width, _) in zip(sums, BACKWARD_ITEMS):
        (gate_ref, up_ref)[index][:, start : start + width] = item.finish()
    for copy in gather + last:
        copy.wait_recv()

    for item in sums:
        item.sent()
    for copy in reduce + gather + last:
        copy.wait_send()
    for j in range(2):
        for step in (1, 2, 3):
            remote(*do_copy(j, step)).wait_send()

        @pl.when(jnp.logical_not((home == c) & (d == j)))
        def _():
            remote(*do_copy(j, 0)).wait_send()

    for which in range(2):
        block = high if which else low

        @pl.when(jnp.logical_not((s == d) & (block == c)))
        def _():
            remote(*dq_copy(which)).wait_send()

    def sent(block, carry):
        @pl.when((block <= high) & jnp.logical_not((s == d) & (block == c)))
        def _():
            remote(*dkv_copy(block)).wait_send()

        return carry

    lax.fori_loop(0, 16, sent, 0)


def final_kernel(
    dq_ref,
    dkv_ref,
    qraw_ref,
    kraw_ref,
    normed_ref,
    x_ref,
    gain_ref,
    qgain_ref,
    kgain_ref,
    row_cos,
    row_sin,
    block_cos,
    block_sin,
    wq_ref,
    wk_ref,
    wv_ref,
    oall_ref,
    branches_ref,
    ghrows_ref,
    feed_ref,
    held_u,
    held_d,
    input_ref,
    late_ref,
    gains_ref,
    up_ref,
    down_ref,
    grads,
    transposed,
    part,
    part_land,
    late,
    late_land,
    late_held,
    gather_rows,
    gains,
    gains_land,
    chunk_in,
    chunk,
    chunk_land,
    chunk_held,
    z_sems,
    core_sems,
    *sum_scratch,
):
    d, c, z = place()
    y, x = c // 4, lax.rem(c, 4)
    barrier = pltpu.get_barrier_semaphore()
    pl.semaphore_signal(barrier, inc=1, device_id=(1 - d, c, z), device_id_type=MESH)
    for step in (1, 2, 3):
        for other in (lax.rem(y + step, 4) * 4 + x, y * 4 + lax.rem(x + step, 4)):
            pl.semaphore_signal(barrier, inc=1, device_id=(d, other, z), device_id_type=MESH)
        pl.semaphore_signal(
            barrier, inc=1, device_id=(d, c, lax.rem(z + step, 4)), device_id_type=MESH
        )
    pl.semaphore_wait(barrier, 10)
    sources = [
        (held_u, held_d)[index].at[:, :, :, start : start + width]
        for index, start, width, _ in FINAL_ITEMS
    ]
    sources += [late_held.at[:, :, :, start : start + width] for start, width, _ in LATE_ITEMS]
    sources += [chunk_held]
    y_firsts = [item[3] for item in FINAL_ITEMS] + [item[2] for item in LATE_ITEMS] + [True]
    sums = plane_sums(sources, y_firsts, sum_scratch)
    early_sums, late_sums, gain_sum = sums[:4], sums[4:6], sums[6]
    for item in early_sums:
        item.start()

    cosine, sine = tables(c, row_cos, row_sin, block_cos, block_sin)
    lane = lanes()
    query_part = jnp.zeros((1, 128), F32)
    for j in range(2):
        columns = slice(j * 128, (j + 1) * 128)
        raw_grad, gain_part = pair_backward(
            dq_ref[:, columns].astype(F32), qraw_ref[:, columns], qgain_ref[...], cosine, sine
        )
        grads[:, columns] = raw_grad.astype(BF16)
        query_part = query_part + gain_part
    first, second = dkv_ref[0], dkv_ref[1]
    raw_grad, key_part = pair_backward(
        jnp.where(lane < 64, first, pltpu.roll(second, 64, 1)),
        kraw_ref[...],
        kgain_ref[...],
        cosine,
        sine,
    )
    grads[:, 256:384] = raw_grad.astype(BF16)
    grads[:, 384:512] = jnp.where(lane < 64, pltpu.roll(first, 64, 1), second).astype(BF16)

    def project(t, carry):
        columns = pl.ds(pl.multiple_of(t * 256, 256), 256)
        value = (
            nt(grads[:, 0:256], wq_ref[columns, :])
            + nt(grads[:, 256:384], wk_ref[columns, :])
            + nt(grads[:, 384:512], wv_ref[columns, :])
        ).astype(BF16)
        for other in range(4):
            part[other, :, columns] = value[other * 96 : (other + 1) * 96]
        return carry

    lax.fori_loop(0, 4, project, 0)
    reduce = z_send(
        lambda other: part.at[other],
        lambda step: part_land.at[step - 1],
        z_sems.at[0, 0],
        z_sems.at[0, 1],
        d,
        c,
        z,
    )

    def transpose(t, carry):
        columns = pl.ds(pl.multiple_of(t * 128, 128), 128)
        transposed[columns, :] = normed_ref[:, columns].T
        return carry

    lax.fori_loop(0, 8, transpose, 0)
    late[:, 0:512] = nn(transposed[...], grads[...]).astype(BF16)

    def transpose_branch(t, carry):
        columns = pl.ds(pl.multiple_of(t * 128, 128), 128)
        transposed[columns, :] = branches_ref[:, columns].T
        return carry

    lax.fori_loop(0, 8, transpose_branch, 0)
    own_heads = oall_ref[:, pl.ds(pl.multiple_of(z * 256, 256), 256)]
    late[:, 512:768] = nn(transposed[...], own_heads).astype(BF16)
    theirs = pl.ds(pl.multiple_of((1 - d) * 512, 512), 512)
    ours = pl.multiple_of(d * 512, 512)
    late_core = remote(
        late.at[theirs], late_land, core_sems.at[0, 0], core_sems.at[1, 0], 1 - d, c, z
    )
    late_core.start()

    for copy in reduce:
        copy.wait_recv()
    rows = pl.ds(pl.multiple_of(z * 96, 96), 96)
    incoming = part[z].astype(F32)
    for step in range(3):
        incoming = incoming + part_land[step].astype(F32)
    values = x_ref[rows, :].astype(F32)
    factor = lax.rsqrt(jnp.mean(values * values, axis=1, keepdims=True) + epsilon)
    weighted = incoming * gain_ref[...]
    projected = jnp.sum(weighted * values, axis=1, keepdims=True) * (1.0 / 1024.0)
    gains[...] = jnp.zeros_like(gains)
    gains[0:1, :] = jnp.sum(incoming * values * factor, axis=0, keepdims=True)
    gains[1:2, :] = feed_ref[0:1, :]
    gains[2:3, 0:128] = query_part + pltpu.roll(query_part, 64, 1)
    gains[3:4, 0:128] = key_part + pltpu.roll(key_part, 64, 1)
    gains_copies = z_send(
        lambda other: gains,
        lambda step: gains_land.at[step - 1],
        z_sems.at[1, 0],
        z_sems.at[1, 1],
        d,
        c,
        z,
    )
    gather_rows[z] = (
        ghrows_ref[...] + factor * weighted - values * (factor * factor * factor * projected)
    ).astype(BF16)
    gather = z_send(
        lambda other: gather_rows.at[z],
        lambda step: gather_rows.at[z],
        z_sems.at[2, 0],
        z_sems.at[2, 1],
        d,
        c,
        z,
    )

    late_core.wait_recv()

    def add_late(r, carry):
        for part_ in range(4):
            here = pl.ds(pl.multiple_of(ours + r * 128 + part_ * 32, 32), 32)
            there = pl.ds(pl.multiple_of(r * 128 + part_ * 32, 32), 32)
            late_held[r, part_] = (
                late[here, :].astype(F32) + late_land[there, :].astype(F32)
            ).astype(BF16)
        return carry

    lax.fori_loop(0, 4, add_late, 0)
    for item in late_sums:
        item.start()

    for copy in gains_copies:
        copy.wait_recv()
    chunk_in[...] = jnp.zeros_like(chunk_in)
    chunk_in[0:8, :] = gains[...] + gains_land[0] + gains_land[1] + gains_land[2]
    column_part = chunk_in[...].T
    row_index = lax.broadcasted_iota(jnp.int32, (1024, 128), 0)
    lane_index = lax.broadcasted_iota(jnp.int32, (1024, 128), 1)
    row_kind = lax.rem(row_index, 32)
    query_total, key_total = chunk_in[2:3, 0:128], chunk_in[3:4, 0:128]
    spread = jnp.where(
        row_kind == 0, query_total, jnp.where(row_kind == 1, key_total, 0.0)
    )
    chunk[...] = jnp.where(lane_index < 64, column_part, spread).astype(BF16)
    chunk_core = remote(
        chunk.at[theirs], chunk_land, core_sems.at[0, 1], core_sems.at[1, 1], 1 - d, c, z
    )
    chunk_core.start()
    for item in early_sums:
        item.middle()
    chunk_core.wait_recv()
    for r in range(4):
        for part_ in range(4):
            here = pl.ds(pl.multiple_of(ours + r * 128 + part_ * 32, 32), 32)
            there = slice(r * 128 + part_ * 32, r * 128 + part_ * 32 + 32)
            chunk_held[r, part_] = (
                chunk[here, :].astype(F32) + chunk_land[there, :].astype(F32)
            ).astype(BF16)
    gain_sum.start()
    for item in late_sums:
        item.middle()
    gain_sum.middle()
    for copy in gather:
        copy.wait_recv()
    for other in range(4):
        input_ref[other * 96 : (other + 1) * 96, :] = gather_rows[other].astype(F32)
    for item, (index, start, width, _) in zip(early_sums, FINAL_ITEMS):
        offset = start - 640 if index == 0 else start
        (up_ref, down_ref)[index][:, offset : offset + width] = item.finish()
    for item, (start, width, _) in zip(late_sums, LATE_ITEMS):
        late_ref[:, start : start + width] = item.finish()
    gains_ref[...] = gain_sum.finish()
    for item in sums:
        item.sent()
    late_core.wait_send()
    chunk_core.wait_send()
    for copy in reduce + gains_copies + gather:
        copy.wait_send()


def kernel_call(body, collective_id, name, ins, outs, scratch, any_inputs=()):
    vmem, anywhere = pl.BlockSpec(memory_space=pltpu.VMEM), pl.BlockSpec(memory_space=pl.ANY)
    return pl.pallas_call(
        body,
        out_shape=[jax.ShapeDtypeStruct(shape, kind) for shape, kind in outs],
        in_specs=[anywhere if i in any_inputs else vmem for i in range(len(ins))],
        out_specs=[vmem] * len(outs),
        scratch_shapes=scratch,
        compiler_params=pltpu.CompilerParams(
            collective_id=collective_id, has_side_effects=True, vmem_limit_bytes=VMEM_LIMIT
        ),
        name=name,
    )(*ins)


def shards(
    inputs,
    cotangent,
    attention_gain,
    query_gain,
    key_gain,
    w_query,
    key_weight,
    value_weight,
    w_out,
    feed_gain,
    w_gate,
    w_up,
    w_down,
):
    dma, v = pltpu.SemaphoreType.DMA, pltpu.VMEM
    position_tables = [jnp.asarray(table) for table in split_columns()]
    attention_gain = attention_gain.reshape(1, 1024)
    feed_gain = feed_gain.reshape(1, 1024)
    query_gain = jnp.tile(query_gain, 2).reshape(1, 128)
    key_gain = jnp.tile(key_gain, 2).reshape(1, 128)
    role_kv, role_q, role_o, role_logs, attended, w_out_all, normed, query_raw, key_raw = kernel_call(
        attention_forward_kernel,
        1,
        "attention_forward",
        [
            inputs,
            attention_gain,
            w_query,
            key_weight,
            value_weight,
            query_gain,
            key_gain,
            *position_tables,
            w_out,
        ],
        [
            ((16, ROWS, 128), BF16),
            ((2, ROWS, 128), BF16),
            ((2, ROWS, 128), BF16),
            ((2, 8, 2 * ROWS), F32),
            ((ROWS, 1024), BF16),
            ((1024, 1024), BF16),
            ((ROWS, 1024), BF16),
            ((ROWS, 256), F32),
            ((ROWS, 128), F32),
        ],
        [
            v((2, ROWS, 128), BF16),
            v((2, ROWS, 128), BF16),
            v((2, 2 * ROWS, 128), BF16),
            v((2, 2 * ROWS, 128), F32),
            v((2, 2 * ROWS, 128), F32),
            dma((2,)),
            dma((2,)),
            dma((16,)),
            dma((16,)),
            dma((2, 4)),
            dma((8,)),
            dma((3,)),
            dma((3,)),
            dma((3,)),
            dma((3,)),
        ],
    )
    (
        down_part,
        hidden_rows,
        grad_hidden_rows,
        branch_rows,
        dob_rows,
        feed_part,
        held_gate,
        held_up,
        held_down,
    ) = kernel_call(
        feed_kernel,
        2,
        "feed_forward",
        [inputs, attended, w_out_all, feed_gain, cotangent, w_gate, w_up, w_down],
        [
            ((4, 96, 1024), BF16),
            ((96, 1024), F32),
            ((96, 1024), F32),
            ((96, 1024), BF16),
            ((96, 1024), BF16),
            ((8, 1024), F32),
            ((512, 1152), BF16),
            ((512, 1152), BF16),
            ((512, 1152), BF16),
        ],
        [
            v((ROWS, 1024), F32),
            v((ROWS, 128), F32),
            v((ROWS, 1024), BF16),
            v((1024, ROWS), BF16),
            v((1024, ROWS), BF16),
            v((ROWS, 1152), BF16),
            v((ROWS, 1152), BF16),
            v((ROWS, 1152), BF16),
            v((ROWS, 1024), F32),
            v((4, 96, 1024), BF16),
            v((3, 96, 1024), BF16),
            v((1024, 1152), BF16),
            v((1024, 1152), BF16),
            v((1024, 1152), BF16),
            v((512, 1152), BF16),
            v((512, 1152), BF16),
            v((512, 1152), BF16),
            dma((2, 3)),
            dma((2, 3)),
        ],
    )
    held_gate, held_up, held_down = [
        held.reshape(4, 4, 32, 1152) for held in (held_gate, held_up, held_down)
    ]
    grad_query, grad_kv, block_out, branches, gate_sum, up_sum = kernel_call(
        attention_backward_kernel,
        3,
        "attention_backward",
        [
            dob_rows,
            role_kv,
            role_q,
            role_o,
            role_logs,
            down_part,
            hidden_rows,
            branch_rows,
            held_gate,
            held_up,
        ],
        [
            ((ROWS, 256), BF16),
            ((2, ROWS, 128), F32),
            ((4, 96, 1024), BF16),
            ((4, 96, 1024), BF16),
            ((32, 1152), F32),
            ((32, 640), F32),
        ],
        [
            v((2, 2 * ROWS, 128), BF16),
            v((2, 2 * ROWS, 128), BF16),
            v((2, 8, 2 * ROWS), F32),
            v((2, ROWS, 128), BF16),
            v((2, 128, 2 * ROWS), F32),
            v((2, ROWS, 128), BF16),
            v((2, ROWS, 128), BF16),
            v((16, ROWS, 128), BF16),
            v((2, 8, ROWS, 128), BF16),
            v((3, 96, 1024), BF16),
            dma((2, 4)),
            dma((2, 4)),
            dma((2,)),
            dma((2,)),
            dma((16,)),
            dma((2, 8)),
            dma((3, 2, 3)),
        ]
        + plane_sum_scratch([item[2] for item in BACKWARD_ITEMS]),
        any_inputs=(8, 9),
    )
    block_out = block_out.reshape(ROWS, 1024)
    branches = branches.reshape(ROWS, 1024)
    input_grad, late_sum, gain_sum, up_sum_2, down_sum = kernel_call(
        final_kernel,
        4,
        "final",
        [
            grad_query,
            grad_kv,
            query_raw,
            key_raw,
            normed,
            inputs,
            attention_gain,
            query_gain,
            key_gain,
            *position_tables,
            w_query,
            key_weight,
            value_weight,
            attended,
            branches,
            grad_hidden_rows,
            feed_part,
            held_up,
            held_down,
        ],
        [
            ((ROWS, 1024), F32),
            ((32, 768), F32),
            ((32, 128), F32),
            ((32, 512), F32),
            ((32, 1152), F32),
        ],
        [
            v((ROWS, 512), BF16),
            v((1024, ROWS), BF16),
            v((4, 96, 1024), BF16),
            v((3, 96, 1024), BF16),
            v((1024, 768), BF16),
            v((512, 768), BF16),
            v((4, 4, 32, 768), BF16),
            v((4, 96, 1024), BF16),
            v((8, 1024), F32),
            v((3, 8, 1024), F32),
            v((128, 1024), F32),
            v((1024, 128), BF16),
            v((512, 128), BF16),
            v((4, 4, 32, 128), BF16),
            dma((3, 2, 3)),
            dma((2, 2)),
        ]
        + plane_sum_scratch(
            [item[2] for item in FINAL_ITEMS] + [item[1] for item in LATE_ITEMS] + [128]
        ),
        any_inputs=(20, 21),
    )
    place_index = lax.axis_index("dp") * 16 + lax.axis_index("ctx")
    pair = 64 + 2 * place_index
    return (
        block_out,
        input_grad,
        gain_sum[:, 0],
        lax.dynamic_slice(gain_sum[0], (pair,), (2,)),
        lax.dynamic_slice(gain_sum[1], (pair,), (2,)),
        late_sum[:, 0:256],
        late_sum[:, 256:384],
        late_sum[:, 384:512],
        late_sum[:, 512:768],
        gain_sum[:, 1],
        gate_sum,
        jnp.concatenate([up_sum, up_sum_2], axis=1),
        down_sum,
    )


def solution(mesh):
    both = ("dp", "ctx")
    by_head = P(None, "head")
    reduced = P(both, "head")
    return jax.shard_map(
        shards,
        mesh=mesh,
        in_specs=(
            P(both, None),
            P(both, None),
            P(),
            P(),
            P(),
            by_head,
            by_head,
            by_head,
            by_head,
            P(),
            by_head,
            by_head,
            by_head,
        ),
        out_specs=(
            P(both, None),
            P(both, None),
            P(both),
            P(both),
            P(both),
            reduced,
            reduced,
            reduced,
            reduced,
            P(both),
            reduced,
            reduced,
            reduced,
        ),
        check_vma=False,
    )
```

```python
from types import SimpleNamespace

import jax
import jax.numpy as jnp
import numpy as np
from jax import lax
from jax.experimental import pallas as pl
from jax.experimental.pallas import tpu as pltpu
from jax.sharding import PartitionSpec as P

epsilon = 1e-05
theta_base = 1000000.0
MESH = pl.DeviceIdType.MESH
F32 = jnp.float32
BF16 = jnp.bfloat16
ROWS = 384
LOG2E = 1.4426950408889634
VMEM_LIMIT = 63 * 1024 * 1024


def remote(src, dst, send_sem, recv_sem, d, c, z):
    return pltpu.make_async_remote_copy(
        src_ref=src,
        dst_ref=dst,
        send_sem=send_sem,
        recv_sem=recv_sem,
        device_id=(d, c, z),
        device_id_type=MESH,
    )


def local_sem(src, dst, sem):
    return pltpu.make_async_copy(src, dst, sem)


def place():
    return lax.axis_index("dp"), lax.axis_index("ctx"), lax.axis_index("head")


def role_of(d, c):
    row, column = c // 4, lax.rem(c, 4)
    low = jnp.where(d == 0, column, 7 - column)
    return row // 2, lax.rem(row, 2), low, 15 - low


def lower(block):
    return jnp.minimum(block, 15 - block)


def spread_heads(pair, upper):
    pair = pair.astype(F32)
    lane = lax.broadcasted_iota(jnp.int32, pair.shape, 1)
    turned = pltpu.roll(pair, 64, 1)
    if upper:
        first, second = jnp.where(lane >= 64, turned, 0.0), jnp.where(lane >= 64, pair, 0.0)
    else:
        first, second = jnp.where(lane < 64, pair, 0.0), jnp.where(lane < 64, turned, 0.0)
    return first.astype(BF16), second.astype(BF16)


def nt(left, right):
    return lax.dot_general(left, right, (((1,), (1,)), ((), ())), preferred_element_type=F32)


def nn(left, right):
    return lax.dot_general(left, right, (((1,), (0,)), ((), ())), preferred_element_type=F32)


SCORE_SCALE = LOG2E / 8.0


def split_columns(half_width=32, rows=ROWS, blocks=16):
    lane = np.arange(128) % half_width
    frequency = theta_base ** (-2.0 * lane / (2 * half_width))
    row_angle = np.arange(rows)[:, None] * frequency[None, :]
    block_angle = (np.arange(blocks) * rows)[:, None] * frequency[None, :]
    return [
        np.asarray(table, np.float32)
        for table in (
            np.cos(row_angle),
            np.sin(row_angle),
            np.cos(block_angle),
            np.sin(block_angle),
        )
    ]


def tables(c, row_cos, row_sin, block_cos, block_sin):
    bc, bs = block_cos[pl.ds(c, 1), :], block_sin[pl.ds(c, 1), :]
    rc, rs = row_cos[...], row_sin[...]
    return rc * bc - rs * bs, rs * bc + rc * bs


def lanes(rows=ROWS):
    return lax.broadcasted_iota(jnp.int32, (rows, 128), 1)


def half_sums(values):
    lane = lanes(values.shape[0])
    first = jnp.sum(jnp.where(lane < 64, values, 0.0), axis=1, keepdims=True)
    second = jnp.sum(jnp.where(lane >= 64, values, 0.0), axis=1, keepdims=True)
    return jnp.where(lane < 64, first, second)


def turn(values):
    lane = lanes(values.shape[0])
    return jnp.where(lax.rem(lane, 64) < 32, -pltpu.roll(values, 96, 1), pltpu.roll(values, 32, 1))


def turn_back(values):
    lane = lanes(values.shape[0])
    return jnp.where(lax.rem(lane, 64) < 32, pltpu.roll(values, 96, 1), -pltpu.roll(values, 32, 1))


def pair_forward(raw, gain, cosine, sine):
    scale = lax.rsqrt(half_sums(raw * raw) * (1.0 / 64.0) + epsilon)
    normed = raw * scale * gain
    return normed * cosine + turn(normed) * sine


def pair_backward(grad, raw, gain, cosine, sine):
    incoming = grad * cosine + turn_back(grad * sine)
    scale = lax.rsqrt(half_sums(raw * raw) * (1.0 / 64.0) + epsilon)
    weighted = incoming * gain
    inner = half_sums(weighted * raw) * (1.0 / 64.0)
    raw_grad = scale * weighted - raw * (scale * scale * scale) * inner
    return raw_grad, jnp.sum(incoming * raw * scale, axis=0, keepdims=True)


def z_send(source_of, landed, sems, d, c, z):
    copies = []
    for step in (2, 1, 3):
        other = lax.rem(z + step, 4)
        copy = remote(
            source_of(other),
            landed(step),
            sems.at[0, step - 1],
            sems.at[1, step - 1],
            d,
            c,
            other,
        )
        copy.start()
        copies.append(copy)
    return copies


class ZReduce:
    def __init__(self, part, land, sems, d, c, z):
        self.part, self.land, self.sems = part, land, sems
        self.d, self.c = d, c
        self.up, self.down, self.across = lax.rem(z + 1, 4), lax.rem(z + 3, 4), lax.rem(z + 2, 4)

    def copy(self, index, source, there, plane):
        copy = remote(
            source, there, self.sems.at[0, index], self.sems.at[1, index], self.d, self.c, plane
        )
        copy.start()
        return copy

    def start(self):
        part, land = self.part, self.land
        self.copies = [
            self.copy(0, part.at[self.across, 0:48], land.at[0, 0:48], self.up),
            self.copy(1, part.at[self.across, 48:96], land.at[0, 48:96], self.down),
            self.copy(2, part.at[self.up, 48:96], land.at[1, 48:96], self.up),
            self.copy(3, part.at[self.down, 0:48], land.at[2, 0:48], self.down),
        ]
        return self

    def relay(self):
        part, land = self.part, self.land
        for index, rows, plane in ((0, slice(0, 48), self.up), (1, slice(48, 96), self.down)):
            self.copies[index].wait_recv()
            part[plane, rows, :] = (
                part[plane, rows, :].astype(F32) + land[0, rows, :].astype(F32)
            ).astype(BF16)
            self.copies.append(
                self.copy(4 + index, part.at[plane, rows], land.at[1 + index, rows], plane)
            )

    def finish(self):
        for copy in self.copies[2:]:
            copy.wait_recv()
        return self.land[1].astype(F32) + self.land[2].astype(F32)


class ZGather(ZReduce):
    def __init__(self, slots, sems, d, c, z):
        super().__init__(slots, None, sems, d, c, z)
        self.z = z

    def start(self):
        low, high = self.part.at[self.z, 0:48], self.part.at[self.z, 48:96]
        self.copies = [
            self.copy(0, low, low, self.up),
            self.copy(1, high, high, self.down),
            self.copy(2, high, high, self.up),
            self.copy(3, low, low, self.down),
        ]
        return self

    def relay(self):
        self.copies[0].wait_recv()
        low = self.part.at[self.down, 0:48]
        self.copies.append(self.copy(4, low, low, self.up))
        self.copies[1].wait_recv()
        high = self.part.at[self.up, 48:96]
        self.copies.append(self.copy(5, high, high, self.down))

    def finish(self):
        for copy in self.copies[2:]:
            copy.wait_recv()


class PlaneSum:
    def __init__(self, index, source, y_first, landed, landed_last, sems):
        self.index, self.source, self.y_first = index, source, y_first
        self.landed, self.landed_last = landed, landed_last
        self.first_sems, self.last_sems = sems
        self.d, c, self.z = place()
        self.y, self.x = c // 4, lax.rem(c, 4)

    def along(self, first, step):
        if first == self.y_first:
            other = lax.rem(self.y + step, 4)
            return other, other * 4 + self.x
        other = lax.rem(self.x + step, 4)
        return other, self.y * 4 + other

    def start(self):
        self.firsts = []
        for step in (2, 1, 3):
            other, chip = self.along(True, step)
            copy = remote(
                self.source.at[other] if self.y_first else self.source.at[:, other],
                self.landed.at[step - 1],
                self.first_sems.at[0, self.index, step - 1],
                self.first_sems.at[1, self.index, step - 1],
                self.d,
                chip,
                self.z,
            )
            copy.start()
            self.firsts.append(copy)

    def middle(self):
        for copy in self.firsts:
            copy.wait_recv()

        def add(r, carry):
            own = self.source.at[self.y, r] if self.y_first else self.source.at[r, self.x]
            total = own[...].astype(F32)
            for step in range(3):
                total = total + self.landed[step, r].astype(F32)
            own[...] = total.astype(BF16)
            return carry

        lax.fori_loop(0, 4, add, 0)
        self.lasts = []
        for step in (2, 1, 3):
            other, chip = self.along(False, step)
            own = self.source.at[self.y, other] if self.y_first else self.source.at[other, self.x]
            copy = remote(
                own,
                self.landed_last.at[step - 1],
                self.last_sems.at[0, self.index, step - 1],
                self.last_sems.at[1, self.index, step - 1],
                self.d,
                chip,
                self.z,
            )
            copy.start()
            self.lasts.append(copy)

    def finish(self):
        for copy in self.lasts:
            copy.wait_recv()
        total = self.source[self.y, self.x].astype(F32)
        for step in range(3):
            total = total + self.landed_last[step].astype(F32)
        return total

    def sent(self):
        for copy in self.firsts + self.lasts:
            copy.wait_send()


FF_ITEMS = (
    (0, 0, 640, True),
    (0, 640, 512, False),
    (1, 0, 512, True),
    (1, 512, 640, False),
    (2, 0, 640, True),
    (2, 640, 512, False),
)
LATE_ITEMS = ((0, 384, True), (384, 384, False))
SUM_WIDTHS = [item[2] for item in FF_ITEMS] + [item[1] for item in LATE_ITEMS] + [128]

INPUTS = [
    "x",
    "attention_gain",
    "wq",
    "wk",
    "wv",
    "query_gain",
    "key_gain",
    "row_cos",
    "row_sin",
    "block_cos",
    "block_sin",
    "feed_gain",
]
STREAMED = ["cot", "wo", "wg", "wu", "wd"]
OUTPUTS = {
    "block": ((4, 96, 1024), BF16),
    "rows_out": ((4, 96, 1024), BF16),
    "gate_sum": ((32, 1152), F32),
    "up_sum": ((32, 1152), F32),
    "down_sum": ((32, 1152), F32),
    "late_sum": ((32, 768), F32),
    "gain_sum": ((32, 128), F32),
}
BUFFERS = {
    "cot": ((ROWS, 1024), BF16),
    "wg": ((1024, 1152), BF16),
    "wu": ((1024, 1152), BF16),
    "wd": ((1024, 1152), BF16),
    "wall": ((1024, 1024), BF16),
    "normed": ((ROWS, 1024), BF16),
    "normed_t": ((1024, ROWS), BF16),
    "pair_gains": ((8, 128), F32),
    "qraw": ((ROWS, 256), F32),
    "kraw": ((ROWS, 128), F32),
    "q": ((2, ROWS, 128), BF16),
    "kv": ((2, ROWS, 128), BF16),
    "kvs": ((16, ROWS, 128), BF16),
    "qs": ((2, ROWS, 128), BF16),
    "os": ((2, ROWS, 128), BF16),
    "l2": ((2, 8, 2 * ROWS), F32),
    "qz": ((2, 2 * ROWS, 128), BF16),
    "acc": ((2, 2 * ROWS, 128), F32),
    "sums": ((2, 2 * ROWS, 128), F32),
    "oall": ((ROWS, 1024), BF16),
    "hidden": ((ROWS, 1024), F32),
    "scale": ((ROWS, 128), F32),
    "mixed": ((ROWS, 1024), BF16),
    "mixed_t": ((1024, ROWS), BF16),
    "cot_t": ((1024, ROWS), BF16),
    "inner": ((ROWS, 1152), BF16),
    "grad_gate": ((ROWS, 1152), BF16),
    "grad_up": ((ROWS, 1152), BF16),
    "total": ((ROWS, 1024), F32),
    "part_send": ((4, 96, 1024), BF16),
    "part_land": ((3, 96, 1024), BF16),
    "down_send": ((4, 96, 1024), BF16),
    "down_land": ((3, 96, 1024), BF16),
    "dw_g": ((2, 4, 4, 32, 1152), BF16),
    "dw_u": ((2, 4, 4, 32, 1152), BF16),
    "dw_d": ((2, 4, 4, 32, 1152), BF16),
    "land_g": ((4, 4, 32, 1152), BF16),
    "land_u": ((4, 4, 32, 1152), BF16),
    "land_d": ((4, 4, 32, 1152), BF16),
    "grad_rows": ((96, 1024), F32),
    "branch": ((4, 96, 1024), BF16),
    "dob": ((96, 1024), BF16),
    "doz": ((2, 2 * ROWS, 128), BF16),
    "delta": ((2, 8, 2 * ROWS), F32),
    "dos": ((2, ROWS, 128), BF16),
    "dqt": ((2, 128, 2 * ROWS), F32),
    "dq_out": ((2, ROWS, 128), BF16),
    "dq_in": ((2, ROWS, 128), BF16),
    "dkv_out": ((16, ROWS, 128), BF16),
    "dkv_in": ((2, 4, ROWS, 128), BF16),
    "dkv_part": ((8, ROWS, 128), BF16),
    "dkv": ((2, ROWS, 128), F32),
    "grads": ((ROWS, 512), BF16),
    "last_send": ((4, 96, 1024), BF16),
    "last_land": ((3, 96, 1024), BF16),
    "late": ((2, 4, 4, 32, 768), BF16),
    "late_land": ((4, 4, 32, 768), BF16),
    "gains": ((8, 1024), F32),
    "gains_land": ((3, 8, 1024), F32),
    "chunk_in": ((128, 1024), F32),
    "chunk": ((2, 4, 4, 32, 128), BF16),
    "chunk_land": ((4, 4, 32, 128), BF16),
}
SEMAPHORES = {
    "load": (5,),
    "q_send": (2,),
    "q_recv": (2,),
    "kv_send": (8,),
    "hand_send": (8,),
    "kv_recv": (16,),
    "o_send": (2, 4),
    "o_recv": (8,),
    "w_sems": (2, 3),
    "wc_sems": (2, 3),
    "mixed_sems": (2, 6),
    "core_sems": (2, 5),
    "do_send": (2, 4),
    "do_recv": (2, 4),
    "branch_sems": (2, 6),
    "down_sems": (2, 6),
    "block_sems": (2, 6),
    "dq_send": (2,),
    "dq_recv": (2,),
    "dkv_send": (16,),
    "dkv_recv": (2, 4),
    "part_send_sem": (16,),
    "part_recv_sem": (8,),
    "last_sems": (2, 6),
    "gain_sems": (2, 3),
    "rows_sems": (2, 6),
    "sum_first": (2, len(SUM_WIDTHS), 3),
    "sum_last": (2, len(SUM_WIDTHS), 3),
}


def columns_of(t, width):
    return pl.ds(pl.multiple_of(t * width, width), width)


def transpose_into(out, source):
    def move(t, carry):
        columns = columns_of(t, 128)
        out[columns, :] = source[:, columns].T
        return carry

    lax.fori_loop(0, 8, move, 0)


def block_kernel(*refs):
    names = INPUTS + ["hbm_" + name for name in STREAMED] + list(OUTPUTS) + list(BUFFERS)
    names += list(SEMAPHORES)
    r = SimpleNamespace(**dict(zip(names, refs)))
    landings = refs[len(names) :]
    d, c, z = place()
    s, j_role, low, high = role_of(d, c)
    x = lax.rem(c, 4)
    slot = jnp.where(c >= 8, 1, 0)
    home_core = jnp.where(lower(c) < 4, 0, 1)
    home_column = jnp.where(home_core == 0, lower(c), 7 - lower(c))

    def home(j):
        return (2 * d + j) * 4 + home_column

    def own(i):
        return jnp.where(d == 0, lax.rem(x - i + 8, 4), 4 + lax.rem(11 - x - i, 4))

    def others(i):
        return jnp.where(d == 0, 4 + lax.rem(11 - x - i, 4), lax.rem(x - i + 8, 4))

    column = columns_of(z, 256)
    lane = lanes()

    barrier = pltpu.get_barrier_semaphore()

    def signal(*device):
        pl.semaphore_signal(barrier, inc=1, device_id=device, device_id_type=MESH)

    def greet(index, carry):
        other_d, other_c = index // 16, lax.rem(index, 16)

        @pl.when((other_d != d) | (other_c != c))
        def _():
            signal(other_d, other_c, z)

        return carry

    lax.fori_loop(0, 32, greet, 0)
    for step in (1, 2, 3):
        other = lax.rem(z + step, 4)
        signal(d, c, other)
        for j in range(2):
            signal(home_core, home(j), other)
        for block in (low, high):
            signal(s, block, other)

    load_wo = local_sem(r.hbm_wo, r.wall.at[:, column], r.load.at[0])
    load_cot = local_sem(r.hbm_cot, r.cot, r.load.at[1])
    load_wg = local_sem(r.hbm_wg, r.wg, r.load.at[2])
    load_wu = local_sem(r.hbm_wu, r.wu, r.load.at[3])
    load_wd = local_sem(r.hbm_wd, r.wd, r.load.at[4])
    for copy in (load_wo, load_cot, load_wg, load_wu, load_wd):
        copy.start()

    def first_norm(t, carry):
        rows = columns_of(t, 96)
        values = r.x[rows, :].astype(F32)
        factor = lax.rsqrt(jnp.mean(values * values, axis=1, keepdims=True) + epsilon)
        r.normed[rows, :] = (values * factor * r.attention_gain[...]).astype(BF16)
        return carry

    lax.fori_loop(0, 4, first_norm, 0)
    normed = r.normed[...]
    for half in (0, 64):
        r.pair_gains[0:1, half : half + 64] = r.query_gain[...]
        r.pair_gains[1:2, half : half + 64] = r.key_gain[...]
    query_gain, key_gain = r.pair_gains[0:1, :], r.pair_gains[1:2, :]
    cosine, sine = tables(c, r.row_cos, r.row_sin, r.block_cos, r.block_sin)
    key_raw = nn(normed, r.wk[...])
    r.kraw[...] = key_raw
    value = nn(normed, r.wv[...])
    key = pair_forward(key_raw, key_gain, cosine, sine)
    r.kv[0] = jnp.where(lane < 64, key, pltpu.roll(value, 64, 1)).astype(BF16)
    r.kv[1] = jnp.where(lane < 64, pltpu.roll(key, 64, 1), value).astype(BF16)
    pl.semaphore_wait(barrier, 31 + 3 + 6 + 6)

    def kv_target(k, j):
        column = lax.rem(jnp.where(home_core == 0, home_column + k, home_column - k + 4), 4)
        core = jnp.where((home_core == 1) & (c <= 8 + column), 1, 0)
        return core, (2 * d + j) * 4 + column, c <= 15 - column

    def kv_copy(k, j):
        core, chip, _ = kv_target(k, j)
        return remote(
            r.kv.at[j], r.kvs.at[c], r.kv_send.at[2 * k + j], r.kv_recv.at[c], core, chip, z
        )

    def kv_start(k, carry):
        for j in range(2):
            core, chip, needed = kv_target(k, j)
            here = (core == d) & (chip == c)

            @pl.when(needed & jnp.logical_not(here))
            def _():
                kv_copy(k, j).start()

            @pl.when(needed & here)
            def _():
                local_sem(r.kv.at[j], r.kvs.at[c], r.kv_recv.at[c]).start()

        return carry

    def q_copy(j):
        return remote(r.q.at[j], r.qs.at[slot], r.q_send.at[j], r.q_recv.at[slot], home_core, home(j), z)

    kv_start(0, 0)
    query_raw = nn(normed, r.wq[...])
    r.qraw[...] = query_raw
    for j in range(2):
        pair = query_raw[:, j * 128 : (j + 1) * 128]
        r.q[j] = pair_forward(pair, query_gain, cosine, sine).astype(BF16)
        here = (home(j) == c) & (home_core == d)

        @pl.when(jnp.logical_not(here))
        def _():
            q_copy(j).start()

        @pl.when(here)
        def _():
            local_sem(r.q.at[j], r.qs.at[slot], r.q_recv.at[slot]).start()

    lax.fori_loop(1, 4, kv_start, 0)

    load_wo.wait()
    mine = columns_of(d, 512)
    w_copies = z_send(
        lambda other: r.wall.at[mine, column],
        lambda step: r.wall.at[mine, column],
        r.w_sems,
        d,
        c,
        z,
    )

    transpose_into(r.normed_t, r.normed)
    load_cot.wait()
    transpose_into(r.cot_t, r.cot)

    r.acc[...] = jnp.zeros_like(r.acc)
    r.sums[...] = jnp.zeros_like(r.sums)
    for which in range(2):
        local_sem(r.q.at[0], r.qs.at[which], r.q_recv.at[which]).wait()
        first, second = spread_heads(r.qs[which], False)
        r.qz[which, 0:ROWS, :] = first
        r.qz[which, ROWS : 2 * ROWS, :] = second

    def kv_wait(block):
        local_sem(r.kv.at[0], r.kvs.at[block], r.kv_recv.at[block]).wait()

    def forward_tile(block, which, masked):
        keys = r.kvs[block]
        for head in range(2):
            rows = slice(head * ROWS, (head + 1) * ROWS)
            weights = jnp.exp2(nt(r.qz[which, rows, :], keys) * SCORE_SCALE)
            if masked:
                row = lax.broadcasted_iota(jnp.int32, weights.shape, 0)
                key = lax.broadcasted_iota(jnp.int32, weights.shape, 1)
                weights = jnp.where(row >= key, weights, 0.0)
            r.sums[which, rows, :] += weights[:, 0:128] + weights[:, 128:256] + weights[:, 256:384]
            r.acc[which, rows, :] += nn(weights.astype(BF16), keys)

    def hand_on(index, block):
        return remote(
            r.kvs.at[block],
            r.kvs.at[block],
            r.hand_send.at[index],
            r.kv_recv.at[block],
            1 - d,
            c,
            z,
        )

    kv_wait(low)
    kv_wait(high)
    hand_on(0, low).start()

    @pl.when(d == 1)
    def _():
        hand_on(1, high).start()

    forward_tile(low, 1, False)
    forward_tile(low, 0, True)
    forward_tile(high, 1, True)

    def forward_step(k, carry):
        first = jnp.where(k < 4, own(k), others(k - 4))
        below = first < low
        kv_wait(first)

        @pl.when(k < 4)
        def _():
            hand_on(2 * k, first).start()

        @pl.when(jnp.logical_not(below))
        def _():
            kv_wait(15 - first)

            @pl.when((k < 4) & (d == 1))
            def _():
                hand_on(2 * k + 1, 15 - first).start()

        forward_tile(first, 1, False)
        forward_tile(jnp.where(below, first, 15 - first), jnp.where(below, 0, 1), False)
        return carry

    lax.fori_loop(1, 8, forward_step, 0)

    def o_copy(which, step):
        block = high if which else low
        other = lax.rem(z + step, 4)
        there = r.oall.at[:, columns_of(z * 2 + j_role, 128)]
        arrived = r.o_recv.at[z * 2 + j_role]
        return r.os.at[which], there, r.o_send.at[which, step], arrived, s, block, other

    for which in range(2):
        total = jnp.sum(r.sums[which], axis=1, keepdims=True)
        result = r.acc[which] / total
        r.os[which] = jnp.where(
            lane < 64, pltpu.roll(result[:ROWS], 64, 1), result[ROWS:]
        ).astype(BF16)
        block = high if which else low
        here = (s == d) & (block == c)
        for step in (2, 1, 3):
            remote(*o_copy(which, step)).start()

        @pl.when(jnp.logical_not(here))
        def _():
            remote(*o_copy(which, 0)).start()

        @pl.when(here)
        def _():
            source, there, _, arrived = o_copy(which, 0)[:4]
            local_sem(source, there, arrived).start()

    forwards = []
    for copy, step in zip(w_copies, (2, 1, 3)):
        copy.wait_recv()
        theirs = columns_of(lax.rem(z + 4 - step, 4), 256)
        forward = remote(
            r.wall.at[mine, theirs],
            r.wall.at[mine, theirs],
            r.wc_sems.at[0, step - 1],
            r.wc_sems.at[1, step - 1],
            1 - d,
            c,
            z,
        )
        forward.start()
        forwards.append(forward)
    for which in range(2):
        total = jnp.sum(r.sums[which], axis=1, keepdims=True)
        logs = jnp.broadcast_to(jnp.log2(total), (2 * ROWS, 128))
        r.l2[which] = logs.T[0:8]
    for forward in forwards:
        forward.wait_recv()
    for source in range(4):
        for j in range(2):
            there = r.oall.at[:, source * 256 + j * 128 : source * 256 + (j + 1) * 128]
            local_sem(r.os.at[0], there, r.o_recv.at[source * 2 + j]).wait()

    def project_out(t, carry):
        columns = columns_of(t, 256)
        r.hidden[:, columns] = r.x[:, columns].astype(F32) + nt(r.oall[...], r.wall[columns, :])
        return carry

    lax.fori_loop(0, 4, project_out, 0)

    def second_norm(t, carry):
        rows = columns_of(t, 96)
        values = r.hidden[rows, :]
        factor = lax.rsqrt(jnp.mean(values * values, axis=1, keepdims=True) + epsilon)
        r.scale[rows, :] = jnp.broadcast_to(factor, (96, 128))
        r.mixed[rows, :] = (values * factor * r.feed_gain[...]).astype(BF16)
        return carry

    lax.fori_loop(0, 4, second_norm, 0)
    r.total[...] = jnp.zeros_like(r.total)
    load_wg.wait()
    load_wu.wait()
    load_wd.wait()

    def units(t, carry):
        columns = columns_of(t, 384)
        gate = nn(r.mixed[...], r.wg[:, columns])
        up = nn(r.mixed[...], r.wu[:, columns])
        sigmoid = 1.0 / (1.0 + jnp.exp(-gate))
        silu = gate * sigmoid
        r.inner[:, columns] = (silu * up).astype(BF16)
        grad_inner = nn(r.cot[...], r.wd[:, columns])
        r.grad_up[:, columns] = (grad_inner * silu).astype(BF16)
        r.grad_gate[:, columns] = (
            grad_inner * up * sigmoid * (1.0 + gate * (1.0 - sigmoid))
        ).astype(BF16)
        r.total[...] += nt(r.grad_gate[:, columns], r.wg[:, columns]) + nt(
            r.grad_up[:, columns], r.wu[:, columns]
        )
        return carry

    lax.fori_loop(0, 3, units, 0)
    for other in range(4):
        r.part_send[other] = r.total[other * 96 : (other + 1) * 96, :].astype(BF16)
    reduce_mixed = ZReduce(r.part_send, r.part_land, r.mixed_sems, d, c, z).start()

    def to_other_core(index, source, land):
        copy = remote(
            source.at[1 - d], land, r.core_sems.at[0, index], r.core_sems.at[1, index], 1 - d, c, z
        )
        copy.start()
        return copy

    def add_cores(copy, source, land):
        copy.wait_recv()

        def add(t, carry):
            source[d, t] = (source[d, t].astype(F32) + land[t].astype(F32)).astype(BF16)
            return carry

        lax.fori_loop(0, 4, add, 0)

    transpose_into(r.mixed_t, r.mixed)
    cores = []
    for index, (left, right, out, land) in enumerate(
        (
            (r.mixed_t, r.grad_gate, r.dw_g, r.land_g),
            (r.mixed_t, r.grad_up, r.dw_u, r.land_u),
            (r.cot_t, r.inner, r.dw_d, r.land_d),
        )
    ):

        def weights(t, carry):
            columns = columns_of(t, 384)
            value = nn(left[...], right[:, columns]).astype(BF16)
            out[:, :, :, :, columns] = value.reshape(2, 4, 4, 32, 384)
            return carry

        lax.fori_loop(0, 3, weights, 0)
        cores.append(to_other_core(index, out, land))
        if index == 0:
            reduce_mixed.relay()

    def project_down(t, carry):
        columns = columns_of(t, 256)
        value = nt(r.inner[...], r.wd[columns, :])
        for other in range(4):
            r.down_send[other, :, columns] = value[other * 96 : (other + 1) * 96].astype(BF16)
        return carry

    lax.fori_loop(0, 4, project_down, 0)

    rows = columns_of(z, 96)
    incoming = r.total[rows, :] + reduce_mixed.finish()
    values = r.hidden[rows, :]
    factor = r.scale[rows, 0:1]
    weighted = incoming * r.feed_gain[...]
    projected = jnp.sum(weighted * values, axis=1, keepdims=True) * (1.0 / 1024.0)
    grad_rows = (
        r.cot[rows, :].astype(F32)
        + factor * weighted
        - values * (factor * factor * factor * projected)
    )
    r.gains[...] = jnp.zeros_like(r.gains)
    r.gains[1:2, :] = jnp.sum(incoming * values * factor, axis=0, keepdims=True)
    r.grad_rows[...] = grad_rows
    r.branch[z] = grad_rows.astype(BF16)

    def attended(t, carry):
        columns = columns_of(t, 256)
        r.dob[:, columns] = nn(r.branch[z], r.wall[:, columns]).astype(BF16)
        return carry

    lax.fori_loop(0, 4, attended, 0)

    def do_copy(j, step):
        other = lax.rem(z + step, 4)
        source = r.dob.at[:, columns_of(other * 2 + j, 128)]
        there = r.dos.at[slot, columns_of(z, 96)]
        sems = (r.do_send.at[j, step], r.do_recv.at[slot, z])
        return source, there, *sems, home_core, home(j), other

    for j in range(2):
        for step in (2, 1, 3):
            remote(*do_copy(j, step)).start()
        here = (home(j) == c) & (home_core == d)

        @pl.when(jnp.logical_not(here))
        def _():
            remote(*do_copy(j, 0)).start()

        @pl.when(here)
        def _():
            source, there, _, arrived = do_copy(j, 0)[:4]
            local_sem(source, there, arrived).start()

    gather_branch = ZGather(r.branch, r.branch_sems, d, c, z).start()
    reduce_down = ZReduce(r.down_send, r.down_land, r.down_sems, d, c, z).start()

    weight_grads = (r.dw_g, r.dw_u, r.dw_d)
    lands = (r.land_g, r.land_u, r.land_d)
    sources = [
        weight_grads[index].at[d, :, :, :, start : start + width]
        for index, start, width, _ in FF_ITEMS
    ]
    sources += [r.late.at[d, :, :, :, start : start + width] for start, width, _ in LATE_ITEMS]
    sources += [r.chunk.at[d]]
    y_firsts = [item[3] for item in FF_ITEMS] + [item[2] for item in LATE_ITEMS] + [True]
    plane = [
        PlaneSum(
            i,
            sources[i],
            y_firsts[i],
            landings[2 * i],
            landings[2 * i + 1],
            (r.sum_first, r.sum_last),
        )
        for i in range(len(sources))
    ]
    gate_items, up_items, down_items = plane[0:2], plane[2:4], plane[4:6]
    late_items, gain_item = plane[6:8], plane[8]

    add_cores(cores[0], r.dw_g, r.land_g)
    for item in gate_items:
        item.start()

    r.dqt[...] = jnp.zeros_like(r.dqt)
    for which in range(2):
        for source in range(4):
            there = r.dos.at[which, source * 96 : (source + 1) * 96]
            local_sem(r.dob.at[:, 0:128], there, r.do_recv.at[which, source]).wait()
        first, second = spread_heads(r.dos[which], True)
        r.doz[which, 0:ROWS, :] = first
        r.doz[which, ROWS : 2 * ROWS, :] = second
        product = (r.dos[which].astype(F32) * r.os[which].astype(F32)).T
        r.delta[which, :, 0:ROWS] = jnp.broadcast_to(
            jnp.sum(product[0:64], axis=0, keepdims=True), (8, ROWS)
        )
        r.delta[which, :, ROWS : 2 * ROWS] = jnp.broadcast_to(
            jnp.sum(product[64:128], axis=0, keepdims=True), (8, ROWS)
        )

    key_scale = jnp.where(lane < 64, 0.125, 1.0)

    def backward_tile(block, which, masked):
        keys = r.kvs[block]
        keys_t = keys.T
        result = None
        for head in range(2):
            rows = slice(head * ROWS, (head + 1) * ROWS)
            q_rows = r.qz[which, rows, :]
            do_rows = r.doz[which, rows, :]
            weights = jnp.exp2(nt(keys, q_rows) * SCORE_SCALE - r.l2[which, 0:1, rows])
            if masked:
                key = lax.broadcasted_iota(jnp.int32, weights.shape, 0)
                row = lax.broadcasted_iota(jnp.int32, weights.shape, 1)
                weights = jnp.where(row >= key, weights, 0.0)
            score_grad = (weights * (nt(keys, do_rows) - r.delta[which, 0:1, rows])).astype(BF16)
            part = nn(score_grad, q_rows) + nn(weights.astype(BF16), do_rows)
            result = part if result is None else result + part
            r.dqt[which, :, rows] += nn(keys_t, score_grad)
        return result * key_scale

    def dkv_copy(block):
        return (
            r.dkv_out.at[block],
            r.dkv_in.at[j_role, x],
            r.dkv_send.at[block],
            r.dkv_recv.at[j_role, x],
            s,
            block,
            z,
        )

    def dkv_start(block):
        here = (s == d) & (block == c)

        @pl.when(jnp.logical_not(here))
        def _():
            remote(*dkv_copy(block)).start()

        @pl.when(here)
        def _():
            source, there, _, arrived = dkv_copy(block)[:4]
            local_sem(source, there, arrived).start()

    def of_both(block):
        return (block < 4) | ((block >= 4) & (block <= 8 + x))

    def class_of(block):
        return jnp.where(lower(block) < 4, 0, 1)

    def part_copy(block):
        index = lax.rem(block, 8)
        return remote(
            r.dkv_out.at[block],
            r.dkv_part.at[index],
            r.part_send_sem.at[block],
            r.part_recv_sem.at[index],
            1 - d,
            c,
            z,
        )

    def dispatch(block):
        both = of_both(block)

        @pl.when(both & (class_of(block) != d))
        def _():
            part_copy(block).start()

        @pl.when(jnp.logical_not(both))
        def _():
            dkv_start(block)

    def combine(block):
        index = lax.rem(block, 8)
        part_copy(block).wait_recv()
        r.dkv_out[block] = (
            r.dkv_out[block].astype(F32) + r.dkv_part[index].astype(F32)
        ).astype(BF16)
        dkv_start(block)

    def combine_own(i):
        first = own(i)
        combine(first)

        @pl.when((d == 1) & (first >= low))
        def _():
            combine(15 - first)

    r.dkv_out[low] = (backward_tile(low, 1, False) + backward_tile(low, 0, True)).astype(BF16)
    r.dkv_out[high] = backward_tile(high, 1, True).astype(BF16)
    dispatch(high)
    gather_branch.relay()
    reduce_down.relay()

    def backward_step(k, carry):
        odd = lax.rem(k, 2) == 1
        first = jnp.where(odd, others((k - 1) // 2), own(k // 2))
        below = first < low
        one = backward_tile(first, 1, False)
        two = backward_tile(jnp.where(below, first, 15 - first), jnp.where(below, 0, 1), False)

        @pl.when(below)
        def _():
            r.dkv_out[first] = (one + two).astype(BF16)
            dispatch(first)

        @pl.when(jnp.logical_not(below))
        def _():
            r.dkv_out[first] = one.astype(BF16)
            dispatch(first)
            r.dkv_out[15 - first] = two.astype(BF16)
            dispatch(15 - first)

        @pl.when(odd & (k >= 3))
        def _():
            combine_own((k - 3) // 2)

        return carry

    lax.fori_loop(1, 8, backward_step, 0)

    def dq_copy(which):
        block = high if which else low
        return (
            r.dq_out.at[which],
            r.dq_in.at[j_role],
            r.dq_send.at[which],
            r.dq_recv.at[j_role],
            s,
            block,
            z,
        )

    for which in range(2):
        flat = r.dqt[which].T * 0.125
        r.dq_out[which] = jnp.where(
            lane < 64, flat[:ROWS], pltpu.roll(flat[ROWS:], 64, 1)
        ).astype(BF16)
        block = high if which else low
        here = (s == d) & (block == c)

        @pl.when(jnp.logical_not(here))
        def _():
            remote(*dq_copy(which)).start()

        @pl.when(here)
        def _():
            source, there, _, arrived = dq_copy(which)[:4]
            local_sem(source, there, arrived).start()

    combine_own(3)
    add_cores(cores[1], r.dw_u, r.land_u)
    for item in up_items:
        item.start()

    block_rows = r.hidden[columns_of(z, 96), :] + r.down_send[z].astype(F32)
    r.block[z] = (block_rows + reduce_down.finish()).astype(BF16)
    gather_block = ZGather(r.block, r.block_sems, d, c, z).start()

    cosine, sine = tables(c, r.row_cos, r.row_sin, r.block_cos, r.block_sin)
    for j in range(2):
        local_sem(r.dq_out.at[0], r.dq_in.at[j], r.dq_recv.at[j]).wait()
    query_part = jnp.zeros((1, 128), F32)
    for j in range(2):
        columns = slice(j * 128, (j + 1) * 128)
        raw_grad, gain_part = pair_backward(
            r.dq_in[j].astype(F32), r.qraw[:, columns], query_gain, cosine, sine
        )
        r.grads[:, columns] = raw_grad.astype(BF16)
        query_part = query_part + gain_part
    r.gains[2:3, 0:128] = query_part + pltpu.roll(query_part, 64, 1)

    def project_query(t, carry):
        columns = columns_of(t, 256)
        r.total[:, columns] = nt(r.grads[:, 0:256], r.wq[columns, :])
        return carry

    lax.fori_loop(0, 4, project_query, 0)
    r.late[:, :, :, :, 0:256] = (
        nn(r.normed_t[...], r.grads[:, 0:256]).astype(BF16).reshape(2, 4, 4, 32, 256)
    )
    gather_branch.finish()
    for source in range(4):

        def move(t, carry):
            columns = columns_of(t, 128)
            r.mixed_t[columns, source * 96 : (source + 1) * 96] = r.branch[source, :, columns].T
            return carry

        lax.fori_loop(0, 8, move, 0)
    r.late[:, :, :, :, 512:768] = (
        nn(r.mixed_t[...], r.oall[:, column]).astype(BF16).reshape(2, 4, 4, 32, 256)
    )
    gather_block.relay()
    for item in gate_items:
        item.middle()

    for j in range(2):
        r.dkv[j] = jnp.zeros((ROWS, 128), F32)

    def collect(column, carry):
        @pl.when(c <= 15 - column)
        def _():
            for j in range(2):
                local_sem(
                    r.dkv_out.at[0], r.dkv_in.at[j, column], r.dkv_recv.at[j, column]
                ).wait()
                r.dkv[j] += r.dkv_in[j, column].astype(F32)

        return carry

    lax.fori_loop(0, 4, collect, 0)
    first, second = r.dkv[0], r.dkv[1]
    raw_grad, key_part = pair_backward(
        jnp.where(lane < 64, first, pltpu.roll(second, 64, 1)),
        r.kraw[...],
        key_gain,
        cosine,
        sine,
    )
    r.grads[:, 256:384] = raw_grad.astype(BF16)
    r.grads[:, 384:512] = jnp.where(lane < 64, pltpu.roll(first, 64, 1), second).astype(BF16)
    r.gains[3:4, 0:128] = key_part + pltpu.roll(key_part, 64, 1)

    def project_keys(t, carry):
        columns = columns_of(t, 256)
        value = (
            r.total[:, columns]
            + nt(r.grads[:, 256:384], r.wk[columns, :])
            + nt(r.grads[:, 384:512], r.wv[columns, :])
        ).astype(BF16)
        for other in range(4):
            r.last_send[other, :, columns] = value[other * 96 : (other + 1) * 96]
        return carry

    lax.fori_loop(0, 4, project_keys, 0)
    reduce_last = ZReduce(r.last_send, r.last_land, r.last_sems, d, c, z).start()
    add_cores(cores[2], r.dw_d, r.land_d)
    for item in down_items:
        item.start()
    r.late[:, :, :, :, 256:512] = (
        nn(r.normed_t[...], r.grads[:, 256:512]).astype(BF16).reshape(2, 4, 4, 32, 256)
    )
    late_core = to_other_core(3, r.late, r.late_land)
    reduce_last.relay()
    for item in up_items:
        item.middle()

    rows = columns_of(z, 96)
    incoming = r.last_send[z].astype(F32) + reduce_last.finish()
    values = r.x[rows, :].astype(F32)
    factor = lax.rsqrt(jnp.mean(values * values, axis=1, keepdims=True) + epsilon)
    weighted = incoming * r.attention_gain[...]
    projected = jnp.sum(weighted * values, axis=1, keepdims=True) * (1.0 / 1024.0)
    r.gains[0:1, :] = jnp.sum(incoming * values * factor, axis=0, keepdims=True)
    gather_gains = z_send(
        lambda other: r.gains, lambda step: r.gains_land.at[step - 1], r.gain_sems, d, c, z
    )
    r.rows_out[z] = (
        r.grad_rows[...] + factor * weighted - values * (factor * factor * factor * projected)
    ).astype(BF16)
    gather_rows = ZGather(r.rows_out, r.rows_sems, d, c, z).start()
    add_cores(late_core, r.late, r.late_land)
    for item in late_items:
        item.start()

    for copy in gather_gains:
        copy.wait_recv()
    r.chunk_in[...] = jnp.zeros_like(r.chunk_in)
    r.chunk_in[0:8, :] = r.gains[...] + r.gains_land[0] + r.gains_land[1] + r.gains_land[2]
    column_part = r.chunk_in[...].T
    row_kind = lax.rem(lax.broadcasted_iota(jnp.int32, (1024, 128), 0), 32)
    lane_index = lax.broadcasted_iota(jnp.int32, (1024, 128), 1)
    query_total, key_total = r.chunk_in[2:3, 0:128], r.chunk_in[3:4, 0:128]
    spread = jnp.where(row_kind == 0, query_total, jnp.where(row_kind == 1, key_total, 0.0))
    r.chunk[...] = (
        jnp.where(lane_index < 64, column_part, spread).astype(BF16).reshape(2, 4, 4, 32, 128)
    )
    chunk_core = to_other_core(4, r.chunk, r.chunk_land)
    gather_rows.relay()
    for item in down_items:
        item.middle()
    add_cores(chunk_core, r.chunk, r.chunk_land)
    gain_item.start()
    for item in late_items:
        item.middle()
    gain_item.middle()

    sums = (r.gate_sum, r.up_sum, r.down_sum)
    for item, (index, start, width, _) in zip(plane[:6], FF_ITEMS):
        sums[index][:, start : start + width] = item.finish()
    for item, (start, width, _) in zip(late_items, LATE_ITEMS):
        r.late_sum[:, start : start + width] = item.finish()
    r.gain_sum[...] = gain_item.finish()
    gather_block.finish()
    gather_rows.finish()

    copies = w_copies + forwards + cores + gather_gains + [late_core, chunk_core]
    for transfer in (
        reduce_mixed,
        gather_branch,
        reduce_down,
        gather_block,
        reduce_last,
        gather_rows,
    ):
        copies = copies + transfer.copies
    for copy in copies:
        copy.wait_send()
    for item in plane:
        item.sent()
    for j in range(2):

        @pl.when(jnp.logical_not((home(j) == c) & (home_core == d)))
        def _():
            q_copy(j).wait_send()
            remote(*do_copy(j, 0)).wait_send()

        for step in (1, 2, 3):
            remote(*do_copy(j, step)).wait_send()

    def kv_sent(k, carry):
        for j in range(2):
            core, chip, needed = kv_target(k, j)

            @pl.when(needed & jnp.logical_not((core == d) & (chip == c)))
            def _():
                kv_copy(k, j).wait_send()

        first = own(k)
        hand_on(2 * k, first).wait_send()

        @pl.when((d == 1) & (first >= low))
        def _():
            hand_on(2 * k + 1, 15 - first).wait_send()

        return carry

    lax.fori_loop(0, 4, kv_sent, 0)
    for which in range(2):
        block = high if which else low
        for step in (1, 2, 3):
            remote(*o_copy(which, step)).wait_send()

        @pl.when(jnp.logical_not((s == d) & (block == c)))
        def _():
            remote(*o_copy(which, 0)).wait_send()
            remote(*dq_copy(which)).wait_send()

    def dkv_sent(block, carry):
        both = of_both(block)
        mine = class_of(block) == d

        @pl.when((block <= high) & both & jnp.logical_not(mine))
        def _():
            part_copy(block).wait_send()

        owner_here = (s == d) & (block == c)

        @pl.when((block <= high) & (jnp.logical_not(both) | mine) & jnp.logical_not(owner_here))
        def _():
            remote(*dkv_copy(block)).wait_send()

        return carry

    lax.fori_loop(0, 16, dkv_sent, 0)


def emit_kernel(
    block, rows, gate, up, down, late, gains,
    block_out, input_grad, attention_gain, query_gain, key_gain,
    wq, wk, wv, wo, feed_gain, wg, wu, wd,
):
    d, c, _ = place()
    for part in range(4):
        block_out[part * 96 : (part + 1) * 96, :] = block[part]
        input_grad[part * 96 : (part + 1) * 96, :] = rows[part].astype(F32)
    wg[...] = gate[...]
    wu[...] = up[...]
    wd[...] = down[...]
    wq[...] = late[:, 0:256]
    wk[...] = late[:, 256:384]
    wv[...] = late[:, 384:512]
    wo[...] = late[:, 512:768]
    turned = gains[...].T
    attention_gain[...] = turned[0:1, :]
    feed_gain[...] = turned[1:2, :]
    first = 64 + 2 * (d * 16 + c)
    lane = lax.broadcasted_iota(jnp.int32, (1, 128), 1)
    pair = lax.broadcasted_iota(jnp.int32, (1, 2), 1)
    for row, out in ((0, query_gain), (1, key_gain)):
        values = gains[row : row + 1, :]
        one = jnp.sum(jnp.where(lane == first, values, 0.0), axis=1, keepdims=True)
        two = jnp.sum(jnp.where(lane == first + 1, values, 0.0), axis=1, keepdims=True)
        out[...] = jnp.where(pair == 0, one, two)


def shards(
    inputs,
    cotangent,
    attention_gain,
    query_gain,
    key_gain,
    w_query,
    key_weight,
    value_weight,
    w_out,
    feed_gain,
    w_gate,
    w_up,
    w_down,
):
    vmem, anywhere = pl.BlockSpec(memory_space=pltpu.VMEM), pl.BlockSpec(memory_space=pl.ANY)
    landings = []
    for width in SUM_WIDTHS:
        landings += [pltpu.VMEM((3, 4, 32, width), BF16), pltpu.VMEM((3, 32, width), BF16)]
    results = pl.pallas_call(
        block_kernel,
        out_shape=[jax.ShapeDtypeStruct(*spec) for spec in OUTPUTS.values()],
        in_specs=[vmem] * len(INPUTS) + [anywhere] * len(STREAMED),
        out_specs=[vmem] * len(OUTPUTS),
        scratch_shapes=[pltpu.VMEM(*spec) for spec in BUFFERS.values()]
        + [pltpu.SemaphoreType.DMA(shape) for shape in SEMAPHORES.values()]
        + landings,
        compiler_params=pltpu.CompilerParams(
            collective_id=1, has_side_effects=True, vmem_limit_bytes=VMEM_LIMIT
        ),
        name="block",
    )(
        inputs,
        attention_gain.reshape(1, 1024),
        w_query,
        key_weight,
        value_weight,
        query_gain.reshape(1, 64),
        key_gain.reshape(1, 64),
        *[jnp.asarray(table) for table in split_columns()],
        feed_gain.reshape(1, 1024),
        cotangent,
        w_out,
        w_gate,
        w_up,
        w_down,
    )
    shapes = [
        ((ROWS, 1024), BF16),
        ((ROWS, 1024), F32),
        ((1, 32), F32),
        ((1, 2), F32),
        ((1, 2), F32),
        ((32, 256), F32),
        ((32, 128), F32),
        ((32, 128), F32),
        ((32, 256), F32),
        ((1, 32), F32),
        ((32, 1152), F32),
        ((32, 1152), F32),
        ((32, 1152), F32),
    ]
    outputs = pl.pallas_call(
        emit_kernel,
        out_shape=[jax.ShapeDtypeStruct(*spec) for spec in shapes],
        in_specs=[vmem] * len(results),
        out_specs=[vmem] * len(shapes),
        compiler_params=pltpu.CompilerParams(vmem_limit_bytes=VMEM_LIMIT),
        name="emit",
    )(*results)
    return tuple(
        value.reshape(-1) if value.shape[0] == 1 else value for value in outputs
    )


def solution(mesh):
    both = ("dp", "ctx")
    by_head = P(None, "head")
    reduced = P(both, "head")
    return jax.shard_map(
        shards,
        mesh=mesh,
        in_specs=(
            P(both, None),
            P(both, None),
            P(),
            P(),
            P(),
            by_head,
            by_head,
            by_head,
            by_head,
            P(),
            by_head,
            by_head,
            by_head,
        ),
        out_specs=(
            P(both, None),
            P(both, None),
            P(both),
            P(both),
            P(both),
            reduced,
            reduced,
            reduced,
            reduced,
            P(both),
            reduced,
            reduced,
            reduced,
        ),
        check_vma=False,
    )
```

```python
from types import SimpleNamespace

import jax
import jax.numpy as jnp
import numpy as np
from jax import lax
from jax.experimental import pallas as pl
from jax.experimental.pallas import tpu as pltpu
from jax.sharding import PartitionSpec as P

epsilon = 1e-05
theta_base = 1000000.0
MESH = pl.DeviceIdType.MESH
F32 = jnp.float32
BF16 = jnp.bfloat16
ROWS = 384
LOG2E = 1.4426950408889634
VMEM_LIMIT = 63 * 1024 * 1024


def remote(src, dst, send_sem, recv_sem, d, c, z):
    return pltpu.make_async_remote_copy(
        src_ref=src,
        dst_ref=dst,
        send_sem=send_sem,
        recv_sem=recv_sem,
        device_id=(d, c, z),
        device_id_type=MESH,
    )


def local_sem(src, dst, sem):
    return pltpu.make_async_copy(src, dst, sem)


def place():
    return lax.axis_index("dp"), lax.axis_index("ctx"), lax.axis_index("head")


def role_of(d, c):
    row, column = c // 4, lax.rem(c, 4)
    low = jnp.where(d == 0, column, 7 - column)
    return row // 2, lax.rem(row, 2), low, 15 - low


def lower(block):
    return jnp.minimum(block, 15 - block)


def spread_heads(pair, upper):
    pair = pair.astype(F32)
    lane = lax.broadcasted_iota(jnp.int32, pair.shape, 1)
    turned = pltpu.roll(pair, 64, 1)
    if upper:
        first, second = jnp.where(lane >= 64, turned, 0.0), jnp.where(lane >= 64, pair, 0.0)
    else:
        first, second = jnp.where(lane < 64, pair, 0.0), jnp.where(lane < 64, turned, 0.0)
    return first.astype(BF16), second.astype(BF16)


def nt(left, right):
    return lax.dot_general(left, right, (((1,), (1,)), ((), ())), preferred_element_type=F32)


def nn(left, right):
    return lax.dot_general(left, right, (((1,), (0,)), ((), ())), preferred_element_type=F32)


SCORE_SCALE = LOG2E / 8.0


def split_columns(half_width=32, rows=ROWS, blocks=16):
    lane = np.arange(128) % half_width
    frequency = theta_base ** (-2.0 * lane / (2 * half_width))
    row_angle = np.arange(rows)[:, None] * frequency[None, :]
    block_angle = (np.arange(blocks) * rows)[:, None] * frequency[None, :]
    return [
        np.asarray(table, np.float32)
        for table in (
            np.cos(row_angle),
            np.sin(row_angle),
            np.cos(block_angle),
            np.sin(block_angle),
        )
    ]


def tables(c, row_cos, row_sin, block_cos, block_sin):
    bc, bs = block_cos[pl.ds(c, 1), :], block_sin[pl.ds(c, 1), :]
    rc, rs = row_cos[...], row_sin[...]
    return rc * bc - rs * bs, rs * bc + rc * bs


def lanes(rows=ROWS):
    return lax.broadcasted_iota(jnp.int32, (rows, 128), 1)


def half_sums(values):
    lane = lanes(values.shape[0])
    first = jnp.sum(jnp.where(lane < 64, values, 0.0), axis=1, keepdims=True)
    second = jnp.sum(jnp.where(lane >= 64, values, 0.0), axis=1, keepdims=True)
    return jnp.where(lane < 64, first, second)


def turn(values):
    lane = lanes(values.shape[0])
    return jnp.where(lax.rem(lane, 64) < 32, -pltpu.roll(values, 96, 1), pltpu.roll(values, 32, 1))


def turn_back(values):
    lane = lanes(values.shape[0])
    return jnp.where(lax.rem(lane, 64) < 32, pltpu.roll(values, 96, 1), -pltpu.roll(values, 32, 1))


def pair_forward(raw, gain, cosine, sine):
    scale = lax.rsqrt(half_sums(raw * raw) * (1.0 / 64.0) + epsilon)
    normed = raw * scale * gain
    return normed * cosine + turn(normed) * sine


def pair_backward(grad, raw, gain, cosine, sine):
    incoming = grad * cosine + turn_back(grad * sine)
    scale = lax.rsqrt(half_sums(raw * raw) * (1.0 / 64.0) + epsilon)
    weighted = incoming * gain
    inner = half_sums(weighted * raw) * (1.0 / 64.0)
    raw_grad = scale * weighted - raw * (scale * scale * scale) * inner
    return raw_grad, jnp.sum(incoming * raw * scale, axis=0, keepdims=True)


def z_send(source_of, landed, sems, d, c, z):
    copies = []
    for step in (2, 1, 3):
        other = lax.rem(z + step, 4)
        copy = remote(
            source_of(other),
            landed(step),
            sems.at[0, step - 1],
            sems.at[1, step - 1],
            d,
            c,
            other,
        )
        copy.start()
        copies.append(copy)
    return copies


class ZDirectReduce:
    def __init__(self, part, land, sems, d, c, z):
        self.args = (lambda other: part.at[other], lambda step: land.at[step - 1], sems, d, c, z)
        self.land = land

    def start(self):
        self.copies = z_send(*self.args)
        return self

    def finish(self):
        for copy in self.copies:
            copy.wait_recv()
        land = self.land
        return land[0].astype(F32) + land[1].astype(F32) + land[2].astype(F32)


class ZDirectGather:
    def __init__(self, slots, sems, d, c, z):
        self.args = (lambda other: slots.at[z], lambda step: slots.at[z], sems, d, c, z)

    def start(self):
        self.copies = z_send(*self.args)
        return self

    def finish(self):
        for copy in self.copies:
            copy.wait_recv()


class ZGather:
    def __init__(self, slots, sems, d, c, z):
        self.slots, self.sems = slots, sems
        self.d, self.c, self.z = d, c, z
        self.up, self.down = lax.rem(z + 1, 4), lax.rem(z + 3, 4)

    def copy(self, index, block, plane):
        copy = remote(
            block, block, self.sems.at[0, index], self.sems.at[1, index], self.d, self.c, plane
        )
        copy.start()
        return copy

    def start(self):
        low, high = self.slots.at[self.z, 0:48], self.slots.at[self.z, 48:96]
        self.copies = [
            self.copy(0, low, self.up),
            self.copy(1, high, self.down),
            self.copy(2, high, self.up),
            self.copy(3, low, self.down),
        ]
        return self

    def relay(self):
        self.copies[0].wait_recv()
        self.copies.append(self.copy(4, self.slots.at[self.down, 0:48], self.up))
        self.copies[1].wait_recv()
        self.copies.append(self.copy(5, self.slots.at[self.up, 48:96], self.down))

    def finish(self):
        for copy in self.copies[2:]:
            copy.wait_recv()


class PlaneSum:
    def __init__(self, index, source, y_first, landed, landed_last, sems):
        self.index, self.source, self.y_first = index, source, y_first
        self.landed, self.landed_last = landed, landed_last
        self.first_sems, self.last_sems = sems
        self.d, c, self.z = place()
        self.y, self.x = c // 4, lax.rem(c, 4)

    def along(self, first, step):
        if first == self.y_first:
            other = lax.rem(self.y + step, 4)
            return other, other * 4 + self.x
        other = lax.rem(self.x + step, 4)
        return other, self.y * 4 + other

    def start(self):
        self.firsts = []
        for step in (2, 1, 3):
            other, chip = self.along(True, step)
            copy = remote(
                self.source.at[other] if self.y_first else self.source.at[:, other],
                self.landed.at[step - 1],
                self.first_sems.at[0, self.index, step - 1],
                self.first_sems.at[1, self.index, step - 1],
                self.d,
                chip,
                self.z,
            )
            copy.start()
            self.firsts.append(copy)

    def middle(self):
        for copy in self.firsts:
            copy.wait_recv()

        def add(r, carry):
            own = self.source.at[self.y, r] if self.y_first else self.source.at[r, self.x]
            total = own[...].astype(F32)
            for step in range(3):
                total = total + self.landed[step, r].astype(F32)
            own[...] = total.astype(BF16)
            return carry

        lax.fori_loop(0, 4, add, 0)
        self.lasts = []
        for step in (2, 1, 3):
            other, chip = self.along(False, step)
            own = self.source.at[self.y, other] if self.y_first else self.source.at[other, self.x]
            copy = remote(
                own,
                self.landed_last.at[step - 1],
                self.last_sems.at[0, self.index, step - 1],
                self.last_sems.at[1, self.index, step - 1],
                self.d,
                chip,
                self.z,
            )
            copy.start()
            self.lasts.append(copy)

    def finish(self):
        for copy in self.lasts:
            copy.wait_recv()
        total = self.source[self.y, self.x].astype(F32)
        for step in range(3):
            total = total + self.landed_last[step].astype(F32)
        return total

    def sent(self):
        for copy in self.firsts + self.lasts:
            copy.wait_send()


FF_ITEMS = (
    (0, 0, 640, True),
    (0, 640, 512, False),
    (1, 0, 512, True),
    (1, 512, 640, False),
    (2, 0, 640, True),
    (2, 640, 512, False),
)
LATE_ITEMS = (
    (0, 0, 256, True, 0),
    (0, 256, 256, False, 512),
    (1, 0, 128, True, 256),
    (1, 128, 128, False, 384),
)
SUM_WIDTHS = [item[2] for item in FF_ITEMS + LATE_ITEMS] + [128]

INPUTS = [
    "x",
    "attention_gain",
    "wq",
    "wk",
    "wv",
    "query_gain",
    "key_gain",
    "row_cos",
    "row_sin",
    "block_cos",
    "block_sin",
    "feed_gain",
]
STREAMED = ["cot", "wo", "wg", "wu", "wd"]
OUTPUTS = {
    "block": ((4, 96, 1024), BF16),
    "rows_out": ((4, 96, 1024), BF16),
    "gate_sum": ((32, 1152), F32),
    "up_sum": ((32, 1152), F32),
    "down_sum": ((32, 1152), F32),
    "late_sum": ((32, 768), F32),
    "gain_sum": ((32, 128), F32),
}
BUFFERS = {
    "cot": ((ROWS, 1024), BF16),
    "wg": ((1024, 1152), BF16),
    "wu": ((1024, 1152), BF16),
    "wd": ((1024, 1152), BF16),
    "wall": ((1024, 1024), BF16),
    "normed": ((ROWS, 1024), BF16),
    "normed_t": ((1024, ROWS), BF16),
    "pair_gains": ((8, 128), F32),
    "qraw": ((ROWS, 256), F32),
    "kraw": ((ROWS, 128), F32),
    "q": ((2, ROWS, 128), BF16),
    "kv": ((2, ROWS, 128), BF16),
    "kvs": ((16, ROWS, 128), BF16),
    "qs": ((2, ROWS, 128), BF16),
    "os": ((2, ROWS, 128), BF16),
    "l2": ((2, 8, 2 * ROWS), F32),
    "qz": ((2, 2 * ROWS, 128), BF16),
    "acc": ((2, 2 * ROWS, 128), F32),
    "sums": ((2, 2 * ROWS, 128), F32),
    "oall": ((ROWS, 1024), BF16),
    "hidden": ((ROWS, 1024), F32),
    "scale": ((ROWS, 128), F32),
    "mixed": ((ROWS, 1024), BF16),
    "mixed_t": ((1024, ROWS), BF16),
    "cot_t": ((1024, ROWS), BF16),
    "inner": ((ROWS, 1152), BF16),
    "grad_gate": ((ROWS, 1152), BF16),
    "grad_up": ((ROWS, 1152), BF16),
    "total": ((ROWS, 1024), F32),
    "part_send": ((4, 96, 1024), BF16),
    "part_land": ((3, 96, 1024), BF16),
    "down_send": ((4, 96, 1024), BF16),
    "down_land": ((3, 96, 1024), BF16),
    "dw_g": ((2, 4, 4, 32, 1152), BF16),
    "dw_u": ((2, 4, 4, 32, 1152), BF16),
    "dw_d": ((2, 4, 4, 32, 1152), BF16),
    "land_g": ((4, 4, 32, 1152), BF16),
    "land_u": ((4, 4, 32, 1152), BF16),
    "land_d": ((4, 4, 32, 1152), BF16),
    "grad_rows": ((96, 1024), F32),
    "branch": ((4, 96, 1024), BF16),
    "dob": ((96, 1024), BF16),
    "doz": ((2, 2 * ROWS, 128), BF16),
    "delta": ((2, 8, 2 * ROWS), F32),
    "dos": ((2, ROWS, 128), BF16),
    "dqt": ((2, 128, 2 * ROWS), F32),
    "dq_out": ((2, ROWS, 128), BF16),
    "dq_in": ((2, ROWS, 128), BF16),
    "dkv_out": ((16, ROWS, 128), BF16),
    "dkv_in": ((2, 4, ROWS, 128), BF16),
    "dkv_part": ((8, ROWS, 128), BF16),
    "dkv": ((2, ROWS, 128), F32),
    "grads": ((ROWS, 512), BF16),
    "last_send": ((4, 96, 1024), BF16),
    "last_land": ((3, 96, 1024), BF16),
    "late": ((2, 4, 4, 32, 512), BF16),
    "late_land": ((4, 4, 32, 512), BF16),
    "last": ((2, 4, 4, 32, 256), BF16),
    "last_core": ((4, 4, 32, 256), BF16),
    "gains": ((8, 1024), F32),
    "gains_land": ((7, 8, 1024), F32),
    "chunk_in": ((128, 1024), F32),
    "chunk": ((4, 4, 32, 128), BF16),
}
SEMAPHORES = {
    "load": (5,),
    "q_send": (2,),
    "q_recv": (2,),
    "kv_send": (8,),
    "hand_send": (8,),
    "kv_recv": (16,),
    "o_send": (2, 4),
    "o_recv": (8,),
    "w_sems": (2, 3),
    "wc_sems": (2, 3),
    "mixed_sems": (2, 6),
    "core_sems": (2, 5),
    "do_send": (2, 4),
    "do_recv": (2, 4),
    "branch_sems": (2, 6),
    "down_sems": (2, 6),
    "block_sems": (2, 6),
    "dq_send": (2,),
    "dq_recv": (2,),
    "dkv_send": (16,),
    "dkv_recv": (2, 4),
    "part_send_sem": (16,),
    "part_recv_sem": (8,),
    "last_sems": (2, 6),
    "gain_sems": (2, 7),
    "rows_sems": (2, 6),
    "sum_first": (2, len(SUM_WIDTHS), 3),
    "sum_last": (2, len(SUM_WIDTHS), 3),
}


def columns_of(t, width):
    return pl.ds(pl.multiple_of(t * width, width), width)


def transpose_into(out, source):
    def move(t, carry):
        columns = columns_of(t, 128)
        out[columns, :] = source[:, columns].T
        return carry

    lax.fori_loop(0, 8, move, 0)


def block_kernel(*refs):
    names = INPUTS + ["hbm_" + name for name in STREAMED] + list(OUTPUTS) + list(BUFFERS)
    names += list(SEMAPHORES)
    r = SimpleNamespace(**dict(zip(names, refs)))
    landings = refs[len(names) :]
    d, c, z = place()
    s, j_role, low, high = role_of(d, c)
    x = lax.rem(c, 4)
    slot = jnp.where(c >= 8, 1, 0)
    home_core = jnp.where(lower(c) < 4, 0, 1)
    home_column = jnp.where(home_core == 0, lower(c), 7 - lower(c))

    def home(j):
        return (2 * d + j) * 4 + home_column

    def own(i):
        return jnp.where(d == 0, lax.rem(x - i + 8, 4), 4 + lax.rem(11 - x - i, 4))

    def others(i):
        return jnp.where(d == 0, 4 + lax.rem(11 - x - i, 4), lax.rem(x - i + 8, 4))

    column = columns_of(z, 256)
    lane = lanes()

    barrier = pltpu.get_barrier_semaphore()

    def signal(*device):
        pl.semaphore_signal(barrier, inc=1, device_id=device, device_id_type=MESH)

    def greet(index, carry):
        other_d, other_c = index // 16, lax.rem(index, 16)

        @pl.when((other_d != d) | (other_c != c))
        def _():
            signal(other_d, other_c, z)

        return carry

    lax.fori_loop(0, 32, greet, 0)
    for step in (1, 2, 3):
        other = lax.rem(z + step, 4)
        signal(d, c, other)
        signal(1 - d, c, other)
        for j in range(2):
            signal(home_core, home(j), other)
        for block in (low, high):
            signal(s, block, other)

    load_wo = local_sem(r.hbm_wo, r.wall.at[:, column], r.load.at[0])
    load_cot = local_sem(r.hbm_cot, r.cot, r.load.at[1])
    load_wg = local_sem(r.hbm_wg, r.wg, r.load.at[2])
    load_wu = local_sem(r.hbm_wu, r.wu, r.load.at[3])
    load_wd = local_sem(r.hbm_wd, r.wd, r.load.at[4])
    for copy in (load_wo, load_cot, load_wg, load_wu, load_wd):
        copy.start()

    def first_norm(t, carry):
        rows = columns_of(t, 96)
        values = r.x[rows, :].astype(F32)
        factor = lax.rsqrt(jnp.mean(values * values, axis=1, keepdims=True) + epsilon)
        r.normed[rows, :] = (values * factor * r.attention_gain[...]).astype(BF16)
        return carry

    lax.fori_loop(0, 4, first_norm, 0)
    normed = r.normed[...]
    for half in (0, 64):
        r.pair_gains[0:1, half : half + 64] = r.query_gain[...]
        r.pair_gains[1:2, half : half + 64] = r.key_gain[...]
    query_gain, key_gain = r.pair_gains[0:1, :], r.pair_gains[1:2, :]
    cosine, sine = tables(c, r.row_cos, r.row_sin, r.block_cos, r.block_sin)
    key_raw = nn(normed, r.wk[...])
    r.kraw[...] = key_raw
    value = nn(normed, r.wv[...])
    key = pair_forward(key_raw, key_gain, cosine, sine)
    r.kv[0] = jnp.where(lane < 64, key, pltpu.roll(value, 64, 1)).astype(BF16)
    r.kv[1] = jnp.where(lane < 64, pltpu.roll(key, 64, 1), value).astype(BF16)
    pl.semaphore_wait(barrier, 31 + 6 + 6 + 6)

    def kv_target(k, j):
        column = lax.rem(jnp.where(home_core == 0, home_column + k, home_column - k + 4), 4)
        core = jnp.where((home_core == 1) & (c <= 8 + column), 1, 0)
        return core, (2 * d + j) * 4 + column, c <= 15 - column

    def kv_copy(k, j):
        core, chip, _ = kv_target(k, j)
        return remote(
            r.kv.at[j], r.kvs.at[c], r.kv_send.at[2 * k + j], r.kv_recv.at[c], core, chip, z
        )

    def kv_start(k, carry):
        for j in range(2):
            core, chip, needed = kv_target(k, j)
            here = (core == d) & (chip == c)

            @pl.when(needed & jnp.logical_not(here))
            def _():
                kv_copy(k, j).start()

            @pl.when(needed & here)
            def _():
                local_sem(r.kv.at[j], r.kvs.at[c], r.kv_recv.at[c]).start()

        return carry

    def q_copy(j):
        return remote(r.q.at[j], r.qs.at[slot], r.q_send.at[j], r.q_recv.at[slot], home_core, home(j), z)

    kv_start(0, 0)
    query_raw = nn(normed, r.wq[...])
    r.qraw[...] = query_raw
    for j in range(2):
        pair = query_raw[:, j * 128 : (j + 1) * 128]
        r.q[j] = pair_forward(pair, query_gain, cosine, sine).astype(BF16)
        here = (home(j) == c) & (home_core == d)

        @pl.when(jnp.logical_not(here))
        def _():
            q_copy(j).start()

        @pl.when(here)
        def _():
            local_sem(r.q.at[j], r.qs.at[slot], r.q_recv.at[slot]).start()

    lax.fori_loop(1, 4, kv_start, 0)

    load_wo.wait()
    mine = columns_of(d, 512)
    w_copies = z_send(
        lambda other: r.wall.at[mine, column],
        lambda step: r.wall.at[mine, column],
        r.w_sems,
        d,
        c,
        z,
    )

    transpose_into(r.normed_t, r.normed)
    load_cot.wait()
    transpose_into(r.cot_t, r.cot)

    r.acc[...] = jnp.zeros_like(r.acc)
    r.sums[...] = jnp.zeros_like(r.sums)
    for which in range(2):
        local_sem(r.q.at[0], r.qs.at[which], r.q_recv.at[which]).wait()
        first, second = spread_heads(r.qs[which], False)
        r.qz[which, 0:ROWS, :] = first
        r.qz[which, ROWS : 2 * ROWS, :] = second

    def kv_wait(block):
        local_sem(r.kv.at[0], r.kvs.at[block], r.kv_recv.at[block]).wait()

    def forward_tile(block, which, masked):
        keys = r.kvs[block]
        for head in range(2):
            rows = slice(head * ROWS, (head + 1) * ROWS)
            weights = jnp.exp2(nt(r.qz[which, rows, :], keys) * SCORE_SCALE)
            if masked:
                row = lax.broadcasted_iota(jnp.int32, weights.shape, 0)
                key = lax.broadcasted_iota(jnp.int32, weights.shape, 1)
                weights = jnp.where(row >= key, weights, 0.0)
            r.sums[which, rows, :] += weights[:, 0:128] + weights[:, 128:256] + weights[:, 256:384]
            r.acc[which, rows, :] += nn(weights.astype(BF16), keys)

    def hand_on(index, block):
        return remote(
            r.kvs.at[block],
            r.kvs.at[block],
            r.hand_send.at[index],
            r.kv_recv.at[block],
            1 - d,
            c,
            z,
        )

    kv_wait(low)
    kv_wait(high)
    hand_on(0, low).start()

    @pl.when(d == 1)
    def _():
        hand_on(1, high).start()

    forward_tile(low, 1, False)
    forward_tile(low, 0, True)
    forward_tile(high, 1, True)

    def forward_step(k, carry):
        first = jnp.where(k < 4, own(k), others(k - 4))
        below = first < low
        kv_wait(first)

        @pl.when(k < 4)
        def _():
            hand_on(2 * k, first).start()

        @pl.when(jnp.logical_not(below))
        def _():
            kv_wait(15 - first)

            @pl.when((k < 4) & (d == 1))
            def _():
                hand_on(2 * k + 1, 15 - first).start()

        forward_tile(first, 1, False)
        forward_tile(jnp.where(below, first, 15 - first), jnp.where(below, 0, 1), False)
        return carry

    lax.fori_loop(1, 8, forward_step, 0)

    def o_copy(which, step):
        block = high if which else low
        other = lax.rem(z + step, 4)
        there = r.oall.at[:, columns_of(z * 2 + j_role, 128)]
        arrived = r.o_recv.at[z * 2 + j_role]
        return r.os.at[which], there, r.o_send.at[which, step], arrived, s, block, other

    for which in range(2):
        total = jnp.sum(r.sums[which], axis=1, keepdims=True)
        result = r.acc[which] / total
        r.os[which] = jnp.where(
            lane < 64, pltpu.roll(result[:ROWS], 64, 1), result[ROWS:]
        ).astype(BF16)
        block = high if which else low
        here = (s == d) & (block == c)
        for step in (2, 1, 3):
            remote(*o_copy(which, step)).start()

        @pl.when(jnp.logical_not(here))
        def _():
            remote(*o_copy(which, 0)).start()

        @pl.when(here)
        def _():
            source, there, _, arrived = o_copy(which, 0)[:4]
            local_sem(source, there, arrived).start()

    forwards = []
    for copy, step in zip(w_copies, (2, 1, 3)):
        copy.wait_recv()
        theirs = columns_of(lax.rem(z + 4 - step, 4), 256)
        forward = remote(
            r.wall.at[mine, theirs],
            r.wall.at[mine, theirs],
            r.wc_sems.at[0, step - 1],
            r.wc_sems.at[1, step - 1],
            1 - d,
            c,
            z,
        )
        forward.start()
        forwards.append(forward)
    for which in range(2):
        total = jnp.sum(r.sums[which], axis=1, keepdims=True)
        logs = jnp.broadcast_to(jnp.log2(total), (2 * ROWS, 128))
        r.l2[which] = logs.T[0:8]
    for forward in forwards:
        forward.wait_recv()
    for source in range(4):
        for j in range(2):
            there = r.oall.at[:, source * 256 + j * 128 : source * 256 + (j + 1) * 128]
            local_sem(r.os.at[0], there, r.o_recv.at[source * 2 + j]).wait()

    def project_out(t, carry):
        columns = columns_of(t, 256)
        r.hidden[:, columns] = r.x[:, columns].astype(F32) + nt(r.oall[...], r.wall[columns, :])
        return carry

    lax.fori_loop(0, 4, project_out, 0)

    def second_norm(t, carry):
        rows = columns_of(t, 96)
        values = r.hidden[rows, :]
        factor = lax.rsqrt(jnp.mean(values * values, axis=1, keepdims=True) + epsilon)
        r.scale[rows, :] = jnp.broadcast_to(factor, (96, 128))
        r.mixed[rows, :] = (values * factor * r.feed_gain[...]).astype(BF16)
        return carry

    lax.fori_loop(0, 4, second_norm, 0)
    r.total[...] = jnp.zeros_like(r.total)
    load_wg.wait()
    load_wu.wait()
    load_wd.wait()

    def units(t, carry):
        columns = columns_of(t, 384)
        gate = nn(r.mixed[...], r.wg[:, columns])
        up = nn(r.mixed[...], r.wu[:, columns])
        sigmoid = 1.0 / (1.0 + jnp.exp(-gate))
        silu = gate * sigmoid
        r.inner[:, columns] = (silu * up).astype(BF16)
        grad_inner = nn(r.cot[...], r.wd[:, columns])
        r.grad_up[:, columns] = (grad_inner * silu).astype(BF16)
        r.grad_gate[:, columns] = (
            grad_inner * up * sigmoid * (1.0 + gate * (1.0 - sigmoid))
        ).astype(BF16)
        r.total[...] += nt(r.grad_gate[:, columns], r.wg[:, columns]) + nt(
            r.grad_up[:, columns], r.wu[:, columns]
        )
        return carry

    lax.fori_loop(0, 3, units, 0)
    for other in range(4):
        r.part_send[other] = r.total[other * 96 : (other + 1) * 96, :].astype(BF16)
    reduce_mixed = ZDirectReduce(r.part_send, r.part_land, r.mixed_sems, d, c, z).start()

    def to_other_core(index, source, land):
        copy = remote(
            source.at[1 - d], land, r.core_sems.at[0, index], r.core_sems.at[1, index], 1 - d, c, z
        )
        copy.start()
        return copy

    def add_cores(copy, source, land):
        copy.wait_recv()

        def add(t, carry):
            source[d, t] = (source[d, t].astype(F32) + land[t].astype(F32)).astype(BF16)
            return carry

        lax.fori_loop(0, 4, add, 0)

    weight_grads = (r.dw_g, r.dw_u, r.dw_d)
    sources = [
        weight_grads[index].at[d, :, :, :, start : start + width]
        for index, start, width, _ in FF_ITEMS
    ]
    sources += [
        (r.late, r.last)[index].at[d, :, :, :, start : start + width]
        for index, start, width, _, _ in LATE_ITEMS
    ]
    sources += [r.chunk]
    y_firsts = [item[3] for item in FF_ITEMS + LATE_ITEMS] + [True]
    plane = [
        PlaneSum(
            i,
            sources[i],
            y_firsts[i],
            landings[2 * i],
            landings[2 * i + 1],
            (r.sum_first, r.sum_last),
        )
        for i in range(len(sources))
    ]
    gate_items, up_items, down_items = plane[0:2], plane[2:4], plane[4:6]
    late_items, last_items, gain_item = plane[6:8], plane[8:10], plane[10]

    cores = []
    for index, (left, right, out, land) in enumerate(
        (
            (r.cot_t, r.inner, r.dw_d, r.land_d),
            (r.mixed_t, r.grad_gate, r.dw_g, r.land_g),
            (r.mixed_t, r.grad_up, r.dw_u, r.land_u),
        )
    ):

        def weights(t, carry):
            columns = columns_of(t, 384)
            value = nn(left[...], right[:, columns]).astype(BF16)
            out[:, :, :, :, columns] = value.reshape(2, 4, 4, 32, 384)
            return carry

        lax.fori_loop(0, 3, weights, 0)
        cores.append(to_other_core(index, out, land))
        if index == 0:
            transpose_into(r.mixed_t, r.mixed)
        elif index == 1:
            add_cores(cores[0], r.dw_d, r.land_d)
            for item in down_items:
                item.start()

    def project_down(t, carry):
        columns = columns_of(t, 256)
        value = nt(r.inner[...], r.wd[columns, :])
        for other in range(4):
            r.down_send[other, :, columns] = value[other * 96 : (other + 1) * 96].astype(BF16)
        return carry

    lax.fori_loop(0, 4, project_down, 0)

    add_cores(cores[1], r.dw_g, r.land_g)
    add_cores(cores[2], r.dw_u, r.land_u)

    rows = columns_of(z, 96)
    incoming = r.total[rows, :] + reduce_mixed.finish()
    values = r.hidden[rows, :]
    factor = r.scale[rows, 0:1]
    weighted = incoming * r.feed_gain[...]
    projected = jnp.sum(weighted * values, axis=1, keepdims=True) * (1.0 / 1024.0)
    grad_rows = (
        r.cot[rows, :].astype(F32)
        + factor * weighted
        - values * (factor * factor * factor * projected)
    )
    r.gains[...] = jnp.zeros_like(r.gains)
    r.gains[1:2, :] = jnp.sum(incoming * values * factor, axis=0, keepdims=True)
    r.grad_rows[...] = grad_rows
    r.branch[z] = grad_rows.astype(BF16)

    def attended(t, carry):
        columns = columns_of(t, 256)
        r.dob[:, columns] = nn(r.branch[z], r.wall[:, columns]).astype(BF16)
        return carry

    lax.fori_loop(0, 4, attended, 0)

    def do_copy(j, step):
        other = lax.rem(z + step, 4)
        source = r.dob.at[:, columns_of(other * 2 + j, 128)]
        there = r.dos.at[slot, columns_of(z, 96)]
        sems = (r.do_send.at[j, step], r.do_recv.at[slot, z])
        return source, there, *sems, home_core, home(j), other

    for j in range(2):
        for step in (2, 1, 3):
            remote(*do_copy(j, step)).start()
        here = (home(j) == c) & (home_core == d)

        @pl.when(jnp.logical_not(here))
        def _():
            remote(*do_copy(j, 0)).start()

        @pl.when(here)
        def _():
            source, there, _, arrived = do_copy(j, 0)[:4]
            local_sem(source, there, arrived).start()

    reduce_down = ZDirectReduce(r.down_send, r.down_land, r.down_sems, d, c, z).start()
    gather_branch = ZGather(r.branch, r.branch_sems, d, c, z).start()
    for item in gate_items:
        item.start()

    r.dqt[...] = jnp.zeros_like(r.dqt)
    for which in range(2):
        for source in range(4):
            there = r.dos.at[which, source * 96 : (source + 1) * 96]
            local_sem(r.dob.at[:, 0:128], there, r.do_recv.at[which, source]).wait()
        first, second = spread_heads(r.dos[which], True)
        r.doz[which, 0:ROWS, :] = first
        r.doz[which, ROWS : 2 * ROWS, :] = second
        product = (r.dos[which].astype(F32) * r.os[which].astype(F32)).T
        r.delta[which, :, 0:ROWS] = jnp.broadcast_to(
            jnp.sum(product[0:64], axis=0, keepdims=True), (8, ROWS)
        )
        r.delta[which, :, ROWS : 2 * ROWS] = jnp.broadcast_to(
            jnp.sum(product[64:128], axis=0, keepdims=True), (8, ROWS)
        )

    key_scale = jnp.where(lane < 64, 0.125, 1.0)

    def backward_tile(block, which, masked):
        keys = r.kvs[block]
        keys_t = keys.T
        result = None
        for head in range(2):
            rows = slice(head * ROWS, (head + 1) * ROWS)
            q_rows = r.qz[which, rows, :]
            do_rows = r.doz[which, rows, :]
            weights = jnp.exp2(nt(keys, q_rows) * SCORE_SCALE - r.l2[which, 0:1, rows])
            if masked:
                key = lax.broadcasted_iota(jnp.int32, weights.shape, 0)
                row = lax.broadcasted_iota(jnp.int32, weights.shape, 1)
                weights = jnp.where(row >= key, weights, 0.0)
            score_grad = (weights * (nt(keys, do_rows) - r.delta[which, 0:1, rows])).astype(BF16)
            part = nn(score_grad, q_rows) + nn(weights.astype(BF16), do_rows)
            result = part if result is None else result + part
            r.dqt[which, :, rows] += nn(keys_t, score_grad)
        return result * key_scale

    def dkv_copy(block):
        return (
            r.dkv_out.at[block],
            r.dkv_in.at[j_role, x],
            r.dkv_send.at[block],
            r.dkv_recv.at[j_role, x],
            s,
            block,
            z,
        )

    def dkv_start(block):
        here = (s == d) & (block == c)

        @pl.when(jnp.logical_not(here))
        def _():
            remote(*dkv_copy(block)).start()

        @pl.when(here)
        def _():
            source, there, _, arrived = dkv_copy(block)[:4]
            local_sem(source, there, arrived).start()

    def of_both(block):
        return (block < 4) | ((block >= 4) & (block <= 8 + x))

    def class_of(block):
        return jnp.where(lower(block) < 4, 0, 1)

    def part_copy(block):
        index = lax.rem(block, 8)
        return remote(
            r.dkv_out.at[block],
            r.dkv_part.at[index],
            r.part_send_sem.at[block],
            r.part_recv_sem.at[index],
            1 - d,
            c,
            z,
        )

    def dispatch(block):
        both = of_both(block)

        @pl.when(both & (class_of(block) != d))
        def _():
            part_copy(block).start()

        @pl.when(jnp.logical_not(both))
        def _():
            dkv_start(block)

    def combine(block):
        index = lax.rem(block, 8)
        part_copy(block).wait_recv()
        r.dkv_out[block] = (
            r.dkv_out[block].astype(F32) + r.dkv_part[index].astype(F32)
        ).astype(BF16)
        dkv_start(block)

    def combine_own(i):
        first = own(i)
        combine(first)

        @pl.when((d == 1) & (first >= low))
        def _():
            combine(15 - first)

    r.dkv_out[low] = (backward_tile(low, 1, False) + backward_tile(low, 0, True)).astype(BF16)
    r.dkv_out[high] = backward_tile(high, 1, True).astype(BF16)
    dispatch(high)

    def backward_step(k, carry):
        odd = lax.rem(k, 2) == 1
        first = jnp.where(odd, others((k - 1) // 2), own(k // 2))
        below = first < low
        one = backward_tile(first, 1, False)
        two = backward_tile(jnp.where(below, first, 15 - first), jnp.where(below, 0, 1), False)

        @pl.when(below)
        def _():
            r.dkv_out[first] = (one + two).astype(BF16)
            dispatch(first)

        @pl.when(jnp.logical_not(below))
        def _():
            r.dkv_out[first] = one.astype(BF16)
            dispatch(first)
            r.dkv_out[15 - first] = two.astype(BF16)
            dispatch(15 - first)

        @pl.when(odd & (k >= 3))
        def _():
            combine_own((k - 3) // 2)

        return carry

    lax.fori_loop(1, 5, backward_step, 0)
    gather_branch.relay()
    block_rows = r.hidden[columns_of(z, 96), :] + r.down_send[z].astype(F32)
    r.block[z] = (block_rows + reduce_down.finish()).astype(BF16)
    gather_block = ZGather(r.block, r.block_sems, d, c, z).start()
    lax.fori_loop(5, 8, backward_step, 0)

    def dq_copy(which):
        block = high if which else low
        return (
            r.dq_out.at[which],
            r.dq_in.at[j_role],
            r.dq_send.at[which],
            r.dq_recv.at[j_role],
            s,
            block,
            z,
        )

    for which in range(2):
        flat = r.dqt[which].T * 0.125
        r.dq_out[which] = jnp.where(
            lane < 64, flat[:ROWS], pltpu.roll(flat[ROWS:], 64, 1)
        ).astype(BF16)
        block = high if which else low
        here = (s == d) & (block == c)

        @pl.when(jnp.logical_not(here))
        def _():
            remote(*dq_copy(which)).start()

        @pl.when(here)
        def _():
            source, there, _, arrived = dq_copy(which)[:4]
            local_sem(source, there, arrived).start()

    combine_own(3)
    for item in up_items:
        item.start()

    cosine, sine = tables(c, r.row_cos, r.row_sin, r.block_cos, r.block_sin)
    for j in range(2):
        local_sem(r.dq_out.at[0], r.dq_in.at[j], r.dq_recv.at[j]).wait()
    query_part = jnp.zeros((1, 128), F32)
    for j in range(2):
        columns = slice(j * 128, (j + 1) * 128)
        raw_grad, gain_part = pair_backward(
            r.dq_in[j].astype(F32), r.qraw[:, columns], query_gain, cosine, sine
        )
        r.grads[:, columns] = raw_grad.astype(BF16)
        query_part = query_part + gain_part
    r.gains[2:3, 0:128] = query_part + pltpu.roll(query_part, 64, 1)

    def project_query(t, carry):
        columns = columns_of(t, 256)
        r.total[:, columns] = nt(r.grads[:, 0:256], r.wq[columns, :])
        return carry

    lax.fori_loop(0, 4, project_query, 0)
    gather_block.relay()

    for j in range(2):
        r.dkv[j] = jnp.zeros((ROWS, 128), F32)

    def collect(column, carry):
        @pl.when(c <= 15 - column)
        def _():
            for j in range(2):
                local_sem(
                    r.dkv_out.at[0], r.dkv_in.at[j, column], r.dkv_recv.at[j, column]
                ).wait()
                r.dkv[j] += r.dkv_in[j, column].astype(F32)

        return carry

    lax.fori_loop(0, 4, collect, 0)
    first, second = r.dkv[0], r.dkv[1]
    raw_grad, key_part = pair_backward(
        jnp.where(lane < 64, first, pltpu.roll(second, 64, 1)),
        r.kraw[...],
        key_gain,
        cosine,
        sine,
    )
    r.grads[:, 256:384] = raw_grad.astype(BF16)
    r.grads[:, 384:512] = jnp.where(lane < 64, pltpu.roll(first, 64, 1), second).astype(BF16)
    r.gains[3:4, 0:128] = key_part + pltpu.roll(key_part, 64, 1)

    def project_keys(t, carry):
        columns = columns_of(t, 256)
        value = (
            r.total[:, columns]
            + nt(r.grads[:, 256:384], r.wk[columns, :])
            + nt(r.grads[:, 384:512], r.wv[columns, :])
        ).astype(BF16)
        for other in range(4):
            r.last_send[other, :, columns] = value[other * 96 : (other + 1) * 96]
        return carry

    lax.fori_loop(0, 4, project_keys, 0)
    reduce_last = ZDirectReduce(r.last_send, r.last_land, r.last_sems, d, c, z).start()

    r.late[:, :, :, :, 0:256] = (
        nn(r.normed_t[...], r.grads[:, 0:256]).astype(BF16).reshape(2, 4, 4, 32, 256)
    )
    gather_branch.finish()
    for source in range(4):

        def move(t, carry):
            columns = columns_of(t, 128)
            r.mixed_t[columns, source * 96 : (source + 1) * 96] = r.branch[source, :, columns].T
            return carry

        lax.fori_loop(0, 8, move, 0)
    r.late[:, :, :, :, 256:512] = (
        nn(r.mixed_t[...], r.oall[:, column]).astype(BF16).reshape(2, 4, 4, 32, 256)
    )
    late_core = to_other_core(3, r.late, r.late_land)
    r.last[...] = nn(r.normed_t[...], r.grads[:, 256:512]).astype(BF16).reshape(2, 4, 4, 32, 256)
    last_core = to_other_core(4, r.last, r.last_core)
    for item in down_items + gate_items:
        item.middle()
    add_cores(late_core, r.late, r.late_land)
    for item in late_items:
        item.start()
    add_cores(last_core, r.last, r.last_core)
    for item in last_items:
        item.start()
    for item in up_items:
        item.middle()

    rows = columns_of(z, 96)
    incoming = r.last_send[z].astype(F32) + reduce_last.finish()
    values = r.x[rows, :].astype(F32)
    factor = lax.rsqrt(jnp.mean(values * values, axis=1, keepdims=True) + epsilon)
    weighted = incoming * r.attention_gain[...]
    projected = jnp.sum(weighted * values, axis=1, keepdims=True) * (1.0 / 1024.0)
    r.gains[0:1, :] = jnp.sum(incoming * values * factor, axis=0, keepdims=True)
    gather_gains = []
    for step in range(1, 8):
        copy = remote(
            r.gains,
            r.gains_land.at[step - 1],
            r.gain_sems.at[0, step - 1],
            r.gain_sems.at[1, step - 1],
            d if step < 4 else 1 - d,
            c,
            lax.rem(z + step, 4),
        )
        copy.start()
        gather_gains.append(copy)
    r.rows_out[z] = (
        r.grad_rows[...] + factor * weighted - values * (factor * factor * factor * projected)
    ).astype(BF16)
    gather_rows = ZDirectGather(r.rows_out, r.rows_sems, d, c, z).start()

    for copy in gather_gains:
        copy.wait_recv()
    r.chunk_in[...] = jnp.zeros_like(r.chunk_in)
    gain_total = r.gains[...]
    for step in range(7):
        gain_total = gain_total + r.gains_land[step]
    r.chunk_in[0:8, :] = gain_total
    column_part = r.chunk_in[:, columns_of(d, 512)].T
    row_kind = lax.rem(lax.broadcasted_iota(jnp.int32, (512, 128), 0), 32)
    lane_index = lax.broadcasted_iota(jnp.int32, (512, 128), 1)
    query_total, key_total = r.chunk_in[2:3, 0:128], r.chunk_in[3:4, 0:128]
    spread = jnp.where(row_kind == 0, query_total, jnp.where(row_kind == 1, key_total, 0.0))
    r.chunk[...] = (
        jnp.where(lane_index < 64, column_part, spread).astype(BF16).reshape(4, 4, 32, 128)
    )
    gain_item.start()
    for item in late_items + last_items:
        item.middle()
    gain_item.middle()

    sums = (r.gate_sum, r.up_sum, r.down_sum)
    for item, (index, start, width, _) in zip(plane[:6], FF_ITEMS):
        sums[index][:, start : start + width] = item.finish()
    for item, (_, _, width, _, start) in zip(late_items + last_items, LATE_ITEMS):
        r.late_sum[:, start : start + width] = item.finish()
    r.gain_sum[...] = gain_item.finish()
    gather_block.finish()
    gather_rows.finish()

    copies = w_copies + forwards + cores + gather_gains + [late_core, last_core]
    for transfer in (
        reduce_mixed,
        gather_branch,
        reduce_down,
        gather_block,
        reduce_last,
        gather_rows,
    ):
        copies = copies + transfer.copies
    for copy in copies:
        copy.wait_send()
    for item in plane:
        item.sent()
    for j in range(2):

        @pl.when(jnp.logical_not((home(j) == c) & (home_core == d)))
        def _():
            q_copy(j).wait_send()
            remote(*do_copy(j, 0)).wait_send()

        for step in (1, 2, 3):
            remote(*do_copy(j, step)).wait_send()

    def kv_sent(k, carry):
        for j in range(2):
            core, chip, needed = kv_target(k, j)

            @pl.when(needed & jnp.logical_not((core == d) & (chip == c)))
            def _():
                kv_copy(k, j).wait_send()

        first = own(k)
        hand_on(2 * k, first).wait_send()

        @pl.when((d == 1) & (first >= low))
        def _():
            hand_on(2 * k + 1, 15 - first).wait_send()

        return carry

    lax.fori_loop(0, 4, kv_sent, 0)
    for which in range(2):
        block = high if which else low
        for step in (1, 2, 3):
            remote(*o_copy(which, step)).wait_send()

        @pl.when(jnp.logical_not((s == d) & (block == c)))
        def _():
            remote(*o_copy(which, 0)).wait_send()
            remote(*dq_copy(which)).wait_send()

    def dkv_sent(block, carry):
        both = of_both(block)
        mine = class_of(block) == d

        @pl.when((block <= high) & both & jnp.logical_not(mine))
        def _():
            part_copy(block).wait_send()

        owner_here = (s == d) & (block == c)

        @pl.when((block <= high) & (jnp.logical_not(both) | mine) & jnp.logical_not(owner_here))
        def _():
            remote(*dkv_copy(block)).wait_send()

        return carry

    lax.fori_loop(0, 16, dkv_sent, 0)


def emit_kernel(
    block, rows, gate, up, down, late, gains,
    block_out, input_grad, attention_gain, query_gain, key_gain,
    wq, wk, wv, wo, feed_gain, wg, wu, wd,
):
    d, c, _ = place()
    for part in range(4):
        block_out[part * 96 : (part + 1) * 96, :] = block[part]
        input_grad[part * 96 : (part + 1) * 96, :] = rows[part].astype(F32)
    wg[...] = gate[...]
    wu[...] = up[...]
    wd[...] = down[...]
    wq[...] = late[:, 0:256]
    wk[...] = late[:, 256:384]
    wv[...] = late[:, 384:512]
    wo[...] = late[:, 512:768]
    turned = gains[...].T
    attention_gain[...] = turned[0:1, :]
    feed_gain[...] = turned[1:2, :]
    first = 64 + 2 * (d * 16 + c)
    lane = lax.broadcasted_iota(jnp.int32, (1, 128), 1)
    pair = lax.broadcasted_iota(jnp.int32, (1, 2), 1)
    for row, out in ((0, query_gain), (1, key_gain)):
        values = gains[row : row + 1, :]
        one = jnp.sum(jnp.where(lane == first, values, 0.0), axis=1, keepdims=True)
        two = jnp.sum(jnp.where(lane == first + 1, values, 0.0), axis=1, keepdims=True)
        out[...] = jnp.where(pair == 0, one, two)


def shards(
    inputs,
    cotangent,
    attention_gain,
    query_gain,
    key_gain,
    w_query,
    key_weight,
    value_weight,
    w_out,
    feed_gain,
    w_gate,
    w_up,
    w_down,
):
    vmem, anywhere = pl.BlockSpec(memory_space=pltpu.VMEM), pl.BlockSpec(memory_space=pl.ANY)
    landings = []
    for width in SUM_WIDTHS:
        landings += [pltpu.VMEM((3, 4, 32, width), BF16), pltpu.VMEM((3, 32, width), BF16)]
    results = pl.pallas_call(
        block_kernel,
        out_shape=[jax.ShapeDtypeStruct(*spec) for spec in OUTPUTS.values()],
        in_specs=[vmem] * len(INPUTS) + [anywhere] * len(STREAMED),
        out_specs=[vmem] * len(OUTPUTS),
        scratch_shapes=[pltpu.VMEM(*spec) for spec in BUFFERS.values()]
        + [pltpu.SemaphoreType.DMA(shape) for shape in SEMAPHORES.values()]
        + landings,
        compiler_params=pltpu.CompilerParams(
            collective_id=1, has_side_effects=True, vmem_limit_bytes=VMEM_LIMIT
        ),
        name="block",
    )(
        inputs,
        attention_gain.reshape(1, 1024),
        w_query,
        key_weight,
        value_weight,
        query_gain.reshape(1, 64),
        key_gain.reshape(1, 64),
        *[jnp.asarray(table) for table in split_columns()],
        feed_gain.reshape(1, 1024),
        cotangent,
        w_out,
        w_gate,
        w_up,
        w_down,
    )
    shapes = [
        ((ROWS, 1024), BF16),
        ((ROWS, 1024), F32),
        ((1, 32), F32),
        ((1, 2), F32),
        ((1, 2), F32),
        ((32, 256), F32),
        ((32, 128), F32),
        ((32, 128), F32),
        ((32, 256), F32),
        ((1, 32), F32),
        ((32, 1152), F32),
        ((32, 1152), F32),
        ((32, 1152), F32),
    ]
    outputs = pl.pallas_call(
        emit_kernel,
        out_shape=[jax.ShapeDtypeStruct(*spec) for spec in shapes],
        in_specs=[vmem] * len(results),
        out_specs=[vmem] * len(shapes),
        compiler_params=pltpu.CompilerParams(vmem_limit_bytes=VMEM_LIMIT),
        name="emit",
    )(*results)
    return tuple(
        value.reshape(-1) if value.shape[0] == 1 else value for value in outputs
    )


def solution(mesh):
    both = ("dp", "ctx")
    by_head = P(None, "head")
    reduced = P(both, "head")
    return jax.shard_map(
        shards,
        mesh=mesh,
        in_specs=(
            P(both, None),
            P(both, None),
            P(),
            P(),
            P(),
            by_head,
            by_head,
            by_head,
            by_head,
            P(),
            by_head,
            by_head,
            by_head,
        ),
        out_specs=(
            P(both, None),
            P(both, None),
            P(both),
            P(both),
            P(both),
            reduced,
            reduced,
            reduced,
            reduced,
            P(both),
            reduced,
            reduced,
            reduced,
        ),
        check_vma=False,
    )
```

```python
from types import SimpleNamespace

import jax
import jax.numpy as jnp
import numpy as np
from jax import lax
from jax.experimental import pallas as pl
from jax.experimental.pallas import tpu as pltpu
from jax.sharding import PartitionSpec as P

epsilon = 1e-05
theta_base = 1000000.0
MESH = pl.DeviceIdType.MESH
F32 = jnp.float32
BF16 = jnp.bfloat16
ROWS = 384
LOG2E = 1.4426950408889634
VMEM_LIMIT = 63 * 1024 * 1024


def remote(src, dst, send_sem, recv_sem, d, c, z):
    return pltpu.make_async_remote_copy(
        src_ref=src,
        dst_ref=dst,
        send_sem=send_sem,
        recv_sem=recv_sem,
        device_id=(d, c, z),
        device_id_type=MESH,
    )


def local_sem(src, dst, sem):
    return pltpu.make_async_copy(src, dst, sem)


def place():
    return lax.axis_index("dp"), lax.axis_index("ctx"), lax.axis_index("head")


def role_of(d, c):
    row, column = c // 4, lax.rem(c, 4)
    low = jnp.where(d == 0, column, 7 - column)
    return row // 2, lax.rem(row, 2), low, 15 - low


def lower(block):
    return jnp.minimum(block, 15 - block)


def spread_heads(pair, upper):
    pair = pair.astype(F32)
    lane = lax.broadcasted_iota(jnp.int32, pair.shape, 1)
    turned = pltpu.roll(pair, 64, 1)
    if upper:
        first, second = jnp.where(lane >= 64, turned, 0.0), jnp.where(lane >= 64, pair, 0.0)
    else:
        first, second = jnp.where(lane < 64, pair, 0.0), jnp.where(lane < 64, turned, 0.0)
    return first.astype(BF16), second.astype(BF16)


def nt(left, right):
    return lax.dot_general(left, right, (((1,), (1,)), ((), ())), preferred_element_type=F32)


def nn(left, right):
    return lax.dot_general(left, right, (((1,), (0,)), ((), ())), preferred_element_type=F32)


SCORE_SCALE = LOG2E / 8.0


def split_columns(half_width=32, rows=ROWS, blocks=16):
    lane = np.arange(128) % half_width
    frequency = theta_base ** (-2.0 * lane / (2 * half_width))
    row_angle = np.arange(rows)[:, None] * frequency[None, :]
    block_angle = (np.arange(blocks) * rows)[:, None] * frequency[None, :]
    return [
        np.asarray(table, np.float32)
        for table in (
            np.cos(row_angle),
            np.sin(row_angle),
            np.cos(block_angle),
            np.sin(block_angle),
        )
    ]


def tables(c, row_cos, row_sin, block_cos, block_sin):
    bc, bs = block_cos[pl.ds(c, 1), :], block_sin[pl.ds(c, 1), :]
    rc, rs = row_cos[...], row_sin[...]
    return rc * bc - rs * bs, rs * bc + rc * bs


def lanes(rows=ROWS):
    return lax.broadcasted_iota(jnp.int32, (rows, 128), 1)


def half_sums(values):
    lane = lanes(values.shape[0])
    first = jnp.sum(jnp.where(lane < 64, values, 0.0), axis=1, keepdims=True)
    second = jnp.sum(jnp.where(lane >= 64, values, 0.0), axis=1, keepdims=True)
    return jnp.where(lane < 64, first, second)


def turn(values):
    lane = lanes(values.shape[0])
    return jnp.where(lax.rem(lane, 64) < 32, -pltpu.roll(values, 96, 1), pltpu.roll(values, 32, 1))


def turn_back(values):
    lane = lanes(values.shape[0])
    return jnp.where(lax.rem(lane, 64) < 32, pltpu.roll(values, 96, 1), -pltpu.roll(values, 32, 1))


def pair_forward(raw, gain, cosine, sine):
    scale = lax.rsqrt(half_sums(raw * raw) * (1.0 / 64.0) + epsilon)
    normed = raw * scale * gain
    return normed * cosine + turn(normed) * sine


def pair_backward(grad, raw, gain, cosine, sine):
    incoming = grad * cosine + turn_back(grad * sine)
    scale = lax.rsqrt(half_sums(raw * raw) * (1.0 / 64.0) + epsilon)
    weighted = incoming * gain
    inner = half_sums(weighted * raw) * (1.0 / 64.0)
    raw_grad = scale * weighted - raw * (scale * scale * scale) * inner
    return raw_grad, jnp.sum(incoming * raw * scale, axis=0, keepdims=True)


def z_send(source_of, landed, sems, d, c, z):
    copies = []
    for step in (2, 1, 3):
        other = lax.rem(z + step, 4)
        copy = remote(
            source_of(other),
            landed(step),
            sems.at[0, step - 1],
            sems.at[1, step - 1],
            d,
            c,
            other,
        )
        copy.start()
        copies.append(copy)
    return copies


class ZDirectReduce:
    def __init__(self, part, land, sems, d, c, z):
        self.args = (lambda other: part.at[other], lambda step: land.at[step - 1], sems, d, c, z)
        self.land = land

    def start(self):
        self.copies = z_send(*self.args)
        return self

    def finish(self):
        for copy in self.copies:
            copy.wait_recv()
        land = self.land
        return land[0].astype(F32) + land[1].astype(F32) + land[2].astype(F32)


class ZDirectGather:
    def __init__(self, slots, sems, d, c, z):
        self.args = (lambda other: slots.at[z], lambda step: slots.at[z], sems, d, c, z)

    def start(self):
        self.copies = z_send(*self.args)
        return self

    def finish(self):
        for copy in self.copies:
            copy.wait_recv()


class ZGather:
    def __init__(self, slots, sems, d, c, z):
        self.slots, self.sems = slots, sems
        self.d, self.c, self.z = d, c, z
        self.up, self.down = lax.rem(z + 1, 4), lax.rem(z + 3, 4)

    def copy(self, index, block, plane):
        copy = remote(
            block, block, self.sems.at[0, index], self.sems.at[1, index], self.d, self.c, plane
        )
        copy.start()
        return copy

    def start(self):
        low, high = self.slots.at[self.z, 0:48], self.slots.at[self.z, 48:96]
        self.copies = [
            self.copy(0, low, self.up),
            self.copy(1, high, self.down),
            self.copy(2, high, self.up),
            self.copy(3, low, self.down),
        ]
        return self

    def relay(self):
        self.copies[0].wait_recv()
        self.copies.append(self.copy(4, self.slots.at[self.down, 0:48], self.up))
        self.copies[1].wait_recv()
        self.copies.append(self.copy(5, self.slots.at[self.up, 48:96], self.down))

    def finish(self):
        for copy in self.copies[2:]:
            copy.wait_recv()


class PlaneSum:
    def __init__(self, index, source, y_first, landed, landed_last, sems):
        self.index, self.source, self.y_first = index, source, y_first
        self.landed, self.landed_last = landed, landed_last
        self.first_sems, self.last_sems = sems
        self.d, c, self.z = place()
        self.y, self.x = c // 4, lax.rem(c, 4)

    def along(self, first, step):
        if first == self.y_first:
            other = lax.rem(self.y + step, 4)
            return other, other * 4 + self.x
        other = lax.rem(self.x + step, 4)
        return other, self.y * 4 + other

    def start(self):
        self.firsts = []
        for step in (2, 1, 3):
            other, chip = self.along(True, step)
            copy = remote(
                self.source.at[other] if self.y_first else self.source.at[:, other],
                self.landed.at[step - 1],
                self.first_sems.at[0, self.index, step - 1],
                self.first_sems.at[1, self.index, step - 1],
                self.d,
                chip,
                self.z,
            )
            copy.start()
            self.firsts.append(copy)

    def middle(self):
        for copy in self.firsts:
            copy.wait_recv()

        def add(r, carry):
            own = self.source.at[self.y, r] if self.y_first else self.source.at[r, self.x]
            total = own[...].astype(F32)
            for step in range(3):
                total = total + self.landed[step, r].astype(F32)
            own[...] = total.astype(BF16)
            return carry

        lax.fori_loop(0, 4, add, 0)
        self.lasts = []
        for step in (2, 1, 3):
            other, chip = self.along(False, step)
            own = self.source.at[self.y, other] if self.y_first else self.source.at[other, self.x]
            copy = remote(
                own,
                self.landed_last.at[step - 1],
                self.last_sems.at[0, self.index, step - 1],
                self.last_sems.at[1, self.index, step - 1],
                self.d,
                chip,
                self.z,
            )
            copy.start()
            self.lasts.append(copy)

    def finish(self):
        for copy in self.lasts:
            copy.wait_recv()
        total = self.source[self.y, self.x].astype(F32)
        for step in range(3):
            total = total + self.landed_last[step].astype(F32)
        return total

    def sent(self):
        for copy in self.firsts + self.lasts:
            copy.wait_send()


FF_ITEMS = (
    (0, 0, 640, True),
    (0, 640, 512, False),
    (1, 0, 512, True),
    (1, 512, 640, False),
    (2, 0, 640, True),
    (2, 640, 512, False),
)
LATE_ITEMS = (
    (0, 0, 256, True, 0),
    (0, 256, 256, False, 512),
    (1, 0, 128, True, 256),
    (1, 128, 128, False, 384),
)
SUM_WIDTHS = [item[2] for item in FF_ITEMS + LATE_ITEMS] + [128]

INPUTS = [
    "attention_gain",
    "query_gain",
    "key_gain",
    "row_cos",
    "row_sin",
    "block_cos",
    "block_sin",
    "feed_gain",
]
STREAMED = ["x", "wk", "wv", "wq", "cot", "wo", "wg", "wu", "wd"]
OUTPUTS = {
    "block": ((4, 96, 1024), BF16),
    "rows_out": ((4, 96, 1024), BF16),
    "gate_sum": ((32, 1152), F32),
    "up_sum": ((32, 1152), F32),
    "down_sum": ((32, 1152), F32),
    "late_sum": ((32, 768), F32),
    "gain_sum": ((32, 128), F32),
}
BUFFERS = {
    "x": ((ROWS, 1024), BF16),
    "wk": ((1024, 128), BF16),
    "wv": ((1024, 128), BF16),
    "wq": ((1024, 256), BF16),
    "cot": ((ROWS, 1024), BF16),
    "wg": ((1024, 1152), BF16),
    "wu": ((1024, 1152), BF16),
    "wd": ((1024, 1152), BF16),
    "wall": ((1024, 1024), BF16),
    "normed": ((ROWS, 1024), BF16),
    "normed_t": ((1024, ROWS), BF16),
    "pair_gains": ((8, 128), F32),
    "qraw": ((ROWS, 256), F32),
    "kraw": ((ROWS, 128), F32),
    "q": ((2, ROWS, 128), BF16),
    "kv": ((2, ROWS, 128), BF16),
    "kvs": ((16, ROWS, 128), BF16),
    "qs": ((2, ROWS, 128), BF16),
    "os": ((2, ROWS, 128), BF16),
    "l2": ((2, 8, 2 * ROWS), F32),
    "qz": ((2, 2 * ROWS, 128), BF16),
    "acc": ((2, 2 * ROWS, 128), F32),
    "sums": ((2, 2 * ROWS, 128), F32),
    "oall": ((ROWS, 1024), BF16),
    "hidden": ((ROWS, 1024), F32),
    "scale": ((ROWS, 128), F32),
    "mixed": ((ROWS, 1024), BF16),
    "mixed_t": ((1024, ROWS), BF16),
    "cot_t": ((1024, ROWS), BF16),
    "inner": ((ROWS, 1152), BF16),
    "grad_gate": ((ROWS, 1152), BF16),
    "grad_up": ((ROWS, 1152), BF16),
    "total": ((ROWS, 1024), F32),
    "part_send": ((4, 96, 1024), BF16),
    "part_land": ((3, 96, 1024), BF16),
    "down_send": ((4, 96, 1024), BF16),
    "down_land": ((3, 96, 1024), BF16),
    "dw_g": ((2, 4, 4, 32, 1152), BF16),
    "dw_u": ((2, 4, 4, 32, 1152), BF16),
    "dw_d": ((2, 4, 4, 32, 1152), BF16),
    "land_g": ((4, 4, 32, 1152), BF16),
    "land_u": ((4, 4, 32, 1152), BF16),
    "land_d": ((4, 4, 32, 1152), BF16),
    "grad_rows": ((96, 1024), F32),
    "branch": ((4, 96, 1024), BF16),
    "dob": ((96, 1024), BF16),
    "doz": ((2, 2 * ROWS, 128), BF16),
    "delta": ((2, 8, 2 * ROWS), F32),
    "dos": ((2, ROWS, 128), BF16),
    "dqt": ((2, 128, 2 * ROWS), F32),
    "dq_out": ((2, ROWS, 128), BF16),
    "dq_in": ((2, ROWS, 128), BF16),
    "dkv_out": ((16, ROWS, 128), BF16),
    "dkv_in": ((2, 4, ROWS, 128), BF16),
    "dkv_part": ((8, ROWS, 128), BF16),
    "dkv": ((2, ROWS, 128), F32),
    "grads": ((ROWS, 512), BF16),
    "last_send": ((4, 96, 1024), BF16),
    "last_land": ((3, 96, 1024), BF16),
    "late": ((2, 4, 4, 32, 512), BF16),
    "late_land": ((4, 4, 32, 512), BF16),
    "last": ((2, 4, 4, 32, 256), BF16),
    "last_core": ((4, 4, 32, 256), BF16),
    "gains": ((8, 1024), F32),
    "gains_land": ((7, 8, 1024), F32),
    "chunk_in": ((128, 1024), F32),
    "chunk": ((4, 4, 32, 128), BF16),
}
SEMAPHORES = {
    "load": (9,),
    "q_send": (2,),
    "q_recv": (2,),
    "kv_send": (8,),
    "hand_send": (8,),
    "kv_recv": (16,),
    "o_send": (2, 4),
    "o_recv": (8,),
    "w_sems": (2, 3),
    "wc_sems": (2, 3),
    "mixed_sems": (2, 6),
    "core_sems": (2, 5),
    "do_send": (2, 4),
    "do_recv": (2, 4),
    "branch_sems": (2, 6),
    "down_sems": (2, 6),
    "block_sems": (2, 6),
    "dq_send": (2,),
    "dq_recv": (2,),
    "dkv_send": (16,),
    "dkv_recv": (2, 4),
    "part_send_sem": (16,),
    "part_recv_sem": (8,),
    "last_sems": (2, 6),
    "gain_sems": (2, 7),
    "rows_sems": (2, 6),
    "sum_first": (2, len(SUM_WIDTHS), 3),
    "sum_last": (2, len(SUM_WIDTHS), 3),
}


def columns_of(t, width):
    return pl.ds(pl.multiple_of(t * width, width), width)


def transpose_into(out, source):
    def move(t, carry):
        columns = columns_of(t, 128)
        out[columns, :] = source[:, columns].T
        return carry

    lax.fori_loop(0, 8, move, 0)


def block_kernel(*refs):
    names = INPUTS + ["hbm_" + name for name in STREAMED] + list(OUTPUTS) + list(BUFFERS)
    names += list(SEMAPHORES)
    r = SimpleNamespace(**dict(zip(names, refs)))
    landings = refs[len(names) :]
    d, c, z = place()
    s, j_role, low, high = role_of(d, c)
    x = lax.rem(c, 4)
    slot = jnp.where(c >= 8, 1, 0)
    home_core = jnp.where(lower(c) < 4, 0, 1)
    home_column = jnp.where(home_core == 0, lower(c), 7 - lower(c))

    def home(j):
        return (2 * d + j) * 4 + home_column

    def own(i):
        return jnp.where(d == 0, lax.rem(x - i + 8, 4), 4 + lax.rem(11 - x - i, 4))

    def others(i):
        return jnp.where(d == 0, 4 + lax.rem(11 - x - i, 4), lax.rem(x - i + 8, 4))

    column = columns_of(z, 256)
    lane = lanes()

    load_wo = local_sem(r.hbm_wo, r.wall.at[:, column], r.load.at[0])
    load_cot = local_sem(r.hbm_cot, r.cot, r.load.at[1])
    load_wg = local_sem(r.hbm_wg, r.wg, r.load.at[2])
    load_wu = local_sem(r.hbm_wu, r.wu, r.load.at[3])
    load_wd = local_sem(r.hbm_wd, r.wd, r.load.at[4])
    load_x = local_sem(r.hbm_x, r.x, r.load.at[5])
    load_wk = local_sem(r.hbm_wk, r.wk, r.load.at[6])
    load_wv = local_sem(r.hbm_wv, r.wv, r.load.at[7])
    load_wq = local_sem(r.hbm_wq, r.wq, r.load.at[8])
    for copy in (load_x, load_wk, load_wv, load_wq, load_wo):
        copy.start()

    barrier = pltpu.get_barrier_semaphore()

    def signal(*device):
        pl.semaphore_signal(barrier, inc=1, device_id=device, device_id_type=MESH)

    def greet(index, carry):
        other_d, other_c = index // 16, lax.rem(index, 16)

        @pl.when((other_d != d) | (other_c != c))
        def _():
            signal(other_d, other_c, z)

        return carry

    lax.fori_loop(0, 32, greet, 0)
    for step in (1, 2, 3):
        other = lax.rem(z + step, 4)
        signal(d, c, other)
        signal(1 - d, c, other)
        for j in range(2):
            signal(home_core, home(j), other)
        for block in (low, high):
            signal(s, block, other)

    load_x.wait()

    def first_norm(t, carry):
        rows = columns_of(t, 96)
        values = r.x[rows, :].astype(F32)
        factor = lax.rsqrt(jnp.mean(values * values, axis=1, keepdims=True) + epsilon)
        r.normed[rows, :] = (values * factor * r.attention_gain[...]).astype(BF16)
        return carry

    lax.fori_loop(0, 4, first_norm, 0)
    normed = r.normed[...]
    for half in (0, 64):
        r.pair_gains[0:1, half : half + 64] = r.query_gain[...]
        r.pair_gains[1:2, half : half + 64] = r.key_gain[...]
    query_gain, key_gain = r.pair_gains[0:1, :], r.pair_gains[1:2, :]
    cosine, sine = tables(c, r.row_cos, r.row_sin, r.block_cos, r.block_sin)
    load_wk.wait()
    load_wv.wait()
    key_raw = nn(normed, r.wk[...])
    r.kraw[...] = key_raw
    value = nn(normed, r.wv[...])
    key = pair_forward(key_raw, key_gain, cosine, sine)
    r.kv[0] = jnp.where(lane < 64, key, pltpu.roll(value, 64, 1)).astype(BF16)
    r.kv[1] = jnp.where(lane < 64, pltpu.roll(key, 64, 1), value).astype(BF16)
    pl.semaphore_wait(barrier, 31 + 6 + 6 + 6)

    def kv_target(k, j):
        column = lax.rem(jnp.where(home_core == 0, home_column + k, home_column - k + 4), 4)
        core = jnp.where((home_core == 1) & (c <= 8 + column), 1, 0)
        return core, (2 * d + j) * 4 + column, c <= 15 - column

    def kv_copy(k, j):
        core, chip, _ = kv_target(k, j)
        return remote(
            r.kv.at[j], r.kvs.at[c], r.kv_send.at[2 * k + j], r.kv_recv.at[c], core, chip, z
        )

    def kv_start(k, carry):
        for j in range(2):
            core, chip, needed = kv_target(k, j)
            here = (core == d) & (chip == c)

            @pl.when(needed & jnp.logical_not(here))
            def _():
                kv_copy(k, j).start()

            @pl.when(needed & here)
            def _():
                local_sem(r.kv.at[j], r.kvs.at[c], r.kv_recv.at[c]).start()

        return carry

    def q_copy(j):
        return remote(r.q.at[j], r.qs.at[slot], r.q_send.at[j], r.q_recv.at[slot], home_core, home(j), z)

    kv_start(0, 0)
    load_wq.wait()
    query_raw = nn(normed, r.wq[...])
    r.qraw[...] = query_raw
    for j in range(2):
        pair = query_raw[:, j * 128 : (j + 1) * 128]
        r.q[j] = pair_forward(pair, query_gain, cosine, sine).astype(BF16)
        here = (home(j) == c) & (home_core == d)

        @pl.when(jnp.logical_not(here))
        def _():
            q_copy(j).start()

        @pl.when(here)
        def _():
            local_sem(r.q.at[j], r.qs.at[slot], r.q_recv.at[slot]).start()

    lax.fori_loop(1, 4, kv_start, 0)

    for copy in (load_cot, load_wg, load_wu, load_wd):
        copy.start()

    load_wo.wait()
    mine = columns_of(d, 512)
    w_copies = z_send(
        lambda other: r.wall.at[mine, column],
        lambda step: r.wall.at[mine, column],
        r.w_sems,
        d,
        c,
        z,
    )

    transpose_into(r.normed_t, r.normed)
    load_cot.wait()
    transpose_into(r.cot_t, r.cot)

    r.acc[...] = jnp.zeros_like(r.acc)
    r.sums[...] = jnp.zeros_like(r.sums)
    for which in range(2):
        local_sem(r.q.at[0], r.qs.at[which], r.q_recv.at[which]).wait()
        first, second = spread_heads(r.qs[which], False)
        r.qz[which, 0:ROWS, :] = first
        r.qz[which, ROWS : 2 * ROWS, :] = second

    def kv_wait(block):
        local_sem(r.kv.at[0], r.kvs.at[block], r.kv_recv.at[block]).wait()

    def forward_tile(block, which, masked):
        keys = r.kvs[block]
        for head in range(2):
            rows = slice(head * ROWS, (head + 1) * ROWS)
            weights = jnp.exp2(nt(r.qz[which, rows, :], keys) * SCORE_SCALE)
            if masked:
                row = lax.broadcasted_iota(jnp.int32, weights.shape, 0)
                key = lax.broadcasted_iota(jnp.int32, weights.shape, 1)
                weights = jnp.where(row >= key, weights, 0.0)
            r.sums[which, rows, :] += weights[:, 0:128] + weights[:, 128:256] + weights[:, 256:384]
            r.acc[which, rows, :] += nn(weights.astype(BF16), keys)

    def hand_on(index, block):
        return remote(
            r.kvs.at[block],
            r.kvs.at[block],
            r.hand_send.at[index],
            r.kv_recv.at[block],
            1 - d,
            c,
            z,
        )

    kv_wait(low)
    kv_wait(high)
    hand_on(0, low).start()

    @pl.when(d == 1)
    def _():
        hand_on(1, high).start()

    forward_tile(low, 1, False)
    forward_tile(low, 0, True)
    forward_tile(high, 1, True)

    def forward_step(k, carry):
        first = jnp.where(k < 4, own(k), others(k - 4))
        below = first < low
        kv_wait(first)

        @pl.when(k < 4)
        def _():
            hand_on(2 * k, first).start()

        @pl.when(jnp.logical_not(below))
        def _():
            kv_wait(15 - first)

            @pl.when((k < 4) & (d == 1))
            def _():
                hand_on(2 * k + 1, 15 - first).start()

        forward_tile(first, 1, False)
        forward_tile(jnp.where(below, first, 15 - first), jnp.where(below, 0, 1), False)
        return carry

    lax.fori_loop(1, 8, forward_step, 0)

    def o_copy(which, step):
        block = high if which else low
        other = lax.rem(z + step, 4)
        there = r.oall.at[:, columns_of(z * 2 + j_role, 128)]
        arrived = r.o_recv.at[z * 2 + j_role]
        return r.os.at[which], there, r.o_send.at[which, step], arrived, s, block, other

    for which in range(2):
        total = jnp.sum(r.sums[which], axis=1, keepdims=True)
        result = r.acc[which] / total
        r.os[which] = jnp.where(
            lane < 64, pltpu.roll(result[:ROWS], 64, 1), result[ROWS:]
        ).astype(BF16)
        block = high if which else low
        here = (s == d) & (block == c)
        for step in (2, 1, 3):
            remote(*o_copy(which, step)).start()

        @pl.when(jnp.logical_not(here))
        def _():
            remote(*o_copy(which, 0)).start()

        @pl.when(here)
        def _():
            source, there, _, arrived = o_copy(which, 0)[:4]
            local_sem(source, there, arrived).start()

    forwards = []
    for copy, step in zip(w_copies, (2, 1, 3)):
        copy.wait_recv()
        theirs = columns_of(lax.rem(z + 4 - step, 4), 256)
        forward = remote(
            r.wall.at[mine, theirs],
            r.wall.at[mine, theirs],
            r.wc_sems.at[0, step - 1],
            r.wc_sems.at[1, step - 1],
            1 - d,
            c,
            z,
        )
        forward.start()
        forwards.append(forward)
    for which in range(2):
        total = jnp.sum(r.sums[which], axis=1, keepdims=True)
        logs = jnp.broadcast_to(jnp.log2(total), (2 * ROWS, 128))
        r.l2[which] = logs.T[0:8]
    for forward in forwards:
        forward.wait_recv()
    for source in range(4):
        for j in range(2):
            there = r.oall.at[:, source * 256 + j * 128 : source * 256 + (j + 1) * 128]
            local_sem(r.os.at[0], there, r.o_recv.at[source * 2 + j]).wait()

    def project_out(t, carry):
        columns = columns_of(t, 256)
        r.hidden[:, columns] = r.x[:, columns].astype(F32) + nt(r.oall[...], r.wall[columns, :])
        return carry

    lax.fori_loop(0, 4, project_out, 0)

    def second_norm(t, carry):
        rows = columns_of(t, 96)
        values = r.hidden[rows, :]
        factor = lax.rsqrt(jnp.mean(values * values, axis=1, keepdims=True) + epsilon)
        r.scale[rows, :] = jnp.broadcast_to(factor, (96, 128))
        r.mixed[rows, :] = (values * factor * r.feed_gain[...]).astype(BF16)
        return carry

    lax.fori_loop(0, 4, second_norm, 0)
    r.total[...] = jnp.zeros_like(r.total)
    load_wg.wait()
    load_wu.wait()
    load_wd.wait()

    def units(t, carry):
        columns = columns_of(t, 384)
        gate = nn(r.mixed[...], r.wg[:, columns])
        up = nn(r.mixed[...], r.wu[:, columns])
        sigmoid = 1.0 / (1.0 + jnp.exp(-gate))
        silu = gate * sigmoid
        r.inner[:, columns] = (silu * up).astype(BF16)
        grad_inner = nn(r.cot[...], r.wd[:, columns])
        r.grad_up[:, columns] = (grad_inner * silu).astype(BF16)
        r.grad_gate[:, columns] = (
            grad_inner * up * sigmoid * (1.0 + gate * (1.0 - sigmoid))
        ).astype(BF16)
        r.total[...] += nt(r.grad_gate[:, columns], r.wg[:, columns]) + nt(
            r.grad_up[:, columns], r.wu[:, columns]
        )
        return carry

    lax.fori_loop(0, 3, units, 0)
    for other in range(4):
        r.part_send[other] = r.total[other * 96 : (other + 1) * 96, :].astype(BF16)
    reduce_mixed = ZDirectReduce(r.part_send, r.part_land, r.mixed_sems, d, c, z).start()

    def to_other_core(index, source, land):
        copy = remote(
            source.at[1 - d], land, r.core_sems.at[0, index], r.core_sems.at[1, index], 1 - d, c, z
        )
        copy.start()
        return copy

    def add_cores(copy, source, land):
        copy.wait_recv()

        def add(t, carry):
            source[d, t] = (source[d, t].astype(F32) + land[t].astype(F32)).astype(BF16)
            return carry

        lax.fori_loop(0, 4, add, 0)

    weight_grads = (r.dw_g, r.dw_u, r.dw_d)
    sources = [
        weight_grads[index].at[d, :, :, :, start : start + width]
        for index, start, width, _ in FF_ITEMS
    ]
    sources += [
        (r.late, r.last)[index].at[d, :, :, :, start : start + width]
        for index, start, width, _, _ in LATE_ITEMS
    ]
    sources += [r.chunk]
    y_firsts = [item[3] for item in FF_ITEMS + LATE_ITEMS] + [True]
    plane = [
        PlaneSum(
            i,
            sources[i],
            y_firsts[i],
            landings[2 * i],
            landings[2 * i + 1],
            (r.sum_first, r.sum_last),
        )
        for i in range(len(sources))
    ]
    gate_items, up_items, down_items = plane[0:2], plane[2:4], plane[4:6]
    late_items, last_items, gain_item = plane[6:8], plane[8:10], plane[10]

    cores = []
    for index, (left, right, out, land) in enumerate(
        (
            (r.cot_t, r.inner, r.dw_d, r.land_d),
            (r.mixed_t, r.grad_gate, r.dw_g, r.land_g),
            (r.mixed_t, r.grad_up, r.dw_u, r.land_u),
        )
    ):

        def weights(t, carry):
            columns = columns_of(t, 384)
            value = nn(left[...], right[:, columns]).astype(BF16)
            out[:, :, :, :, columns] = value.reshape(2, 4, 4, 32, 384)
            return carry

        lax.fori_loop(0, 3, weights, 0)
        cores.append(to_other_core(index, out, land))
        if index == 0:
            transpose_into(r.mixed_t, r.mixed)
        elif index == 1:
            add_cores(cores[0], r.dw_d, r.land_d)
            for item in down_items:
                item.start()

    def project_down(t, carry):
        columns = columns_of(t, 256)
        value = nt(r.inner[...], r.wd[columns, :])
        for other in range(4):
            r.down_send[other, :, columns] = value[other * 96 : (other + 1) * 96].astype(BF16)
        return carry

    lax.fori_loop(0, 4, project_down, 0)

    add_cores(cores[1], r.dw_g, r.land_g)
    add_cores(cores[2], r.dw_u, r.land_u)

    rows = columns_of(z, 96)
    incoming = r.total[rows, :] + reduce_mixed.finish()
    values = r.hidden[rows, :]
    factor = r.scale[rows, 0:1]
    weighted = incoming * r.feed_gain[...]
    projected = jnp.sum(weighted * values, axis=1, keepdims=True) * (1.0 / 1024.0)
    grad_rows = (
        r.cot[rows, :].astype(F32)
        + factor * weighted
        - values * (factor * factor * factor * projected)
    )
    r.gains[...] = jnp.zeros_like(r.gains)
    r.gains[1:2, :] = jnp.sum(incoming * values * factor, axis=0, keepdims=True)
    r.grad_rows[...] = grad_rows
    r.branch[z] = grad_rows.astype(BF16)

    def attended(t, carry):
        columns = columns_of(t, 256)
        r.dob[:, columns] = nn(r.branch[z], r.wall[:, columns]).astype(BF16)
        return carry

    lax.fori_loop(0, 4, attended, 0)

    def do_copy(j, step):
        other = lax.rem(z + step, 4)
        source = r.dob.at[:, columns_of(other * 2 + j, 128)]
        there = r.dos.at[slot, columns_of(z, 96)]
        sems = (r.do_send.at[j, step], r.do_recv.at[slot, z])
        return source, there, *sems, home_core, home(j), other

    for j in range(2):
        for step in (2, 1, 3):
            remote(*do_copy(j, step)).start()
        here = (home(j) == c) & (home_core == d)

        @pl.when(jnp.logical_not(here))
        def _():
            remote(*do_copy(j, 0)).start()

        @pl.when(here)
        def _():
            source, there, _, arrived = do_copy(j, 0)[:4]
            local_sem(source, there, arrived).start()

    reduce_down = ZDirectReduce(r.down_send, r.down_land, r.down_sems, d, c, z).start()
    gather_branch = ZGather(r.branch, r.branch_sems, d, c, z).start()
    for item in gate_items:
        item.start()

    r.dqt[...] = jnp.zeros_like(r.dqt)
    for which in range(2):
        for source in range(4):
            there = r.dos.at[which, source * 96 : (source + 1) * 96]
            local_sem(r.dob.at[:, 0:128], there, r.do_recv.at[which, source]).wait()
        first, second = spread_heads(r.dos[which], True)
        r.doz[which, 0:ROWS, :] = first
        r.doz[which, ROWS : 2 * ROWS, :] = second
        product = (r.dos[which].astype(F32) * r.os[which].astype(F32)).T
        r.delta[which, :, 0:ROWS] = jnp.broadcast_to(
            jnp.sum(product[0:64], axis=0, keepdims=True), (8, ROWS)
        )
        r.delta[which, :, ROWS : 2 * ROWS] = jnp.broadcast_to(
            jnp.sum(product[64:128], axis=0, keepdims=True), (8, ROWS)
        )

    key_scale = jnp.where(lane < 64, 0.125, 1.0)

    def backward_tile(block, which, masked):
        keys = r.kvs[block]
        keys_t = keys.T
        result = None
        for head in range(2):
            rows = slice(head * ROWS, (head + 1) * ROWS)
            q_rows = r.qz[which, rows, :]
            do_rows = r.doz[which, rows, :]
            weights = jnp.exp2(nt(keys, q_rows) * SCORE_SCALE - r.l2[which, 0:1, rows])
            if masked:
                key = lax.broadcasted_iota(jnp.int32, weights.shape, 0)
                row = lax.broadcasted_iota(jnp.int32, weights.shape, 1)
                weights = jnp.where(row >= key, weights, 0.0)
            score_grad = (weights * (nt(keys, do_rows) - r.delta[which, 0:1, rows])).astype(BF16)
            part = nn(score_grad, q_rows) + nn(weights.astype(BF16), do_rows)
            result = part if result is None else result + part
            r.dqt[which, :, rows] += nn(keys_t, score_grad)
        return result * key_scale

    def dkv_copy(block):
        return (
            r.dkv_out.at[block],
            r.dkv_in.at[j_role, x],
            r.dkv_send.at[block],
            r.dkv_recv.at[j_role, x],
            s,
            block,
            z,
        )

    def dkv_start(block):
        here = (s == d) & (block == c)

        @pl.when(jnp.logical_not(here))
        def _():
            remote(*dkv_copy(block)).start()

        @pl.when(here)
        def _():
            source, there, _, arrived = dkv_copy(block)[:4]
            local_sem(source, there, arrived).start()

    def of_both(block):
        return (block < 4) | ((block >= 4) & (block <= 8 + x))

    def class_of(block):
        return jnp.where(lower(block) < 4, 0, 1)

    def part_copy(block):
        index = lax.rem(block, 8)
        return remote(
            r.dkv_out.at[block],
            r.dkv_part.at[index],
            r.part_send_sem.at[block],
            r.part_recv_sem.at[index],
            1 - d,
            c,
            z,
        )

    def dispatch(block):
        both = of_both(block)

        @pl.when(both & (class_of(block) != d))
        def _():
            part_copy(block).start()

        @pl.when(jnp.logical_not(both))
        def _():
            dkv_start(block)

    def combine(block):
        index = lax.rem(block, 8)
        part_copy(block).wait_recv()
        r.dkv_out[block] = (
            r.dkv_out[block].astype(F32) + r.dkv_part[index].astype(F32)
        ).astype(BF16)
        dkv_start(block)

    def combine_own(i):
        first = own(i)
        combine(first)

        @pl.when((d == 1) & (first >= low))
        def _():
            combine(15 - first)

    r.dkv_out[low] = (backward_tile(low, 1, False) + backward_tile(low, 0, True)).astype(BF16)
    r.dkv_out[high] = backward_tile(high, 1, True).astype(BF16)
    dispatch(high)

    def backward_step(k, carry):
        odd = lax.rem(k, 2) == 1
        first = jnp.where(odd, others((k - 1) // 2), own(k // 2))
        below = first < low
        one = backward_tile(first, 1, False)
        two = backward_tile(jnp.where(below, first, 15 - first), jnp.where(below, 0, 1), False)

        @pl.when(below)
        def _():
            r.dkv_out[first] = (one + two).astype(BF16)
            dispatch(first)

        @pl.when(jnp.logical_not(below))
        def _():
            r.dkv_out[first] = one.astype(BF16)
            dispatch(first)
            r.dkv_out[15 - first] = two.astype(BF16)
            dispatch(15 - first)

        @pl.when(odd & (k >= 3))
        def _():
            combine_own((k - 3) // 2)

        return carry

    lax.fori_loop(1, 5, backward_step, 0)
    gather_branch.relay()
    block_rows = r.hidden[columns_of(z, 96), :] + r.down_send[z].astype(F32)
    r.block[z] = (block_rows + reduce_down.finish()).astype(BF16)
    gather_block = ZGather(r.block, r.block_sems, d, c, z).start()
    lax.fori_loop(5, 8, backward_step, 0)

    def dq_copy(which):
        block = high if which else low
        return (
            r.dq_out.at[which],
            r.dq_in.at[j_role],
            r.dq_send.at[which],
            r.dq_recv.at[j_role],
            s,
            block,
            z,
        )

    for which in range(2):
        flat = r.dqt[which].T * 0.125
        r.dq_out[which] = jnp.where(
            lane < 64, flat[:ROWS], pltpu.roll(flat[ROWS:], 64, 1)
        ).astype(BF16)
        block = high if which else low
        here = (s == d) & (block == c)

        @pl.when(jnp.logical_not(here))
        def _():
            remote(*dq_copy(which)).start()

        @pl.when(here)
        def _():
            source, there, _, arrived = dq_copy(which)[:4]
            local_sem(source, there, arrived).start()

    combine_own(3)
    for item in up_items:
        item.start()

    cosine, sine = tables(c, r.row_cos, r.row_sin, r.block_cos, r.block_sin)
    for j in range(2):
        local_sem(r.dq_out.at[0], r.dq_in.at[j], r.dq_recv.at[j]).wait()
    query_part = jnp.zeros((1, 128), F32)
    for j in range(2):
        columns = slice(j * 128, (j + 1) * 128)
        raw_grad, gain_part = pair_backward(
            r.dq_in[j].astype(F32), r.qraw[:, columns], query_gain, cosine, sine
        )
        r.grads[:, columns] = raw_grad.astype(BF16)
        query_part = query_part + gain_part
    r.gains[2:3, 0:128] = query_part + pltpu.roll(query_part, 64, 1)

    def project_query(t, carry):
        columns = columns_of(t, 256)
        r.total[:, columns] = nt(r.grads[:, 0:256], r.wq[columns, :])
        return carry

    lax.fori_loop(0, 4, project_query, 0)
    gather_block.relay()

    for j in range(2):
        r.dkv[j] = jnp.zeros((ROWS, 128), F32)

    def collect(column, carry):
        @pl.when(c <= 15 - column)
        def _():
            for j in range(2):
                local_sem(
                    r.dkv_out.at[0], r.dkv_in.at[j, column], r.dkv_recv.at[j, column]
                ).wait()
                r.dkv[j] += r.dkv_in[j, column].astype(F32)

        return carry

    lax.fori_loop(0, 4, collect, 0)
    first, second = r.dkv[0], r.dkv[1]
    raw_grad, key_part = pair_backward(
        jnp.where(lane < 64, first, pltpu.roll(second, 64, 1)),
        r.kraw[...],
        key_gain,
        cosine,
        sine,
    )
    r.grads[:, 256:384] = raw_grad.astype(BF16)
    r.grads[:, 384:512] = jnp.where(lane < 64, pltpu.roll(first, 64, 1), second).astype(BF16)
    r.gains[3:4, 0:128] = key_part + pltpu.roll(key_part, 64, 1)

    def project_keys(t, carry):
        columns = columns_of(t, 256)
        value = (
            r.total[:, columns]
            + nt(r.grads[:, 256:384], r.wk[columns, :])
            + nt(r.grads[:, 384:512], r.wv[columns, :])
        ).astype(BF16)
        for other in range(4):
            r.last_send[other, :, columns] = value[other * 96 : (other + 1) * 96]
        return carry

    lax.fori_loop(0, 4, project_keys, 0)
    reduce_last = ZDirectReduce(r.last_send, r.last_land, r.last_sems, d, c, z).start()

    r.late[:, :, :, :, 0:256] = (
        nn(r.normed_t[...], r.grads[:, 0:256]).astype(BF16).reshape(2, 4, 4, 32, 256)
    )
    gather_branch.finish()
    for source in range(4):

        def move(t, carry):
            columns = columns_of(t, 128)
            r.mixed_t[columns, source * 96 : (source + 1) * 96] = r.branch[source, :, columns].T
            return carry

        lax.fori_loop(0, 8, move, 0)
    r.late[:, :, :, :, 256:512] = (
        nn(r.mixed_t[...], r.oall[:, column]).astype(BF16).reshape(2, 4, 4, 32, 256)
    )
    late_core = to_other_core(3, r.late, r.late_land)
    r.last[...] = nn(r.normed_t[...], r.grads[:, 256:512]).astype(BF16).reshape(2, 4, 4, 32, 256)
    last_core = to_other_core(4, r.last, r.last_core)
    for item in down_items + gate_items:
        item.middle()
    add_cores(late_core, r.late, r.late_land)
    for item in late_items:
        item.start()
    add_cores(last_core, r.last, r.last_core)
    for item in last_items:
        item.start()
    for item in up_items:
        item.middle()

    rows = columns_of(z, 96)
    incoming = r.last_send[z].astype(F32) + reduce_last.finish()
    values = r.x[rows, :].astype(F32)
    factor = lax.rsqrt(jnp.mean(values * values, axis=1, keepdims=True) + epsilon)
    weighted = incoming * r.attention_gain[...]
    projected = jnp.sum(weighted * values, axis=1, keepdims=True) * (1.0 / 1024.0)
    r.gains[0:1, :] = jnp.sum(incoming * values * factor, axis=0, keepdims=True)
    gather_gains = []
    for step in range(1, 8):
        copy = remote(
            r.gains,
            r.gains_land.at[step - 1],
            r.gain_sems.at[0, step - 1],
            r.gain_sems.at[1, step - 1],
            d if step < 4 else 1 - d,
            c,
            lax.rem(z + step, 4),
        )
        copy.start()
        gather_gains.append(copy)
    r.rows_out[z] = (
        r.grad_rows[...] + factor * weighted - values * (factor * factor * factor * projected)
    ).astype(BF16)
    gather_rows = ZDirectGather(r.rows_out, r.rows_sems, d, c, z).start()

    for copy in gather_gains:
        copy.wait_recv()
    r.chunk_in[...] = jnp.zeros_like(r.chunk_in)
    gain_total = r.gains[...]
    for step in range(7):
        gain_total = gain_total + r.gains_land[step]
    r.chunk_in[0:8, :] = gain_total
    column_part = r.chunk_in[:, columns_of(d, 512)].T
    row_kind = lax.rem(lax.broadcasted_iota(jnp.int32, (512, 128), 0), 32)
    lane_index = lax.broadcasted_iota(jnp.int32, (512, 128), 1)
    query_total, key_total = r.chunk_in[2:3, 0:128], r.chunk_in[3:4, 0:128]
    spread = jnp.where(row_kind == 0, query_total, jnp.where(row_kind == 1, key_total, 0.0))
    r.chunk[...] = (
        jnp.where(lane_index < 64, column_part, spread).astype(BF16).reshape(4, 4, 32, 128)
    )
    gain_item.start()
    for item in late_items + last_items:
        item.middle()
    gain_item.middle()

    sums = (r.gate_sum, r.up_sum, r.down_sum)
    for item, (index, start, width, _) in zip(plane[:6], FF_ITEMS):
        sums[index][:, start : start + width] = item.finish()
    for item, (_, _, width, _, start) in zip(late_items + last_items, LATE_ITEMS):
        r.late_sum[:, start : start + width] = item.finish()
    r.gain_sum[...] = gain_item.finish()
    gather_block.finish()
    gather_rows.finish()

    copies = w_copies + forwards + cores + gather_gains + [late_core, last_core]
    for transfer in (
        reduce_mixed,
        gather_branch,
        reduce_down,
        gather_block,
        reduce_last,
        gather_rows,
    ):
        copies = copies + transfer.copies
    for copy in copies:
        copy.wait_send()
    for item in plane:
        item.sent()
    for j in range(2):

        @pl.when(jnp.logical_not((home(j) == c) & (home_core == d)))
        def _():
            q_copy(j).wait_send()
            remote(*do_copy(j, 0)).wait_send()

        for step in (1, 2, 3):
            remote(*do_copy(j, step)).wait_send()

    def kv_sent(k, carry):
        for j in range(2):
            core, chip, needed = kv_target(k, j)

            @pl.when(needed & jnp.logical_not((core == d) & (chip == c)))
            def _():
                kv_copy(k, j).wait_send()

        first = own(k)
        hand_on(2 * k, first).wait_send()

        @pl.when((d == 1) & (first >= low))
        def _():
            hand_on(2 * k + 1, 15 - first).wait_send()

        return carry

    lax.fori_loop(0, 4, kv_sent, 0)
    for which in range(2):
        block = high if which else low
        for step in (1, 2, 3):
            remote(*o_copy(which, step)).wait_send()

        @pl.when(jnp.logical_not((s == d) & (block == c)))
        def _():
            remote(*o_copy(which, 0)).wait_send()
            remote(*dq_copy(which)).wait_send()

    def dkv_sent(block, carry):
        both = of_both(block)
        mine = class_of(block) == d

        @pl.when((block <= high) & both & jnp.logical_not(mine))
        def _():
            part_copy(block).wait_send()

        owner_here = (s == d) & (block == c)

        @pl.when((block <= high) & (jnp.logical_not(both) | mine) & jnp.logical_not(owner_here))
        def _():
            remote(*dkv_copy(block)).wait_send()

        return carry

    lax.fori_loop(0, 16, dkv_sent, 0)


def emit_kernel(
    block, rows, gate, up, down, late, gains,
    block_out, input_grad, attention_gain, query_gain, key_gain,
    wq, wk, wv, wo, feed_gain, wg, wu, wd,
):
    d, c, _ = place()
    for part in range(4):
        block_out[part * 96 : (part + 1) * 96, :] = block[part]
        input_grad[part * 96 : (part + 1) * 96, :] = rows[part].astype(F32)
    wg[...] = gate[...]
    wu[...] = up[...]
    wd[...] = down[...]
    wq[...] = late[:, 0:256]
    wk[...] = late[:, 256:384]
    wv[...] = late[:, 384:512]
    wo[...] = late[:, 512:768]
    turned = gains[...].T
    attention_gain[...] = turned[0:1, :]
    feed_gain[...] = turned[1:2, :]
    first = 64 + 2 * (d * 16 + c)
    lane = lax.broadcasted_iota(jnp.int32, (1, 128), 1)
    pair = lax.broadcasted_iota(jnp.int32, (1, 2), 1)
    for row, out in ((0, query_gain), (1, key_gain)):
        values = gains[row : row + 1, :]
        one = jnp.sum(jnp.where(lane == first, values, 0.0), axis=1, keepdims=True)
        two = jnp.sum(jnp.where(lane == first + 1, values, 0.0), axis=1, keepdims=True)
        out[...] = jnp.where(pair == 0, one, two)


def shards(
    inputs,
    cotangent,
    attention_gain,
    query_gain,
    key_gain,
    w_query,
    key_weight,
    value_weight,
    w_out,
    feed_gain,
    w_gate,
    w_up,
    w_down,
):
    vmem, anywhere = pl.BlockSpec(memory_space=pltpu.VMEM), pl.BlockSpec(memory_space=pl.ANY)
    landings = []
    for width in SUM_WIDTHS:
        landings += [pltpu.VMEM((3, 4, 32, width), BF16), pltpu.VMEM((3, 32, width), BF16)]
    results = pl.pallas_call(
        block_kernel,
        out_shape=[jax.ShapeDtypeStruct(*spec) for spec in OUTPUTS.values()],
        in_specs=[vmem] * len(INPUTS) + [anywhere] * len(STREAMED),
        out_specs=[vmem] * len(OUTPUTS),
        scratch_shapes=[pltpu.VMEM(*spec) for spec in BUFFERS.values()]
        + [pltpu.SemaphoreType.DMA(shape) for shape in SEMAPHORES.values()]
        + landings,
        compiler_params=pltpu.CompilerParams(
            collective_id=1, has_side_effects=True, vmem_limit_bytes=VMEM_LIMIT
        ),
        name="block",
    )(
        attention_gain.reshape(1, 1024),
        query_gain.reshape(1, 64),
        key_gain.reshape(1, 64),
        *[jnp.asarray(table) for table in split_columns()],
        feed_gain.reshape(1, 1024),
        inputs,
        key_weight,
        value_weight,
        w_query,
        cotangent,
        w_out,
        w_gate,
        w_up,
        w_down,
    )
    shapes = [
        ((ROWS, 1024), BF16),
        ((ROWS, 1024), F32),
        ((1, 32), F32),
        ((1, 2), F32),
        ((1, 2), F32),
        ((32, 256), F32),
        ((32, 128), F32),
        ((32, 128), F32),
        ((32, 256), F32),
        ((1, 32), F32),
        ((32, 1152), F32),
        ((32, 1152), F32),
        ((32, 1152), F32),
    ]
    outputs = pl.pallas_call(
        emit_kernel,
        out_shape=[jax.ShapeDtypeStruct(*spec) for spec in shapes],
        in_specs=[vmem] * len(results),
        out_specs=[vmem] * len(shapes),
        compiler_params=pltpu.CompilerParams(vmem_limit_bytes=VMEM_LIMIT),
        name="emit",
    )(*results)
    return tuple(
        value.reshape(-1) if value.shape[0] == 1 else value for value in outputs
    )


def solution(mesh):
    both = ("dp", "ctx")
    by_head = P(None, "head")
    reduced = P(both, "head")
    return jax.shard_map(
        shards,
        mesh=mesh,
        in_specs=(
            P(both, None),
            P(both, None),
            P(),
            P(),
            P(),
            by_head,
            by_head,
            by_head,
            by_head,
            P(),
            by_head,
            by_head,
            by_head,
        ),
        out_specs=(
            P(both, None),
            P(both, None),
            P(both),
            P(both),
            P(both),
            reduced,
            reduced,
            reduced,
            reduced,
            P(both),
            reduced,
            reduced,
            reduced,
        ),
        check_vma=False,
    )
```
